128 devices in a mesh: gx: 16 (over y, z), gy: 4 (over x), ta: 2 (over core).
Axes of the slice: x: 4, y: 4, z: 4, core: 2. Of those that a mesh axis runs over, the one named last changes fastest.
Arguments:
- features: bfloat16 [2, 256, 256, 1280], P('ta', 'gx', 'gy'), may hold values from -6 to 6
- cotangent: bfloat16 [2, 256, 256, 1280], P('ta', 'gx', 'gy'), may hold values from -6 to 6
- spectral_weight: bfloat16 [48, 24, 2, 20, 960], P('gx', 'gy'), may hold values from -3 to 3
- mixing_weight: bfloat16 [20, 20], replicated, may hold values from -1.25 to 1.25
Outputs:
- activated: bfloat16 [2, 256, 256, 1280], P('ta', 'gx', 'gy')
- grad_features: bfloat16 [2, 256, 256, 1280], P('ta', 'gx', 'gy')
- grad_spectral: float32 [48, 24, 2, 20, 960], P('gx', ('gy', 'ta'))
- grad_mixing: float32 [20, 20], replicated
The draws below stay inside these ranges and needn't reach their ends.
All inputs are finite; a program needn't handle non-finite values.
Results may differ from the reference program's by a relative error of at most 0.028.
Values may be sent and summed in bfloat16 or wider, within the bound.
A program may use at most 192 MiB of HBM per device.

```python
import math
import jax
import jax.numpy as jnp
from jax import lax

NX = 256
NY = 256
NZ = 64
C = 20
M = 24
NT = 2
KEPT = 48
CZ = 1280
N_GY = 4


def shard_levels(stream_key, shape, shards, smallest, largest):
    level, own = 1.0, jax.random.fold_in(stream_key, 6)
    for dim, blocks in shards:
        steps = jnp.exp(jax.random.uniform(jax.random.fold_in(own, dim), (blocks,), jnp.float32, smallest / len(shards), largest / len(shards)))
        level = level * jnp.repeat(steps, shape[dim] // blocks).reshape([-1 if axis == dim else 1 for axis in range(len(shape))])
    return level


def scatter_about(key, shape, width, limit, pieces=(), held_as=jnp.bfloat16):
    values = width * jax.random.normal(key, shape, jnp.float32)
    if pieces:
        values = values * shard_levels(key, shape, pieces, -0.22, 0.18)
    return jnp.clip(values, -limit, limit).astype(held_as)


def setup_inputs(seed: int = 0) -> dict:
    keys = jax.random.split(jax.random.key(seed), 5)
    return {
        "features": scatter_about(keys[0], (NT, NX, NY, CZ), 1.0, 6.0, ((0, 2), (1, 16), (2, 4))),
        "cotangent": scatter_about(keys[1], (NT, NX, NY, CZ), 1.0, 6.0, ((0, 2), (1, 16), (2, 4))),
        "spectral_weight": scatter_about(keys[2], (KEPT, M, 2, C, C * KEPT), 0.5, 3.0, ((0, 16), (1, 4))),
        "mixing_weight": scatter_about(keys[3], (C, C), C ** -0.5, 1.25),
    }


def frequencies(length, count, folded):
    position = jnp.arange(count, dtype=jnp.int32)
    if folded:
        position = jnp.where(position < count // 2, position, position + length - count)
    return position

def cos_sin(length, count, folded, positions):
    freq_list = frequencies(length, count, folded)
    phases = positions[:, None] * freq_list[None, :] % length
    angles = phases.astype(jnp.float32) * (2.0 * math.pi / length)
    return (jnp.cos(angles).astype(jnp.bfloat16), jnp.sin(angles).astype(jnp.bfloat16))

def complex_table(length, count, positions):
    cosine, sine = cos_sin(length, count, True, positions)
    return jnp.stack([jnp.stack([cosine, -sine], 1), jnp.stack([sine, cosine], 1)], 0)

def depth_table():
    cosine, sine = cos_sin(NZ, M, False, jnp.arange(NZ, dtype=jnp.int32))
    return jnp.stack([cosine, -sine], 1)

def single(array):
    return array.astype(jnp.float32)

def forward_spectrum(signal, depth_tab, width_tab, height_tab):
    kept_modes = 2 * M
    block_rows = NY // N_GY
    depth_part = jnp.einsum('xycz,zqj->xycqj', single(signal), single(depth_tab)).astype(jnp.bfloat16)
    depth_part = depth_part.reshape(NX, N_GY, block_rows, C, 2, M)
    blocked_tab = height_tab.reshape(2, N_GY, block_rows, 2, kept_modes)
    partial_value = jnp.einsum('xbycpj,pbyqk->bxkjqc', single(depth_part), single(blocked_tab)).astype(jnp.bfloat16)
    height_part = lax.optimization_barrier(jnp.sum(single(partial_value), axis=0)).astype(jnp.bfloat16)
    return jnp.einsum('xkjpc,pxqi->kjqci', single(height_part), single(width_tab))

def inverse_spectrum(spectral, depth_tab, width_tab, height_tab):
    back_x = jnp.einsum('kjpci,qxpi->kjqcx', single(spectral), single(width_tab)).astype(jnp.bfloat16)
    back_y = jnp.einsum('kjpcx,qypk->xycqj', single(back_x), single(height_tab)).astype(jnp.bfloat16)
    return jnp.einsum('xycqj,zqj->xycz', single(back_y), single(depth_tab))

def mix_forward(spectrum, weight):
    real_in, imag_in = (single(spectrum[:, :, 0]), single(spectrum[:, :, 1]))
    real_w, imag_w = (single(weight[:, :, 0]), single(weight[:, :, 1]))

    def product(left, right):
        return jnp.einsum('kjci,kjcoi->kjoi', left, right)
    real_out = product(real_in, real_w) - product(imag_in, imag_w)
    imag_out = product(real_in, imag_w) + product(imag_in, real_w)
    return jnp.stack([real_out, imag_out], 2)

def mix_adjoint(grad_spectrum, weight):
    real_grad, imag_grad = (single(grad_spectrum[:, :, 0]), single(grad_spectrum[:, :, 1]))
    real_w, imag_w = (single(weight[:, :, 0]), single(weight[:, :, 1]))

    def product(left, right):
        return jnp.einsum('kjoi,kjcoi->kjci', left, right)
    real_out = product(real_grad, real_w) + product(imag_grad, imag_w)
    imag_out = product(imag_grad, real_w) - product(real_grad, imag_w)
    return jnp.stack([real_out, imag_out], 2)

def weight_gradient(spectrum, grad_spectrum):
    real_in, imag_in = (single(spectrum[:, :, 0]), single(spectrum[:, :, 1]))
    real_grad, imag_grad = (single(grad_spectrum[:, :, 0]), single(grad_spectrum[:, :, 1]))

    def product(left, right):
        return jnp.einsum('kjci,kjoi->kjcoi', left, right)
    real_part = product(real_in, real_grad) + product(imag_in, imag_grad)
    imag_part = product(real_in, imag_grad) - product(imag_in, real_grad)
    return jnp.stack([real_part, imag_part], 2)

def reference(features, cotangent, spectral_weight, mixing_weight):
    kept_modes = 2 * M
    depth_tab = depth_table()
    width_tab = complex_table(NX, kept_modes, jnp.arange(NX, dtype=jnp.int32))
    height_tab = complex_table(NY, kept_modes, jnp.arange(NY, dtype=jnp.int32))
    weight = spectral_weight.reshape(kept_modes, M, 2, C, C, kept_modes)
    depth_ids = jnp.arange(M, dtype=jnp.int32)
    mode_scale = jnp.where(depth_ids == 0, 1.0, 2.0).astype(jnp.float32) / float(NX * NY * NZ)
    mode_scale = mode_scale.reshape(1, M, 1, 1, 1)
    mixing_single = single(mixing_weight)

    def one_step(carry, inputs):
        grad_sum, mixing_sum = carry
        feature_step, cotangent_step = inputs
        signal = feature_step.reshape(NX, NY, C, NZ)
        upstream = cotangent_step.reshape(NX, NY, C, NZ)
        spectrum = forward_spectrum(signal, depth_tab, width_tab, height_tab).astype(jnp.bfloat16)
        mixed = (mix_forward(spectrum, weight) * mode_scale).astype(jnp.bfloat16)
        spectral_term = inverse_spectrum(mixed, depth_tab, width_tab, height_tab)
        linear_term = jnp.einsum('xycz,cd->xydz', single(signal), mixing_single)
        preact = spectral_term + linear_term
        activated, gelu_back = jax.vjp(jax.nn.gelu, preact)
        grad_pre = gelu_back(single(upstream))[0].astype(jnp.bfloat16)
        grad_spectrum = (forward_spectrum(grad_pre, depth_tab, width_tab, height_tab) * mode_scale).astype(jnp.bfloat16)
        step_grad = weight_gradient(spectrum, grad_spectrum)
        back_spectrum = mix_adjoint(grad_spectrum, weight).astype(jnp.bfloat16)
        grad_term = inverse_spectrum(back_spectrum, depth_tab, width_tab, height_tab)
        transposed = jnp.einsum('xydz,cd->xycz', single(grad_pre), mixing_single)
        grad_features = (grad_term + transposed).astype(jnp.bfloat16).reshape(NX, NY, C * NZ)
        step_mixing = jnp.einsum('xycz,xydz->cd', single(signal), single(grad_pre))
        outputs = (activated.astype(jnp.bfloat16).reshape(NX, NY, C * NZ), grad_features)
        return ((grad_sum + step_grad, mixing_sum + step_mixing), outputs)
    initial = (jnp.zeros((kept_modes, M, 2, C, C, kept_modes), jnp.float32), jnp.zeros((C, C), jnp.float32))
    totals, outputs = lax.scan(one_step, initial, (features, cotangent))
    grad_sum, mixing_sum = totals
    activated, grad_features = outputs
    grad_spectral = grad_sum.reshape(kept_modes, M, 2, C, C * kept_modes)
    grad_mixing = mixing_sum / math.sqrt(NT * NX * NY * NZ)
    return (activated, grad_features, grad_spectral, grad_mixing)
```

```python
import math

import jax
import jax.numpy as jnp
import ml_dtypes
import numpy as np
from jax import lax
from jax.experimental import pallas as pl
from jax.experimental.pallas import tpu as pltpu
from jax.sharding import PartitionSpec as P

NX = 256
NY = 256
NZ = 64
C = 20
M = 24
KEPT = 48
CZ = C * NZ
GX = 16
GY = 4
ROWS = 1024
HALF = 512
F32 = jnp.float32
BF16 = jnp.bfloat16
MESH = pl.DeviceIdType.MESH
NT = (((1,), (1,)), ((), ()))
TN = (((0,), (0,)), ((), ()))


def cos_sin(length, count, folded):
    freq = np.arange(count)
    if folded:
        freq = np.where(freq < count // 2, freq, freq + length - count)
    phases = np.arange(length)[:, None] * freq[None, :] % length
    angles = phases.astype(np.float32) * np.float32(2.0 * math.pi / length)
    return np.cos(angles), np.sin(angles)


def complex_table(length, count):
    cosine, sine = cos_sin(length, count, True)
    return np.stack([np.stack([cosine, -sine], 1), np.stack([sine, cosine], 1)], 0)


def tables():
    cosine, sine = cos_sin(NZ, M, False)
    depth = np.stack([cosine, -sine], 1)
    ee = np.zeros((GY, C, NZ, 2, 128), np.float32)
    for h in range(GY):
        for jl in range(6):
            for c in range(C):
                ee[h, c, :, :, jl * C + c] = depth[:, :, h * 6 + jl]
    ee = ee.reshape(GY, CZ, 256)
    eet = np.ascontiguousarray(ee.transpose(0, 2, 1)).reshape(GY * 256, CZ)
    height = complex_table(NY, KEPT).reshape(2, GY, 64, 2, KEPT)
    a2 = np.zeros((GY, 2, 2, KEPT, 2, 2, 64), np.float32)
    for x2 in range(2):
        a2[:, x2, :, :, x2] = height.transpose(1, 3, 4, 0, 2)
    a2 = a2.reshape(GY, 192, 256)
    at2 = np.ascontiguousarray(a2.transpose(0, 2, 1))
    width = complex_table(NX, KEPT).reshape(2, GX, 2, 8, 2, KEPT)
    fx = np.zeros((2, GX, 2, 8, 2, 1024), np.float32)
    fx[..., : C * KEPT] = np.tile(width.transpose(2, 1, 0, 3, 4, 5), (1, 1, 1, 1, 1, C))
    fx = fx.reshape(512, 2048)
    pad = np.zeros((6, 24, 128), np.float32)
    for jl in range(6):
        for c in range(C):
            pad[jl, c, jl * C + c] = 1.0
    pad = pad.reshape(144, 128)
    return [t.astype(ml_dtypes.bfloat16) for t in (ee, eet, a2, at2, fx, pad)]


def kernel(
    u_hbm, cot_hbm, w_ref, mix_ref, mixt_ref, ee_hbm, eet_hbm, a2_hbm, at2_hbm, fx_hbm, pad_hbm,
    act_hbm, gf_hbm, gs_ref, gm_ref,
    u, cot, g, out, ee, eet, kron, lin, fx, pad, a2, at2, wp, uh, ut, lw, gss, gsr,
    part, dg, fl, fr, hs, hr, bs, br, ag, by, s, mask, gh, gmx, gmy, gma,
    in_sem, out_sem, rs_ss, rs_rs, h_ss, h_rs, b_ss, b_rs, ag_ss, ag_rs, gs_sem, gy_ss, gy_rs, gx_ss, gx_rs, ta_sem,
):
    me_x = lax.axis_index("gx")
    me_y = lax.axis_index("gy")
    me_t = lax.axis_index("ta")

    def at_y(rel):
        return (me_x, lax.rem(me_y + rel, GY), me_t)

    def at_x(d):
        return (lax.rem(me_x + d, GX), me_y, me_t)

    twin = (me_x, me_y, 1 - me_t)

    loads = [
        pltpu.make_async_copy(src, dst, in_sem.at[i])
        for i, (src, dst) in enumerate([
            (u_hbm, u), (ee_hbm, ee), (a2_hbm.at[me_y], a2), (fx_hbm, fx), (pad_hbm, pad),
            (at2_hbm.at[me_y], at2), (eet_hbm, eet), (cot_hbm, cot),
        ])
    ]
    for load in loads:
        load.start()

    barrier = pltpu.get_barrier_semaphore()
    for rel in (1, 2, 3):
        pl.semaphore_signal(barrier, inc=1, device_id=at_y(rel), device_id_type=MESH)

    def greet(d, carry):
        pl.semaphore_signal(barrier, inc=1, device_id=at_x(d), device_id_type=MESH)
        return carry

    lax.fori_loop(1, GX, greet, 0)
    pl.semaphore_signal(barrier, inc=1, device_id=twin, device_id_type=MESH)

    def remote(src, dst, ss, rs, dev):
        return pltpu.make_async_remote_copy(
            src_ref=src, dst_ref=dst, send_sem=ss, recv_sem=rs, device_id=dev, device_id_type=MESH
        )

    def rs_copy(t, i):
        src, dst, rel = [
            (part.at[2, 0], dg.at[t, 0], 1),
            (part.at[3, 0], fr.at[t, 0], 3),
            (part.at[1, 0], fl.at[t, 0], 1),
            (part.at[2, 1], dg.at[t, 1], 3),
            (part.at[1, 1], fl.at[t, 1], 1),
            (part.at[3, 1], fr.at[t, 1], 3),
        ][i]
        return remote(src, dst, rs_ss.at[t, i], rs_rs.at[t, i], at_y(rel))

    def ag_copy(t, i):
        src, dst, rel = [
            (ag.at[t, 0, 0], ag.at[t, 3, 0], 1),
            (ag.at[t, 0, 0], ag.at[t, 1, 0], 3),
            (ag.at[t, 3, 0], ag.at[t, 2, 0], 1),
            (ag.at[t, 0, 1], ag.at[t, 1, 1], 3),
            (ag.at[t, 0, 1], ag.at[t, 3, 1], 1),
            (ag.at[t, 1, 1], ag.at[t, 2, 1], 3),
        ][i]
        return remote(src, dst, ag_ss.at[t, i], ag_rs.at[t, i], at_y(rel))

    def h_copy(t, xc, d):
        to = lax.rem(me_x + d, GX)
        return remote(hs.at[xc, to], hr.at[t, xc, me_x], h_ss.at[t, xc, d], h_rs.at[t, xc, d], at_x(d))

    def b_copy(t, xc, d):
        to = lax.rem(me_x + d, GX)
        return remote(bs.at[xc, to], br.at[t, xc, me_x], b_ss.at[t, xc, d], b_rs.at[t, xc, d], at_x(d))

    def over_gx(fn):
        def step(d, carry):
            fn(d)
            return carry

        lax.fori_loop(1, GX, step, 0)

    def scale(jl):
        first = (me_y == 0) & (jl == 0)
        return jnp.where(first, 1.0, 2.0).astype(F32) * (1.0 / float(NX * NY * NZ))

    def forward_block(src, xc, rel):
        h = lax.rem(me_y + rel, GY)
        d = jnp.dot(src[xc * HALF:(xc + 1) * HALF, :], ee[h], preferred_element_type=F32).astype(BF16)
        for xp in range(4):
            r = xp * 128
            rhs = jnp.concatenate(
                [d[r:r + 64, :128], d[r:r + 64, 128:], d[r + 64:r + 128, :128], d[r + 64:r + 128, 128:]], 0
            )
            o = jnp.dot(a2[...], rhs, preferred_element_type=F32)
            part[rel, xc, xp * 192:(xp + 1) * 192, :] = o.astype(BF16)

    def add_part(rel, xc, other):
        part[rel, xc] = (part[rel, xc].astype(F32) + other.astype(F32)).astype(BF16)

    def sum_and_send(t, xc):
        s[...] = part[0, xc].astype(F32) + fl[t, xc].astype(F32) + fr[t, xc].astype(F32)

        def block(gx, carry):
            for k in range(3):
                r = gx * 3 + k
                top = s[pl.ds(r, 8, stride=96), :]
                low = s[pl.ds(r + KEPT, 8, stride=96), :]
                hs[xc, gx, k] = jnp.concatenate([top, low], 0).astype(BF16)
            return carry

        lax.fori_loop(0, GX, block, 0)
        over_gx(lambda d: h_copy(t, xc, d).start())
        hr[t, xc, me_x] = hs[xc, me_x]

    def x_transform(t, k, dst, index):
        hk = hr[t, :, :, k].reshape(512, 128)
        ht = lax.dot_general(pad[...], hk, NT, preferred_element_type=F32).astype(BF16)
        for n in range(4):
            dst[index, :, n * 512:(n + 1) * 512] = jnp.dot(
                ht, fx[:, n * 512:(n + 1) * 512], preferred_element_type=F32
            )

    def x_inverse_and_send(t):
        for xc in range(2):
            def block(k, carry):
                bx = lax.dot_general(fx[xc * 256:(xc + 1) * 256, :], lw[k], NT, preferred_element_type=F32)
                bx = jnp.dot(bx.astype(BF16), pad[...], preferred_element_type=F32).astype(BF16)
                bs[xc, :, k] = bx.reshape(GX, 16, 128)
                return carry

            lax.fori_loop(0, 3, block, 0)
            over_gx(lambda d: b_copy(t, xc, d).start())
            br[t, xc, me_x] = bs[xc, me_x]

    def gather_block(t, xc):
        over_gx(lambda d: b_copy(t, xc, d).wait_recv())

        def block(gx, carry):
            for k in range(3):
                r = gx * 3 + k
                v = br[t, xc, gx, k].astype(F32)
                s[pl.ds(r, 8, stride=96), :] = v[:8]
                s[pl.ds(r + KEPT, 8, stride=96), :] = v[8:]
            return carry

        lax.fori_loop(0, GX, block, 0)
        ag[t, 0, xc] = s[...].astype(BF16)

    def y_inverse(t, xc):
        def block(rel, carry):
            h = lax.rem(me_y + rel, GY)
            off = pl.multiple_of(h * 256, 256)
            for xp in range(4):
                v = jnp.dot(
                    at2[...], ag[t, rel, xc, xp * 192:(xp + 1) * 192, :], preferred_element_type=F32
                ).astype(BF16)
                for x2 in range(2):
                    rows = slice(xp * 128 + x2 * 64, xp * 128 + x2 * 64 + 64)
                    by[rows, pl.ds(off, 128)] = v[x2 * 128:x2 * 128 + 64]
                    by[rows, pl.ds(off + 128, 128)] = v[x2 * 128 + 64:x2 * 128 + 128]
            return carry

        lax.fori_loop(0, GY, block, 0)

    def depth_inverse(xc, finish):
        def block(n, carry):
            cols = pl.ds(pl.multiple_of(n * 256, 256), 256)
            for rb in range(2):
                rows = slice(xc * HALF + rb * 256, xc * HALF + rb * 256 + 256)
                v = jnp.dot(by[rb * 256:rb * 256 + 256, :], eet[:, cols], preferred_element_type=F32)
                finish(rows, cols, v + lin[rows, cols])
            return carry

        lax.fori_loop(0, 5, block, 0)

    def finish_forward(rows, cols, x):
        k0 = math.sqrt(2.0 / math.pi)
        x2 = x * x
        th = jnp.tanh(k0 * x * (1.0 + 0.044715 * x2))
        half = 0.5 * (1.0 + th)
        out[rows, cols] = (x * half).astype(BF16)
        slope = half + 0.5 * x * (1.0 - th * th) * (k0 * (1.0 + 3.0 * 0.044715 * x2))
        g[rows, cols] = (cot[rows, cols].astype(F32) * slope).astype(BF16)

    def finish_backward(rows, cols, x):
        out[rows, cols] = x.astype(BF16)

    def build_kron(ref):
        lane = lax.broadcasted_iota(jnp.int32, (NZ, CZ), 1) & (NZ - 1)
        row = lax.broadcasted_iota(jnp.int32, (NZ, CZ), 0)
        eye = jnp.where(lane == row, 1.0, 0.0).astype(F32)

        def block(c, carry):
            kron[pl.ds(pl.multiple_of(c * NZ, NZ), NZ), :] = (eye * ref[pl.ds(c, 1), :]).astype(BF16)
            return carry

        lax.fori_loop(0, C, block, 0)

    def linear(src):
        def block(n, carry):
            cols = pl.ds(pl.multiple_of(n * 256, 256), 256)
            for rb in range(2):
                rows = slice(rb * 512, rb * 512 + 512)
                lin[rows, cols] = jnp.dot(src[rows, :], kron[:, cols], preferred_element_type=F32)
            return carry

        lax.fori_loop(0, 5, block, 0)

    def fill_weights():
        wp[...] = jnp.zeros_like(wp)
        for k in range(3):
            def block(j, carry):
                for p in range(2):
                    wp[k, j, p, :C, :C * KEPT] = w_ref[k, j, p].astype(F32)
                return carry

            lax.fori_loop(0, 6, block, 0)
        lane = lax.broadcasted_iota(jnp.int32, (24, 1024), 1)
        first = lax.broadcasted_iota(jnp.int32, (24, 1024), 0) * KEPT
        mask[...] = jnp.where((lane >= first) & (lane < first + KEPT) & (lane < C * KEPT), 1.0, 0.0).astype(F32)

    def mix_block(k, carry):
        x_transform(0, k, uh, k)
        for jp in range(3):
            re, im = [], []
            for j in (2 * jp, 2 * jp + 1):
                a = uh[k, j * 24:(j + 1) * 24, :1024]
                b = uh[k, j * 24:(j + 1) * 24, 1024:]
                r, w = wp[k, j, 0], wp[k, j, 1]
                re.append(mask[...] * (jnp.sum(a * r - b * w, 0, keepdims=True) * scale(j)))
                im.append(mask[...] * (jnp.sum(a * w + b * r, 0, keepdims=True) * scale(j)))
            lw[k, jp * 48:(jp + 1) * 48, :1024] = jnp.concatenate(re, 0).astype(BF16)
            lw[k, jp * 48:(jp + 1) * 48, 1024:] = jnp.concatenate(im, 0).astype(BF16)
        return carry

    def adjoint_block(k, carry):
        x_transform(1, k, ut, 0)
        for jp in range(3):
            re, im = [], []
            for j in (2 * jp, 2 * jp + 1):
                r, w = wp[k, j, 0], wp[k, j, 1]
                gr = jnp.sum(ut[0, j * 24:(j + 1) * 24, :1024] * mask[...], 0, keepdims=True) * scale(j)
                gi = jnp.sum(ut[0, j * 24:(j + 1) * 24, 1024:] * mask[...], 0, keepdims=True) * scale(j)
                gh[k, j, 0:1, :] = gr
                gh[k, j, 1:2, :] = gi
                re.append(gr * r + gi * w)
                im.append(gi * r - gr * w)
            lw[k, jp * 48:(jp + 1) * 48, :1024] = jnp.concatenate(re, 0).astype(BF16)
            lw[k, jp * 48:(jp + 1) * 48, 1024:] = jnp.concatenate(im, 0).astype(BF16)
        return carry

    def weight_terms(k, j):
        rows = pl.ds(pl.multiple_of(j * 24, 8), 24)
        a, b = uh[k, rows, :1024], uh[k, rows, 1024:]
        gr, gi = gh[k, j, 0:1, :], gh[k, j, 1:2, :]
        return a * gr + b * gi, a * gi - b * gr

    def gs_copy():
        return remote(gss, gsr, gs_sem.at[0], gs_sem.at[1], twin)

    def weight_gradient_send():
        def block(k, carry):
            for jj in range(3):
                re, im = weight_terms(k, (1 - me_t) * 3 + jj)
                at = pl.multiple_of(k * 144 + jj * 48, 48)
                gss[pl.ds(at, 48), :] = jnp.concatenate([re, im], 0).astype(BF16)
            return carry

        lax.fori_loop(0, 3, block, 0)
        gs_copy().start()

    def weight_gradient_finish():
        gs_copy().wait_recv()

        def block(k, carry):
            for jj in range(3):
                re, im = weight_terms(k, me_t * 3 + jj)
                at = pl.multiple_of(k * 144 + jj * 48, 48)
                other = gsr[pl.ds(at, 48), :].astype(F32)
                gs_ref[k, jj, 0] = (re + other[:24])[:C, :C * KEPT]
                gs_ref[k, jj, 1] = (im + other[24:])[:C, :C * KEPT]
            return carry

        lax.fori_loop(0, 3, block, 0)

    def mixing_terms():
        lane = lax.broadcasted_iota(jnp.int32, (256, 256), 1) & (NZ - 1)
        row = lax.broadcasted_iota(jnp.int32, (256, 256), 0) & (NZ - 1)
        eye = jnp.where(lane == row, 1.0, 0.0).astype(F32)

        def block(cb, carry):
            cols = pl.ds(pl.multiple_of(cb * 256, 256), 256)
            for nb in range(5):
                o = lax.dot_general(
                    u[:, cols], g[:, nb * 256:(nb + 1) * 256], TN, preferred_element_type=F32
                )
                gmx[cb, 0:4, nb * 256:(nb + 1) * 256] = jnp.sum((o * eye).reshape(4, NZ, 256), 1)
            return carry

        gmx[...] = jnp.zeros_like(gmx)
        lax.fori_loop(0, 5, block, 0)
        v = gmx[...].reshape(40, CZ)
        hi = v.astype(BF16)
        low = (v - hi.astype(F32)).astype(BF16)
        sel = lax.broadcasted_iota(jnp.int32, (CZ, 128), 0) >> 6
        sel = jnp.where(sel == lax.broadcasted_iota(jnp.int32, (CZ, 128), 1), 1.0, 0.0).astype(BF16)
        gmy[0] = jnp.dot(hi, sel, preferred_element_type=F32) + jnp.dot(low, sel, preferred_element_type=F32)

    def gy_copy(rel):
        return remote(gmy.at[0], gmy.at[rel], gy_ss.at[rel], gy_rs.at[rel], at_y(rel))

    def gx_copy(d):
        return remote(gma.at[0], gma.at[d], gx_ss.at[d], gx_rs.at[d], at_x(d))

    def ta_copy():
        return remote(gma.at[16], gma.at[17], ta_sem.at[0], ta_sem.at[1], twin)

    pl.semaphore_wait(barrier, 19)
    for i in range(3):
        loads[i].wait()

    forward_block(u, 0, 2)
    rs_copy(0, 0).start()
    forward_block(u, 0, 3)
    rs_copy(0, 1).start()
    forward_block(u, 1, 2)
    rs_copy(0, 3).start()
    forward_block(u, 1, 1)
    rs_copy(0, 4).start()
    forward_block(u, 0, 1)
    forward_block(u, 1, 3)
    rs_copy(0, 0).wait_recv()
    add_part(1, 0, dg[0, 0])
    rs_copy(0, 2).start()
    rs_copy(0, 3).wait_recv()
    add_part(3, 1, dg[0, 1])
    rs_copy(0, 5).start()
    forward_block(u, 0, 0)
    forward_block(u, 1, 0)
    fill_weights()
    build_kron(mix_ref)
    linear(u)
    for i in range(3, 8):
        loads[i].wait()
    rs_copy(0, 1).wait_recv()
    rs_copy(0, 2).wait_recv()
    sum_and_send(0, 0)
    rs_copy(0, 4).wait_recv()
    rs_copy(0, 5).wait_recv()
    sum_and_send(0, 1)
    over_gx(lambda d: h_copy(0, 0, d).wait_recv())
    over_gx(lambda d: h_copy(0, 1, d).wait_recv())

    lax.fori_loop(0, 3, mix_block, 0)
    x_inverse_and_send(0)

    def gather(t):
        gather_block(t, 0)
        ag_copy(t, 0).start()
        ag_copy(t, 1).start()
        gather_block(t, 1)
        ag_copy(t, 3).start()
        ag_copy(t, 0).wait_recv()
        ag_copy(t, 2).start()
        ag_copy(t, 4).start()
        ag_copy(t, 3).wait_recv()
        ag_copy(t, 5).start()

    gather(0)
    for i in range(6):
        rs_copy(0, i).wait_send()
    for xc in range(2):
        over_gx(lambda d: h_copy(0, xc, d).wait_send())
        over_gx(lambda d: b_copy(0, xc, d).wait_send())

    ag_copy(0, 1).wait_recv()
    ag_copy(0, 2).wait_recv()
    y_inverse(0, 0)
    depth_inverse(0, finish_forward)
    act_out = [
        pltpu.make_async_copy(out.at[pl.ds(xc * HALF, HALF)], act_hbm.at[pl.ds(xc * HALF, HALF)], out_sem.at[0, xc])
        for xc in range(2)
    ]
    act_out[0].start()
    forward_block(g, 0, 2)
    rs_copy(1, 0).start()
    forward_block(g, 0, 3)
    rs_copy(1, 1).start()
    ag_copy(0, 4).wait_recv()
    ag_copy(0, 5).wait_recv()
    y_inverse(0, 1)
    depth_inverse(1, finish_forward)
    act_out[1].start()
    forward_block(g, 1, 2)
    rs_copy(1, 3).start()
    forward_block(g, 1, 1)
    rs_copy(1, 4).start()
    forward_block(g, 0, 1)
    rs_copy(1, 0).wait_recv()
    add_part(1, 0, dg[1, 0])
    rs_copy(1, 2).start()
    forward_block(g, 1, 3)
    rs_copy(1, 3).wait_recv()
    add_part(3, 1, dg[1, 1])
    rs_copy(1, 5).start()
    forward_block(g, 0, 0)
    forward_block(g, 1, 0)
    mixing_terms()
    for rel in (1, 2, 3):
        gy_copy(rel).start()
    rs_copy(1, 1).wait_recv()
    rs_copy(1, 2).wait_recv()
    sum_and_send(1, 0)
    rs_copy(1, 4).wait_recv()
    rs_copy(1, 5).wait_recv()
    sum_and_send(1, 1)
    for rel in (1, 2, 3):
        gy_copy(rel).wait_recv()
    gma[0] = gmy[0] + gmy[1] + gmy[2] + gmy[3]
    over_gx(lambda d: gx_copy(d).start())
    over_gx(lambda d: h_copy(1, 0, d).wait_recv())
    over_gx(lambda d: h_copy(1, 1, d).wait_recv())

    lax.fori_loop(0, 3, adjoint_block, 0)
    x_inverse_and_send(1)
    weight_gradient_send()
    gather(1)
    build_kron(mixt_ref)
    linear(g)
    over_gx(lambda d: gx_copy(d).wait_recv())
    gma[16] = jnp.sum(gma[0:16], 0)
    ta_copy().start()
    weight_gradient_finish()
    act_out[0].wait()
    act_out[1].wait()
    ag_copy(1, 1).wait_recv()
    ag_copy(1, 2).wait_recv()
    y_inverse(1, 0)
    depth_inverse(0, finish_backward)
    gf_out = [
        pltpu.make_async_copy(out.at[pl.ds(xc * HALF, HALF)], gf_hbm.at[pl.ds(xc * HALF, HALF)], out_sem.at[1, xc])
        for xc in range(2)
    ]
    gf_out[0].start()
    ag_copy(1, 4).wait_recv()
    ag_copy(1, 5).wait_recv()
    y_inverse(1, 1)
    depth_inverse(1, finish_backward)
    gf_out[1].start()
    ta_copy().wait_recv()
    total = (gma[16] + gma[17]) * (1.0 / math.sqrt(2 * NX * NY * NZ))
    for cb in range(5):
        gm_ref[cb * 4:(cb + 1) * 4, :] = total[cb * 8:cb * 8 + 4, :C]

    for t in range(2):
        for i in range(6):
            ag_copy(t, i).wait_send()
    for i in range(6):
        rs_copy(1, i).wait_send()
    for xc in range(2):
        over_gx(lambda d: h_copy(1, xc, d).wait_send())
        over_gx(lambda d: b_copy(1, xc, d).wait_send())
    gs_copy().wait_send()
    for rel in (1, 2, 3):
        gy_copy(rel).wait_send()
    over_gx(lambda d: gx_copy(d).wait_send())
    ta_copy().wait_send()
    gf_out[0].wait()
    gf_out[1].wait()


def shards(features, cotangent, spectral_weight, mixing_weight):
    mixing = mixing_weight.astype(F32)
    mix = jnp.repeat(mixing, NZ, axis=1)
    mixt = jnp.repeat(mixing.T, NZ, axis=1)
    consts = [jnp.asarray(t) for t in tables()]
    dma = pltpu.SemaphoreType.DMA
    vmem = pltpu.VMEM
    hbm = pl.BlockSpec(memory_space=pl.ANY)
    local = pl.BlockSpec(memory_space=pltpu.VMEM)
    act, gf, gs, gm = pl.pallas_call(
        kernel,
        out_shape=(
            jax.ShapeDtypeStruct((ROWS, CZ), BF16),
            jax.ShapeDtypeStruct((ROWS, CZ), BF16),
            jax.ShapeDtypeStruct((3, 3, 2, C, C * KEPT), F32),
            jax.ShapeDtypeStruct((C, C), F32),
        ),
        in_specs=[hbm, hbm, local, local, local] + [hbm] * 6,
        out_specs=(hbm, hbm, local, local),
        scratch_shapes=[
            vmem((ROWS, CZ), BF16),
            vmem((ROWS, CZ), BF16),
            vmem((ROWS, CZ), BF16),
            vmem((ROWS, CZ), BF16),
            vmem((GY, CZ, 256), BF16),
            vmem((GY * 256, CZ), BF16),
            vmem((CZ, CZ), BF16),
            vmem((ROWS, CZ), F32),
            vmem((512, 2048), BF16),
            vmem((144, 128), BF16),
            vmem((192, 256), BF16),
            vmem((256, 192), BF16),
            vmem((3, 6, 2, 24, 1024), F32),
            vmem((3, 144, 2048), F32),
            vmem((1, 144, 2048), F32),
            vmem((3, 144, 2048), BF16),
            vmem((432, 1024), BF16),
            vmem((432, 1024), BF16),
            vmem((4, 2, 768, 128), BF16),
            vmem((2, 2, 768, 128), BF16),
            vmem((2, 2, 768, 128), BF16),
            vmem((2, 2, 768, 128), BF16),
            vmem((2, GX, 3, 16, 128), BF16),
            vmem((2, 2, GX, 3, 16, 128), BF16),
            vmem((2, GX, 3, 16, 128), BF16),
            vmem((2, 2, GX, 3, 16, 128), BF16),
            vmem((2, 4, 2, 768, 128), BF16),
            vmem((HALF, 1024), BF16),
            vmem((768, 128), F32),
            vmem((24, 1024), F32),
            vmem((3, 6, 8, 1024), F32),
            vmem((5, 8, CZ), F32),
            vmem((4, 40, 128), F32),
            vmem((18, 40, 128), F32),
            dma((8,)),
            dma((2, 2)),
            dma((2, 6)),
            dma((2, 6)),
            dma((2, 2, GX)),
            dma((2, 2, GX)),
            dma((2, 2, GX)),
            dma((2, 2, GX)),
            dma((2, 6)),
            dma((2, 6)),
            dma((2,)),
            dma((4,)),
            dma((4,)),
            dma((GX,)),
            dma((GX,)),
            dma((2,)),
        ],
        compiler_params=pltpu.CompilerParams(
            collective_id=0, has_side_effects=True, vmem_limit_bytes=60 * 1024 * 1024
        ),
    )(
        features.reshape(ROWS, CZ), cotangent.reshape(ROWS, CZ), spectral_weight, mix, mixt, *consts,
    )
    return act.reshape(features.shape), gf.reshape(features.shape), gs, gm


def solution(mesh):
    in_specs = (
        P("ta", "gx", "gy", None),
        P("ta", "gx", "gy", None),
        P("gx", "gy", None, None, None),
        P(),
    )
    out_specs = (
        P("ta", "gx", "gy", None),
        P("ta", "gx", "gy", None),
        P("gx", ("gy", "ta"), None, None, None),
        P(),
    )
    return jax.shard_map(shards, mesh=mesh, in_specs=in_specs, out_specs=out_specs, check_vma=False)
```

```python
import math

import jax
import jax.numpy as jnp
import ml_dtypes
import numpy as np
from jax import lax
from jax.experimental import pallas as pl
from jax.experimental.pallas import tpu as pltpu
from jax.sharding import PartitionSpec as P

NX = 256
NY = 256
NZ = 64
C = 20
M = 24
KEPT = 48
CZ = C * NZ
GX = 16
GY = 4
ROWS = 1024
HALF = 512
F32 = jnp.float32
BF16 = jnp.bfloat16
MESH = pl.DeviceIdType.MESH
NT = (((1,), (1,)), ((), ()))
TN = (((0,), (0,)), ((), ()))


def cos_sin(length, count, folded):
    freq = np.arange(count)
    if folded:
        freq = np.where(freq < count // 2, freq, freq + length - count)
    phases = np.arange(length)[:, None] * freq[None, :] % length
    angles = phases.astype(np.float32) * np.float32(2.0 * math.pi / length)
    return np.cos(angles), np.sin(angles)


def complex_table(length, count):
    cosine, sine = cos_sin(length, count, True)
    return np.stack([np.stack([cosine, -sine], 1), np.stack([sine, cosine], 1)], 0)


def tables():
    cosine, sine = cos_sin(NZ, M, False)
    depth = np.stack([cosine, -sine], 1)
    ee = np.zeros((GY, C, NZ, 2, 128), np.float32)
    for h in range(GY):
        for jl in range(6):
            for c in range(C):
                ee[h, c, :, :, jl * C + c] = depth[:, :, h * 6 + jl]
    ee = ee.reshape(GY, CZ, 256)
    eet = np.ascontiguousarray(ee.transpose(0, 2, 1)).reshape(GY * 256, CZ)
    height = complex_table(NY, KEPT).reshape(2, GY, 64, 2, KEPT)
    a2 = np.zeros((GY, 2, 2, KEPT, 2, 2, 64), np.float32)
    for x2 in range(2):
        a2[:, x2, :, :, x2] = height.transpose(1, 3, 4, 0, 2)
    a2 = a2.reshape(GY, 192, 256)
    at2 = np.ascontiguousarray(a2.transpose(0, 2, 1))
    width = complex_table(NX, KEPT).reshape(2, GX, 2, 8, 2, KEPT)
    fx = np.zeros((2, GX, 2, 8, 2, 128), np.float32)
    fx[..., :KEPT] = width.transpose(2, 1, 0, 3, 4, 5)
    fx = fx.reshape(512, 256)
    spread = np.zeros((128, 1024), np.float32)
    for c in range(C):
        spread[np.arange(KEPT), c * KEPT + np.arange(KEPT)] = 1.0
    fold = np.ascontiguousarray(spread.T)
    pad = np.zeros((6, 24, 128), np.float32)
    for jl in range(6):
        for c in range(C):
            pad[jl, c, jl * C + c] = 1.0
    pad = pad.reshape(144, 128)
    padt = np.ascontiguousarray(pad.T)
    return [t.astype(ml_dtypes.bfloat16) for t in (ee, eet, a2, at2, fx, pad, padt, spread, fold)]


def kernel(
    u_hbm, cot_hbm, w_hbm, mix_ref, ee_hbm, eet_hbm, a2_hbm, at2_hbm, fx_hbm, pad_hbm, padt_hbm, spread_hbm, fold_hbm,
    act_hbm, gf_hbm, gs_ref, gm_ref,
    u, cot, g, out, ee, eet, kron, lin, fx, pad, padt, spread, fold, a2, at2, w, mixrows, wp, uh, ht, yk, lw, gss, gsr,
    part, dg, fl, fr, hs, hr, bs, br, ag, by, s, mask, gh, gmx, gmy, gma,
    in_sem, out_sem, rs_ss, rs_rs, h_ss, h_rs, b_ss, b_rs, ag_ss, ag_rs, gs_sem, gy_ss, gy_rs, gx_ss, gx_rs, ta_sem,
):
    me_x = lax.axis_index("gx")
    me_y = lax.axis_index("gy")
    me_t = lax.axis_index("ta")

    def at_y(rel):
        return (me_x, lax.rem(me_y + rel, GY), me_t)

    def at_x(d):
        return (lax.rem(me_x + d, GX), me_y, me_t)

    twin = (me_x, me_y, 1 - me_t)

    opposite, left = lax.rem(me_y + 2, GY), lax.rem(me_y + 3, GY)
    right = lax.rem(me_y + 1, GY)
    first, second = pl.ds(0, HALF), pl.ds(HALF, HALF)
    loads = [
        pltpu.make_async_copy(src, dst, in_sem.at[i])
        for i, (src, dst) in enumerate([
            (u_hbm.at[first], u.at[first]), (ee_hbm.at[opposite], ee.at[opposite]), (a2_hbm.at[me_y], a2),
            (ee_hbm.at[left], ee.at[left]), (u_hbm.at[second], u.at[second]), (ee_hbm.at[right], ee.at[right]),
            (ee_hbm.at[me_y], ee.at[me_y]), (w_hbm, w), (fx_hbm, fx), (pad_hbm, pad), (padt_hbm, padt),
            (spread_hbm, spread), (fold_hbm, fold), (at2_hbm.at[me_y], at2), (eet_hbm, eet), (cot_hbm, cot),
        ])
    ]
    for load in loads:
        load.start()

    barrier = pltpu.get_barrier_semaphore()
    for rel in (1, 2, 3):
        pl.semaphore_signal(barrier, inc=1, device_id=at_y(rel), device_id_type=MESH)

    def greet(d, carry):
        pl.semaphore_signal(barrier, inc=1, device_id=at_x(d), device_id_type=MESH)
        return carry

    lax.fori_loop(1, GX, greet, 0)
    pl.semaphore_signal(barrier, inc=1, device_id=twin, device_id_type=MESH)

    def remote(src, dst, ss, rs, dev):
        return pltpu.make_async_remote_copy(
            src_ref=src, dst_ref=dst, send_sem=ss, recv_sem=rs, device_id=dev, device_id_type=MESH
        )

    def rs_copy(t, i):
        src, dst, rel = [
            (part.at[2, 0], dg.at[t, 0], 1),
            (part.at[3, 0], fr.at[t, 0], 3),
            (part.at[1, 0], fl.at[t, 0], 1),
            (part.at[2, 1], dg.at[t, 1], 3),
            (part.at[1, 1], fl.at[t, 1], 1),
            (part.at[3, 1], fr.at[t, 1], 3),
        ][i]
        return remote(src, dst, rs_ss.at[t, i], rs_rs.at[t, i], at_y(rel))

    def ag_copy(t, i):
        src, dst, rel = [
            (ag.at[t, 0, 0], ag.at[t, 3, 0], 1),
            (ag.at[t, 0, 0], ag.at[t, 1, 0], 3),
            (ag.at[t, 3, 0], ag.at[t, 2, 0], 1),
            (ag.at[t, 0, 1], ag.at[t, 1, 1], 3),
            (ag.at[t, 0, 1], ag.at[t, 3, 1], 1),
            (ag.at[t, 1, 1], ag.at[t, 2, 1], 3),
        ][i]
        return remote(src, dst, ag_ss.at[t, i], ag_rs.at[t, i], at_y(rel))

    def h_copy(t, xc, d):
        to = lax.rem(me_x + d, GX)
        return remote(hs.at[xc, to], hr.at[t, xc, me_x], h_ss.at[t, xc, d], h_rs.at[t, xc, d], at_x(d))

    def b_copy(t, xc, d):
        to = lax.rem(me_x + d, GX)
        return remote(bs.at[xc, to], br.at[t, xc, me_x], b_ss.at[t, xc, d], b_rs.at[t, xc, d], at_x(d))

    def over_gx(fn):
        def step(d, carry):
            fn(d)
            return carry

        lax.fori_loop(1, GX, step, 0)

    def scale(jl):
        first = (me_y == 0) & (jl == 0)
        return jnp.where(first, 1.0, 2.0).astype(F32) * (1.0 / float(NX * NY * NZ))

    def forward_block(src, xc, rel):
        h = lax.rem(me_y + rel, GY)
        d = jnp.dot(src[xc * HALF:(xc + 1) * HALF, :], ee[h], preferred_element_type=F32).astype(BF16)
        for xp in range(4):
            r = xp * 128
            rhs = jnp.concatenate(
                [d[r:r + 64, :128], d[r:r + 64, 128:], d[r + 64:r + 128, :128], d[r + 64:r + 128, 128:]], 0
            )
            o = jnp.dot(a2[...], rhs, preferred_element_type=F32)
            part[rel, xc, xp * 192:(xp + 1) * 192, :] = o.astype(BF16)

    def add_part(rel, xc, other):
        part[rel, xc] = (part[rel, xc].astype(F32) + other.astype(F32)).astype(BF16)

    def sum_and_send(t, xc):
        s[...] = part[0, xc].astype(F32) + fl[t, xc].astype(F32) + fr[t, xc].astype(F32)

        def block(gx, carry):
            for k in range(3):
                r = gx * 3 + k
                top = s[pl.ds(r, 8, stride=96), :]
                low = s[pl.ds(r + KEPT, 8, stride=96), :]
                hs[xc, gx, k] = jnp.concatenate([top, low], 0).astype(BF16)
            return carry

        lax.fori_loop(0, GX, block, 0)
        over_gx(lambda d: h_copy(t, xc, d).start())
        hr[t, xc, me_x] = hs[xc, me_x]

    def x_transform(t, put):
        for k in range(3):
            hk = hr[t, :, :, k].reshape(512, 128)
            ht[k * 144:(k + 1) * 144, :] = lax.dot_general(
                pad[...], hk, NT, preferred_element_type=F32
            ).astype(BF16)
        v = jnp.dot(ht[...], fx[...], preferred_element_type=F32).astype(BF16)
        for q in range(2):
            for n in range(2):
                put(q, n * 512, jnp.dot(
                    v[:, q * 128:(q + 1) * 128], spread[:, n * 512:(n + 1) * 512], preferred_element_type=F32
                ))

    def x_inverse_and_send(t):
        y = jnp.dot(lw[...], fold[...], preferred_element_type=F32).astype(BF16)
        for k in range(3):
            both = jnp.concatenate([y[k * 144:(k + 1) * 144], y[432 + k * 144:432 + (k + 1) * 144]], 1)
            yk[k] = jnp.dot(padt[...], both, preferred_element_type=F32).astype(BF16)
        for xc in range(2):
            for k in range(3):
                bx = lax.dot_general(fx[xc * 256:(xc + 1) * 256, :], yk[k], NT, preferred_element_type=F32)
                bs[xc, :, k] = bx.astype(BF16).reshape(GX, 16, 128)
            over_gx(lambda d: b_copy(t, xc, d).start())
            br[t, xc, me_x] = bs[xc, me_x]

    def gather_block(t, xc):
        over_gx(lambda d: b_copy(t, xc, d).wait_recv())

        def block(gx, carry):
            for k in range(3):
                r = gx * 3 + k
                v = br[t, xc, gx, k].astype(F32)
                s[pl.ds(r, 8, stride=96), :] = v[:8]
                s[pl.ds(r + KEPT, 8, stride=96), :] = v[8:]
            return carry

        lax.fori_loop(0, GX, block, 0)
        ag[t, 0, xc] = s[...].astype(BF16)

    def y_inverse(t, xc):
        def block(rel, carry):
            h = lax.rem(me_y + rel, GY)
            off = pl.multiple_of(h * 256, 256)
            for xp in range(4):
                v = jnp.dot(
                    at2[...], ag[t, rel, xc, xp * 192:(xp + 1) * 192, :], preferred_element_type=F32
                ).astype(BF16)
                for x2 in range(2):
                    rows = slice(xp * 128 + x2 * 64, xp * 128 + x2 * 64 + 64)
                    by[rows, pl.ds(off, 128)] = v[x2 * 128:x2 * 128 + 64]
                    by[rows, pl.ds(off + 128, 128)] = v[x2 * 128 + 64:x2 * 128 + 128]
            return carry

        lax.fori_loop(0, GY, block, 0)

    def depth_inverse(xc, finish, start=0, stop=5):
        def block(n, carry):
            cols = pl.ds(pl.multiple_of(n * 256, 256), 256)
            for rb in range(2):
                rows = slice(xc * HALF + rb * 256, xc * HALF + rb * 256 + 256)
                v = jnp.dot(by[rb * 256:rb * 256 + 256, :], eet[:, cols], preferred_element_type=F32)
                finish(rows, cols, v + lin[rows, cols])
            return carry

        lax.fori_loop(start, stop, block, 0)

    def finish_forward(rows, cols, x):
        k0 = math.sqrt(2.0 / math.pi)
        x2 = x * x
        th = jnp.tanh(k0 * x * (1.0 + 0.044715 * x2))
        half = 0.5 * (1.0 + th)
        out[rows, cols] = (x * half).astype(BF16)
        slope = half + 0.5 * x * (1.0 - th * th) * (k0 * (1.0 + 3.0 * 0.044715 * x2))
        g[rows, cols] = (cot[rows, cols].astype(F32) * slope).astype(BF16)

    def finish_backward(rows, cols, x):
        out[rows, cols] = x.astype(BF16)

    def build_kron(dims):
        at = lax.broadcasted_iota(jnp.int32, (C, CZ), 1) >> 6
        one = jnp.where(at == lax.broadcasted_iota(jnp.int32, (C, CZ), 0), 1.0, 0.0).astype(BF16)
        mixrows[...] = lax.dot_general(mix_ref[...], one, dims, preferred_element_type=F32)

        lane = lax.broadcasted_iota(jnp.int32, (NZ, CZ), 1) & (NZ - 1)
        row = lax.broadcasted_iota(jnp.int32, (NZ, CZ), 0)
        eye = jnp.where(lane == row, 1.0, 0.0).astype(F32)

        def block(c, carry):
            kron[pl.ds(pl.multiple_of(c * NZ, NZ), NZ), :] = (eye * mixrows[pl.ds(c, 1), :]).astype(BF16)
            return carry

        lax.fori_loop(0, C, block, 0)

    def linear(src, rb):
        def block(n, carry):
            cols = pl.ds(pl.multiple_of(n * 256, 256), 256)
            rows = slice(rb * 512, rb * 512 + 512)
            lin[rows, cols] = jnp.dot(src[rows, :], kron[:, cols], preferred_element_type=F32)
            return carry

        lax.fori_loop(0, 5, block, 0)

    def fill_weights():
        wp[...] = jnp.zeros_like(wp)
        for k in range(3):
            def block(j, carry):
                v = w[k, j].astype(F32)
                for p in range(2):
                    wp[k, j, p, :C, :C * KEPT] = v[:, p, :]
                return carry

            lax.fori_loop(0, 6, block, 0)
        lane = lax.broadcasted_iota(jnp.int32, (24, 1024), 1)
        first = lax.broadcasted_iota(jnp.int32, (24, 1024), 0) * KEPT
        mask[...] = jnp.where((lane >= first) & (lane < first + KEPT) & (lane < C * KEPT), 1.0, 0.0).astype(F32)

    def put_uh(q, at, v):
        uh[q, :, at:at + 512] = v

    def put_lin(q, at, v):
        lin[q * 432:(q + 1) * 432, at:at + 512] = v

    def put_rows(k, jp, re, im):
        at = pl.multiple_of(k * 144 + jp * 48, 48)
        lw[pl.ds(at, 48), :] = jnp.concatenate(re, 0).astype(BF16)
        lw[pl.ds(at + 432, 48), :] = jnp.concatenate(im, 0).astype(BF16)

    def mix_block(k, carry):
        for jp in range(3):
            re, im = [], []
            for j in (2 * jp, 2 * jp + 1):
                rows = pl.ds(pl.multiple_of(k * 144 + j * 24, 8), 24)
                a, b = uh[0, rows, :], uh[1, rows, :]
                r, w = wp[k, j, 0], wp[k, j, 1]
                re.append(mask[...] * (jnp.sum(a * r - b * w, 0, keepdims=True) * scale(j)))
                im.append(mask[...] * (jnp.sum(a * w + b * r, 0, keepdims=True) * scale(j)))
            put_rows(k, jp, re, im)
        return carry

    def adjoint_block(k, carry):
        for jp in range(3):
            re, im = [], []
            for j in (2 * jp, 2 * jp + 1):
                at = pl.multiple_of(k * 144 + j * 24, 8)
                r, w = wp[k, j, 0], wp[k, j, 1]
                gr = jnp.sum(lin[pl.ds(at, 24), :1024] * mask[...], 0, keepdims=True) * scale(j)
                gi = jnp.sum(lin[pl.ds(at + 432, 24), :1024] * mask[...], 0, keepdims=True) * scale(j)
                gh[k, j, 0:1, :] = gr
                gh[k, j, 1:2, :] = gi
                re.append(gr * r + gi * w)
                im.append(gi * r - gr * w)
            put_rows(k, jp, re, im)
        return carry

    def weight_terms(k, j):
        rows = pl.ds(pl.multiple_of(k * 144 + j * 24, 8), 24)
        a, b = uh[0, rows, :], uh[1, rows, :]
        gr, gi = gh[k, j, 0:1, :], gh[k, j, 1:2, :]
        return a * gr + b * gi, a * gi - b * gr

    def gs_copy():
        return remote(gss, gsr, gs_sem.at[0], gs_sem.at[1], twin)

    def weight_gradient_send():
        def block(k, carry):
            for jj in range(3):
                re, im = weight_terms(k, (1 - me_t) * 3 + jj)
                at = pl.multiple_of(k * 144 + jj * 48, 48)
                gss[pl.ds(at, 48), :] = jnp.concatenate([re, im], 0).astype(BF16)
            return carry

        lax.fori_loop(0, 3, block, 0)
        gs_copy().start()

    def weight_gradient_finish():
        gs_copy().wait_recv()

        def block(k, carry):
            for jj in range(3):
                re, im = weight_terms(k, me_t * 3 + jj)
                at = pl.multiple_of(k * 144 + jj * 48, 48)
                other = gsr[pl.ds(at, 48), :].astype(F32)
                gs_ref[k, jj, :, 0, :] = (re + other[:24])[:C, :C * KEPT]
                gs_ref[k, jj, :, 1, :] = (im + other[24:])[:C, :C * KEPT]
            return carry

        lax.fori_loop(0, 3, block, 0)

    def mixing_terms():
        lane = lax.broadcasted_iota(jnp.int32, (256, 256), 1) & (NZ - 1)
        row = lax.broadcasted_iota(jnp.int32, (256, 256), 0) & (NZ - 1)
        eye = jnp.where(lane == row, 1.0, 0.0).astype(F32)

        def block(cb, carry):
            cols = pl.ds(pl.multiple_of(cb * 256, 256), 256)
            for nb in range(5):
                o = lax.dot_general(
                    u[:, cols], g[:, nb * 256:(nb + 1) * 256], TN, preferred_element_type=F32
                )
                gmx[cb, 0:4, nb * 256:(nb + 1) * 256] = jnp.sum((o * eye).reshape(4, NZ, 256), 1)
            return carry

        gmx[...] = jnp.zeros_like(gmx)
        lax.fori_loop(0, 5, block, 0)
        v = gmx[...].reshape(40, CZ)
        hi = v.astype(BF16)
        low = (v - hi.astype(F32)).astype(BF16)
        sel = lax.broadcasted_iota(jnp.int32, (CZ, 128), 0) >> 6
        sel = jnp.where(sel == lax.broadcasted_iota(jnp.int32, (CZ, 128), 1), 1.0, 0.0).astype(BF16)
        gmy[0] = jnp.dot(hi, sel, preferred_element_type=F32) + jnp.dot(low, sel, preferred_element_type=F32)

    def gy_copy(rel):
        return remote(gmy.at[0], gmy.at[rel], gy_ss.at[rel], gy_rs.at[rel], at_y(rel))

    def gx_copy(d):
        return remote(gma.at[0], gma.at[d], gx_ss.at[d], gx_rs.at[d], at_x(d))

    def ta_copy():
        return remote(gma.at[16], gma.at[17], ta_sem.at[0], ta_sem.at[1], twin)

    for i in range(3):
        loads[i].wait()
    forward_block(u, 0, 2)
    pl.semaphore_wait(barrier, 19)
    rs_copy(0, 0).start()
    loads[3].wait()
    forward_block(u, 0, 3)
    rs_copy(0, 1).start()
    loads[4].wait()
    forward_block(u, 1, 2)
    rs_copy(0, 3).start()
    loads[5].wait()
    forward_block(u, 1, 1)
    rs_copy(0, 4).start()
    forward_block(u, 0, 1)
    loads[6].wait()
    forward_block(u, 0, 0)
    rs_copy(0, 0).wait_recv()
    add_part(1, 0, dg[0, 0])
    rs_copy(0, 2).start()
    forward_block(u, 1, 3)
    rs_copy(0, 3).wait_recv()
    add_part(3, 1, dg[0, 1])
    rs_copy(0, 5).start()
    forward_block(u, 1, 0)
    loads[7].wait()
    fill_weights()
    build_kron((((1,), (0,)), ((), ())))
    for i in range(8, 16):
        loads[i].wait()
    rs_copy(0, 1).wait_recv()
    rs_copy(0, 2).wait_recv()
    sum_and_send(0, 0)
    rs_copy(0, 4).wait_recv()
    rs_copy(0, 5).wait_recv()
    sum_and_send(0, 1)
    over_gx(lambda d: h_copy(0, 0, d).wait_recv())
    over_gx(lambda d: h_copy(0, 1, d).wait_recv())

    x_transform(0, put_uh)
    lax.fori_loop(0, 3, mix_block, 0)
    x_inverse_and_send(0)

    def gather(t, src):
        gather_block(t, 0)
        ag_copy(t, 0).start()
        ag_copy(t, 1).start()
        gather_block(t, 1)
        ag_copy(t, 3).start()
        linear(src, 0)
        ag_copy(t, 0).wait_recv()
        ag_copy(t, 2).start()
        ag_copy(t, 4).start()
        ag_copy(t, 3).wait_recv()
        ag_copy(t, 5).start()
        linear(src, 1)

    gather(0, u)
    for i in range(6):
        rs_copy(0, i).wait_send()
    for xc in range(2):
        over_gx(lambda d: h_copy(0, xc, d).wait_send())
        over_gx(lambda d: b_copy(0, xc, d).wait_send())

    ag_copy(0, 1).wait_recv()
    ag_copy(0, 2).wait_recv()
    y_inverse(0, 0)
    depth_inverse(0, finish_forward)
    act_out = [
        pltpu.make_async_copy(out.at[pl.ds(xc * HALF, HALF)], act_hbm.at[pl.ds(xc * HALF, HALF)], out_sem.at[0, xc])
        for xc in range(2)
    ]
    act_out[0].start()
    forward_block(g, 0, 2)
    rs_copy(1, 0).start()
    forward_block(g, 0, 3)
    rs_copy(1, 1).start()
    forward_block(g, 0, 1)
    ag_copy(0, 4).wait_recv()
    ag_copy(0, 5).wait_recv()
    y_inverse(0, 1)
    depth_inverse(1, finish_forward, 0, 3)
    rs_copy(1, 0).wait_recv()
    add_part(1, 0, dg[1, 0])
    rs_copy(1, 2).start()
    depth_inverse(1, finish_forward, 3, 5)
    act_out[1].start()
    forward_block(g, 1, 2)
    rs_copy(1, 3).start()
    forward_block(g, 1, 1)
    rs_copy(1, 4).start()
    forward_block(g, 1, 3)
    forward_block(g, 0, 0)
    forward_block(g, 1, 0)
    rs_copy(1, 3).wait_recv()
    add_part(3, 1, dg[1, 1])
    rs_copy(1, 5).start()
    mixing_terms()
    for rel in (1, 2, 3):
        gy_copy(rel).start()
    rs_copy(1, 1).wait_recv()
    rs_copy(1, 2).wait_recv()
    sum_and_send(1, 0)
    rs_copy(1, 4).wait_recv()
    rs_copy(1, 5).wait_recv()
    sum_and_send(1, 1)
    for rel in (1, 2, 3):
        gy_copy(rel).wait_recv()
    gma[0] = gmy[0] + gmy[1] + gmy[2] + gmy[3]
    over_gx(lambda d: gx_copy(d).start())
    over_gx(lambda d: h_copy(1, 0, d).wait_recv())
    over_gx(lambda d: h_copy(1, 1, d).wait_recv())

    x_transform(1, put_lin)
    lax.fori_loop(0, 3, adjoint_block, 0)
    x_inverse_and_send(1)
    weight_gradient_send()
    build_kron(TN)
    gather(1, g)
    over_gx(lambda d: gx_copy(d).wait_recv())
    gma[16] = jnp.sum(gma[0:16], 0)
    ta_copy().start()
    weight_gradient_finish()
    act_out[0].wait()
    act_out[1].wait()
    ag_copy(1, 1).wait_recv()
    ag_copy(1, 2).wait_recv()
    y_inverse(1, 0)
    depth_inverse(0, finish_backward)
    gf_out = [
        pltpu.make_async_copy(out.at[pl.ds(xc * HALF, HALF)], gf_hbm.at[pl.ds(xc * HALF, HALF)], out_sem.at[1, xc])
        for xc in range(2)
    ]
    gf_out[0].start()
    ag_copy(1, 4).wait_recv()
    ag_copy(1, 5).wait_recv()
    y_inverse(1, 1)
    depth_inverse(1, finish_backward)
    gf_out[1].start()
    ta_copy().wait_recv()
    total = (gma[16] + gma[17]) * (1.0 / math.sqrt(2 * NX * NY * NZ))
    for cb in range(5):
        gm_ref[cb * 4:(cb + 1) * 4, :] = total[cb * 8:cb * 8 + 4, :C]

    for t in range(2):
        for i in range(6):
            ag_copy(t, i).wait_send()
    for i in range(6):
        rs_copy(1, i).wait_send()
    for xc in range(2):
        over_gx(lambda d: h_copy(1, xc, d).wait_send())
        over_gx(lambda d: b_copy(1, xc, d).wait_send())
    gs_copy().wait_send()
    for rel in (1, 2, 3):
        gy_copy(rel).wait_send()
    over_gx(lambda d: gx_copy(d).wait_send())
    ta_copy().wait_send()
    gf_out[0].wait()
    gf_out[1].wait()


def hand_over(act_in, gf_in, gs_in, gm_in, act_out, gf_out, gs_out, gm_out, act, gf, gs, gm, in_sem, out_sem):
    pieces = [(gs_in.at[k], gs.at[k], gs_out.at[k]) for k in range(3)] + [(gm_in, gm, gm_out)]
    for i in range(4):
        rows = pl.ds(i * 256, 256)
        pieces.append((act_in.at[rows], act.at[rows], act_out.at[rows]))
        pieces.append((gf_in.at[rows], gf.at[rows], gf_out.at[rows]))
    loads = [pltpu.make_async_copy(p[0], p[1], in_sem.at[i]) for i, p in enumerate(pieces)]
    stores = [pltpu.make_async_copy(p[1], p[2], out_sem.at[i]) for i, p in enumerate(pieces)]
    for load in loads:
        load.start()
    for load, store in zip(loads, stores):
        load.wait()
        store.start()
    for store in stores:
        store.wait()


def shards(features, cotangent, spectral_weight, mixing_weight):
    consts = [jnp.asarray(t) for t in tables()]
    dma = pltpu.SemaphoreType.DMA
    vmem = pltpu.VMEM
    hbm = pl.BlockSpec(memory_space=pl.ANY)
    local = pl.BlockSpec(memory_space=pltpu.VMEM)
    results = (
        jax.ShapeDtypeStruct((ROWS, CZ), BF16),
        jax.ShapeDtypeStruct((ROWS, CZ), BF16),
        jax.ShapeDtypeStruct((3, 3, C, 2, C * KEPT), F32),
        jax.ShapeDtypeStruct((C, C), F32),
    )
    parts = pl.pallas_call(
        kernel,
        out_shape=results,
        in_specs=[hbm, hbm, hbm, local] + [hbm] * 9,
        out_specs=(hbm, hbm, local, local),
        scratch_shapes=[
            vmem((ROWS, CZ), BF16),
            vmem((ROWS, CZ), BF16),
            vmem((ROWS, CZ), BF16),
            vmem((ROWS, CZ), BF16),
            vmem((GY, CZ, 256), BF16),
            vmem((GY * 256, CZ), BF16),
            vmem((CZ, CZ), BF16),
            vmem((ROWS, CZ), F32),
            vmem((512, 256), BF16),
            vmem((144, 128), BF16),
            vmem((128, 144), BF16),
            vmem((128, 1024), BF16),
            vmem((1024, 128), BF16),
            vmem((192, 256), BF16),
            vmem((256, 192), BF16),
            vmem((3, 6, C, 2, C * KEPT), BF16),
            vmem((C, CZ), F32),
            vmem((3, 6, 2, 24, 1024), F32),
            vmem((2, 432, 1024), F32),
            vmem((432, 512), BF16),
            vmem((3, 128, 256), BF16),
            vmem((864, 1024), BF16),
            vmem((432, 1024), BF16),
            vmem((432, 1024), BF16),
            vmem((4, 2, 768, 128), BF16),
            vmem((2, 2, 768, 128), BF16),
            vmem((2, 2, 768, 128), BF16),
            vmem((2, 2, 768, 128), BF16),
            vmem((2, GX, 3, 16, 128), BF16),
            vmem((2, 2, GX, 3, 16, 128), BF16),
            vmem((2, GX, 3, 16, 128), BF16),
            vmem((2, 2, GX, 3, 16, 128), BF16),
            vmem((2, 4, 2, 768, 128), BF16),
            vmem((HALF, 1024), BF16),
            vmem((768, 128), F32),
            vmem((24, 1024), F32),
            vmem((3, 6, 8, 1024), F32),
            vmem((5, 8, CZ), F32),
            vmem((4, 40, 128), F32),
            vmem((18, 40, 128), F32),
            dma((16,)),
            dma((2, 2)),
            dma((2, 6)),
            dma((2, 6)),
            dma((2, 2, GX)),
            dma((2, 2, GX)),
            dma((2, 2, GX)),
            dma((2, 2, GX)),
            dma((2, 6)),
            dma((2, 6)),
            dma((2,)),
            dma((4,)),
            dma((4,)),
            dma((GX,)),
            dma((GX,)),
            dma((2,)),
        ],
        compiler_params=pltpu.CompilerParams(
            collective_id=0, has_side_effects=True, vmem_limit_bytes=60 * 1024 * 1024
        ),
    )(
        features.reshape(ROWS, CZ), cotangent.reshape(ROWS, CZ),
        spectral_weight.transpose(0, 1, 3, 2, 4), mixing_weight, *consts,
    )
    act, gf, gs, gm = pl.pallas_call(
        hand_over,
        out_shape=results,
        in_specs=[hbm] * 4,
        out_specs=(hbm,) * 4,
        scratch_shapes=[vmem(r.shape, r.dtype) for r in results] + [dma((12,)), dma((12,))],
        compiler_params=pltpu.CompilerParams(vmem_limit_bytes=60 * 1024 * 1024),
    )(*parts)
    return act.reshape(features.shape), gf.reshape(features.shape), gs.transpose(0, 1, 3, 2, 4), gm


def solution(mesh):
    in_specs = (
        P("ta", "gx", "gy", None),
        P("ta", "gx", "gy", None),
        P("gx", "gy", None, None, None),
        P(),
    )
    out_specs = (
        P("ta", "gx", "gy", None),
        P("ta", "gx", "gy", None),
        P("gx", ("gy", "ta"), None, None, None),
        P(),
    )
    return jax.shard_map(shards, mesh=mesh, in_specs=in_specs, out_specs=out_specs, check_vma=False)
```

```python
import math

import jax
import jax.numpy as jnp
import ml_dtypes
import numpy as np
from jax import lax
from jax.experimental import pallas as pl
from jax.experimental.pallas import tpu as pltpu
from jax.sharding import PartitionSpec as P

NX = 256
NY = 256
NZ = 64
C = 20
M = 24
KEPT = 48
CZ = C * NZ
GX = 16
GY = 4
ROWS = 1024
HALF = 512
F32 = jnp.float32
BF16 = jnp.bfloat16
MESH = pl.DeviceIdType.MESH
NT = (((1,), (1,)), ((), ()))
TN = (((0,), (0,)), ((), ()))


def cos_sin(length, count, folded):
    freq = np.arange(count)
    if folded:
        freq = np.where(freq < count // 2, freq, freq + length - count)
    phases = np.arange(length)[:, None] * freq[None, :] % length
    angles = phases.astype(np.float32) * np.float32(2.0 * math.pi / length)
    return np.cos(angles), np.sin(angles)


def complex_table(length, count):
    cosine, sine = cos_sin(length, count, True)
    return np.stack([np.stack([cosine, -sine], 1), np.stack([sine, cosine], 1)], 0)


def tables():
    cosine, sine = cos_sin(NZ, M, False)
    depth = np.stack([cosine, -sine], 1)
    ee = np.zeros((GY, C, NZ, 2, 128), np.float32)
    for h in range(GY):
        for jl in range(6):
            for c in range(C):
                ee[h, c, :, :, jl * C + c] = depth[:, :, h * 6 + jl]
    ee = ee.reshape(GY, CZ, 256)
    eet = np.ascontiguousarray(ee.transpose(0, 2, 1)).reshape(GY * 256, CZ)
    height = complex_table(NY, KEPT).reshape(2, GY, 64, 2, KEPT)
    height = height.transpose(1, 3, 4, 0, 2).reshape(GY, 2, GX, 3, 2, 64)
    a2 = np.zeros((GY, 192, 2, 2, 64), np.float32)
    for x2 in range(2):
        a2[:, x2 * 64:x2 * 64 + 64, x2] = height[:, :, :, :2].reshape(GY, 64, 2, 64)
        a2[:, 128 + x2 * 32:160 + x2 * 32, x2] = height[:, :, :, 2].reshape(GY, 32, 2, 64)
    a2 = a2.reshape(GY, 192, 256)
    at2 = np.ascontiguousarray(a2.transpose(0, 2, 1))
    width = complex_table(NX, KEPT).reshape(2, GX, 2, 8, 2, KEPT)
    fx = np.zeros((2, GX, 2, 8, 2, 64), np.float32)
    fx[..., :KEPT] = width.transpose(2, 1, 0, 3, 4, 5)
    fx = fx.reshape(512, 128)
    spread = np.zeros((2, 128, 1024), np.float32)
    for q in range(2):
        for c in range(C):
            spread[q, q * 64 + np.arange(KEPT), c * KEPT + np.arange(KEPT)] = 1.0
    fold = np.ascontiguousarray(spread.transpose(0, 2, 1))
    pad = np.zeros((6, 24, 128), np.float32)
    for jl in range(6):
        for c in range(C):
            pad[jl, c, jl * C + c] = 1.0
    pad = pad.reshape(144, 128)
    padt = np.ascontiguousarray(pad.T)
    return [t.astype(ml_dtypes.bfloat16) for t in (ee, eet, a2, at2, fx, pad, padt, spread, fold)]


def kernel(
    u_hbm, cot_hbm, w_hbm, mix_ref, ee_hbm, eet_hbm, a2_hbm, at2_hbm, fx_hbm, pad_hbm, padt_hbm, spread_hbm, fold_hbm,
    act_hbm, gf_hbm, gs_ref, gm_ref,
    u, cot, g, out, ee, eet, kron, lin, fx, pad, padt, spread, fold, a2, at2, w, mixrows, wp, uh, ht, yk, lw, gss, gsr,
    part, dg, fl, fr, hs, hr, bs, br, ag, hsb, hrb, bsb, brb, pu, pb, yb, agb, by, s, sb, mask, gh, gmx, gmy, gma,
    in_sem, out_sem, rs_ss, rs_rs, h_ss, h_rs, b_ss, b_rs, ag_ss, ag_rs,
    hb_ss, hb_rs, bb_ss, bb_rs, pb_ss, pb_rs, yb_ss, yb_rs, gs_sem, gy_ss, gy_rs, gx_ss, gx_rs, ta_sem,
):
    me_x = lax.axis_index("gx")
    me_y = lax.axis_index("gy")
    me_t = lax.axis_index("ta")

    def at_y(rel):
        return (me_x, lax.rem(me_y + rel, GY), me_t)

    def at_x(d):
        return (lax.rem(me_x + d, GX), me_y, me_t)

    twin = (me_x, me_y, 1 - me_t)

    opposite, left = lax.rem(me_y + 2, GY), lax.rem(me_y + 3, GY)
    right = lax.rem(me_y + 1, GY)
    first, second = pl.ds(0, HALF), pl.ds(HALF, HALF)
    loads = [
        pltpu.make_async_copy(src, dst, in_sem.at[i])
        for i, (src, dst) in enumerate([
            (u_hbm.at[first], u.at[first]), (ee_hbm.at[opposite], ee.at[opposite]), (a2_hbm.at[me_y], a2),
            (ee_hbm.at[left], ee.at[left]), (u_hbm.at[second], u.at[second]), (ee_hbm.at[right], ee.at[right]),
            (ee_hbm.at[me_y], ee.at[me_y]), (w_hbm, w), (fx_hbm, fx), (pad_hbm, pad), (padt_hbm, padt),
            (spread_hbm, spread), (fold_hbm, fold), (at2_hbm.at[me_y], at2), (eet_hbm, eet), (cot_hbm, cot),
        ])
    ]
    for load in loads:
        load.start()

    barrier = pltpu.get_barrier_semaphore()
    for rel in (1, 2, 3):
        pl.semaphore_signal(barrier, inc=1, device_id=at_y(rel), device_id_type=MESH)

    def greet(d, carry):
        pl.semaphore_signal(barrier, inc=1, device_id=at_x(d), device_id_type=MESH)
        return carry

    lax.fori_loop(1, GX, greet, 0)
    pl.semaphore_signal(barrier, inc=1, device_id=twin, device_id_type=MESH)

    def remote(src, dst, ss, rs, dev):
        return pltpu.make_async_remote_copy(
            src_ref=src, dst_ref=dst, send_sem=ss, recv_sem=rs, device_id=dev, device_id_type=MESH
        )

    def rs_copy(t, i):
        src, dst, rel = [
            (part.at[2, 0], dg.at[t, 0], 1),
            (part.at[3, 0], fr.at[t, 0], 3),
            (part.at[1, 0], fl.at[t, 0], 1),
            (part.at[2, 1], dg.at[t, 1], 3),
            (part.at[1, 1], fl.at[t, 1], 1),
            (part.at[3, 1], fr.at[t, 1], 3),
        ][i]
        return remote(src, dst, rs_ss.at[t, i], rs_rs.at[t, i], at_y(rel))

    def ag_copy(t, i):
        src, dst, rel = [
            (ag.at[t, 0, 0], ag.at[t, 3, 0], 1),
            (ag.at[t, 0, 0], ag.at[t, 1, 0], 3),
            (ag.at[t, 3, 0], ag.at[t, 2, 0], 1),
            (ag.at[t, 0, 1], ag.at[t, 1, 1], 3),
            (ag.at[t, 0, 1], ag.at[t, 3, 1], 1),
            (ag.at[t, 1, 1], ag.at[t, 2, 1], 3),
        ][i]
        return remote(src, dst, ag_ss.at[t, i], ag_rs.at[t, i], at_y(rel))

    def h_copy(t, xc, d):
        to = lax.rem(me_x + d, GX)
        return remote(hs.at[xc, to], hr.at[t, xc, me_x], h_ss.at[t, xc, d], h_rs.at[t, xc, d], at_x(d))

    def b_copy(t, xc, d):
        to = lax.rem(me_x + d, GX)
        return remote(bs.at[xc, to], br.at[t, xc, me_x], b_ss.at[t, xc, d], b_rs.at[t, xc, d], at_x(d))

    def hb_copy(t, xc, d):
        to = lax.rem(me_x + d, GX)
        return remote(hsb.at[xc, to], hrb.at[t, xc, me_x], hb_ss.at[t, xc, d], hb_rs.at[t, xc, d], at_x(d))

    def bb_copy(t, xc, d):
        to = lax.rem(me_x + d, GX)
        return remote(bsb.at[xc, to], brb.at[t, xc, me_x], bb_ss.at[t, xc, d], bb_rs.at[t, xc, d], at_x(d))

    def pb_copy(t, rel):
        return remote(pu.at[2 + rel], pb.at[t, rel], pb_ss.at[t, rel], pb_rs.at[t, rel], at_y(rel))

    def yb_copy(t, rel):
        return remote(yb.at[t, 0], yb.at[t, GY - rel], yb_ss.at[t, rel], yb_rs.at[t, rel], at_y(rel))

    def over_gx(fn):
        def step(d, carry):
            fn(d)
            return carry

        lax.fori_loop(1, GX, step, 0)

    def scale(jl):
        first = (me_y == 0) & (jl == 0)
        return jnp.where(first, 1.0, 2.0).astype(F32) * (1.0 / float(NX * NY * NZ))

    def forward_block(src, xc, rel):
        h = lax.rem(me_y + rel, GY)
        d = jnp.dot(src[xc * HALF:(xc + 1) * HALF, :], ee[h], preferred_element_type=F32).astype(BF16)
        for xp in range(4):
            r = xp * 128
            rhs = jnp.concatenate(
                [d[r:r + 64, :128], d[r:r + 64, 128:], d[r + 64:r + 128, :128], d[r + 64:r + 128, 128:]], 0
            )
            o = jnp.dot(a2[...], rhs, preferred_element_type=F32)
            part[rel, xc, xp * 128:(xp + 1) * 128, :] = o[:128].astype(BF16)
            sb[xp * 64:(xp + 1) * 64, :] = o[128:]
        for gx in range(GX):
            top = sb[pl.ds(gx, 8, stride=32), :]
            low = sb[pl.ds(gx + GX, 8, stride=32), :]
            hsb[xc, gx, rel] = jnp.concatenate([top, low], 0).astype(BF16)

    def send_third(t, xc):
        over_gx(lambda d: hb_copy(t, xc, d).start())
        hrb[t, xc, me_x] = hsb[xc, me_x]

    def add_part(rel, xc, other):
        part[rel, xc] = (part[rel, xc].astype(F32) + other.astype(F32)).astype(BF16)

    def sum_and_send(t, xc):
        s[...] = part[0, xc].astype(F32) + fl[t, xc].astype(F32) + fr[t, xc].astype(F32)

        def block(gx, carry):
            for k in range(2):
                r = gx * 2 + k
                top = s[pl.ds(r, 8, stride=64), :]
                low = s[pl.ds(r + 32, 8, stride=64), :]
                hs[xc, gx, k] = jnp.concatenate([top, low], 0).astype(BF16)
            return carry

        lax.fori_loop(0, GX, block, 0)
        over_gx(lambda d: h_copy(t, xc, d).start())
        hr[t, xc, me_x] = hs[xc, me_x]

    def x_third(t):
        for rel in range(GY):
            hk = hrb[t, :, :, rel].reshape(512, 128)
            ht[rel * 144:(rel + 1) * 144, :] = lax.dot_general(
                pad[...], hk, NT, preferred_element_type=F32
            ).astype(BF16)
        v = jnp.dot(ht[...], fx[...], preferred_element_type=F32).astype(BF16)
        pu[2] = v[:144]
        for rel in (1, 2, 3):
            pu[2 + rel] = v[rel * 144:(rel + 1) * 144]
            pb_copy(t, rel).start()

    def x_transform(t, put):
        for k in range(2):
            hk = hr[t, :, :, k].reshape(512, 128)
            v = lax.dot_general(pad[...], hk, NT, preferred_element_type=F32).astype(BF16)
            pu[k] = jnp.dot(v, fx[...], preferred_element_type=F32).astype(BF16)
        for rel in (1, 2, 3):
            pb_copy(t, rel).wait_recv()
        third = pu[2].astype(F32) + pb[t, 1].astype(F32) + pb[t, 2].astype(F32) + pb[t, 3].astype(F32)
        v = jnp.concatenate([pu[0], pu[1], third.astype(BF16)], 0)
        for q in range(2):
            for n in range(2):
                put(q, n * 512, jnp.dot(v, spread[q, :, n * 512:(n + 1) * 512], preferred_element_type=F32))

    def x_inverse_and_send(t):
        y = jnp.dot(lw[:432, :], fold[0], preferred_element_type=F32)
        y = (y + jnp.dot(lw[432:, :], fold[1], preferred_element_type=F32)).astype(BF16)
        for k in (2, 0, 1):
            v = jnp.dot(padt[...], y[k * 144:(k + 1) * 144], preferred_element_type=F32).astype(BF16)
            if k == 2:
                yb[t, 0] = v
                for rel in (1, 2, 3):
                    yb_copy(t, rel).start()
            else:
                yk[k] = v
        for xc in range(2):
            for k in range(2):
                bx = lax.dot_general(fx[xc * 256:(xc + 1) * 256, :], yk[k], NT, preferred_element_type=F32)
                bs[xc, :, k] = bx.astype(BF16).reshape(GX, 16, 128)
            over_gx(lambda d: b_copy(t, xc, d).start())
            br[t, xc, me_x] = bs[xc, me_x]

    def third_inverse_and_send(t):
        for rel in (1, 2, 3):
            yb_copy(t, rel).wait_recv()
        for xc in range(2):
            for rel in range(GY):
                bx = lax.dot_general(fx[xc * 256:(xc + 1) * 256, :], yb[t, rel], NT, preferred_element_type=F32)
                bsb[xc, :, rel] = bx.astype(BF16).reshape(GX, 16, 128)
            over_gx(lambda d: bb_copy(t, xc, d).start())
            brb[t, xc, me_x] = bsb[xc, me_x]

    def gather_block(t, xc):
        over_gx(lambda d: b_copy(t, xc, d).wait_recv())

        def block(gx, carry):
            for k in range(2):
                r = gx * 2 + k
                v = br[t, xc, gx, k].astype(F32)
                s[pl.ds(r, 8, stride=64), :] = v[:8]
                s[pl.ds(r + 32, 8, stride=64), :] = v[8:]
            return carry

        lax.fori_loop(0, GX, block, 0)
        ag[t, 0, xc] = s[...].astype(BF16)

    def gather_third(t, xc):
        over_gx(lambda d: bb_copy(t, xc, d).wait_recv())
        for rel in range(GY):
            for gx in range(GX):
                v = brb[t, xc, gx, rel].astype(F32)
                sb[pl.ds(gx, 8, stride=32), :] = v[:8]
                sb[pl.ds(gx + GX, 8, stride=32), :] = v[8:]
            agb[rel] = sb[...].astype(BF16)

    def y_inverse(t, xc):
        for rel in range(GY):
            h = lax.rem(me_y + rel, GY)
            off = pl.multiple_of(h * 256, 256)
            for xp in range(4):
                rhs = jnp.concatenate(
                    [ag[t, rel, xc, xp * 128:(xp + 1) * 128, :], agb[rel, xp * 64:(xp + 1) * 64, :]], 0
                )
                v = jnp.dot(at2[...], rhs, preferred_element_type=F32).astype(BF16)
                for x2 in range(2):
                    rows = slice(xp * 128 + x2 * 64, xp * 128 + x2 * 64 + 64)
                    by[rows, pl.ds(off, 128)] = v[x2 * 128:x2 * 128 + 64]
                    by[rows, pl.ds(off + 128, 128)] = v[x2 * 128 + 64:x2 * 128 + 128]

    def depth_inverse(xc, finish, start=0, stop=5):
        def block(n, carry):
            cols = pl.ds(pl.multiple_of(n * 256, 256), 256)
            for rb in range(2):
                rows = slice(xc * HALF + rb * 256, xc * HALF + rb * 256 + 256)
                v = jnp.dot(by[rb * 256:rb * 256 + 256, :], eet[:, cols], preferred_element_type=F32)
                finish(rows, cols, v + lin[rows, cols])
            return carry

        lax.fori_loop(start, stop, block, 0, unroll=True)

    def finish_forward(rows, cols, x):
        k0 = math.sqrt(2.0 / math.pi)
        x2 = x * x
        th = jnp.tanh(k0 * x * (1.0 + 0.044715 * x2))
        half = 0.5 * (1.0 + th)
        out[rows, cols] = (x * half).astype(BF16)
        slope = half + 0.5 * x * (1.0 - th * th) * (k0 * (1.0 + 3.0 * 0.044715 * x2))
        g[rows, cols] = (cot[rows, cols].astype(F32) * slope).astype(BF16)

    def finish_backward(rows, cols, x):
        out[rows, cols] = x.astype(BF16)

    def build_kron(dims):
        at = lax.broadcasted_iota(jnp.int32, (C, CZ), 1) >> 6
        one = jnp.where(at == lax.broadcasted_iota(jnp.int32, (C, CZ), 0), 1.0, 0.0).astype(BF16)
        mixrows[...] = lax.dot_general(mix_ref[...], one, dims, preferred_element_type=F32)

        lane = lax.broadcasted_iota(jnp.int32, (NZ, CZ), 1) & (NZ - 1)
        row = lax.broadcasted_iota(jnp.int32, (NZ, CZ), 0)
        eye = jnp.where(lane == row, 1.0, 0.0).astype(F32)

        def block(c, carry):
            kron[pl.ds(pl.multiple_of(c * NZ, NZ), NZ), :] = (eye * mixrows[pl.ds(c, 1), :]).astype(BF16)
            return carry

        lax.fori_loop(0, C, block, 0)

    def linear(src, rb):
        def block(n, carry):
            cols = pl.ds(pl.multiple_of(n * 256, 256), 256)
            rows = slice(rb * 512, rb * 512 + 512)
            lin[rows, cols] = jnp.dot(src[rows, :], kron[:, cols], preferred_element_type=F32)
            return carry

        lax.fori_loop(0, 5, block, 0)

    def fill_weights():
        wp[...] = jnp.zeros_like(wp)
        for k in range(3):
            def block(j, carry):
                v = w[k, j].astype(F32)
                for p in range(2):
                    wp[k, j, p, :C, :C * KEPT] = v[:, p, :]
                return carry

            lax.fori_loop(0, 6, block, 0)
        lane = lax.broadcasted_iota(jnp.int32, (24, 1024), 1)
        first = lax.broadcasted_iota(jnp.int32, (24, 1024), 0) * KEPT
        mask[...] = jnp.where((lane >= first) & (lane < first + KEPT) & (lane < C * KEPT), 1.0, 0.0).astype(F32)

    def put_uh(q, at, v):
        uh[q, :, at:at + 512] = v

    def put_lin(q, at, v):
        lin[q * 432:(q + 1) * 432, at:at + 512] = v

    def put_rows(k, jp, re, im):
        at = pl.multiple_of(k * 144 + jp * 48, 48)
        lw[pl.ds(at, 48), :] = jnp.concatenate(re, 0).astype(BF16)
        lw[pl.ds(at + 432, 48), :] = jnp.concatenate(im, 0).astype(BF16)

    def mix_block(k, carry):
        for jp in range(3):
            re, im = [], []
            for j in (2 * jp, 2 * jp + 1):
                rows = pl.ds(pl.multiple_of(k * 144 + j * 24, 8), 24)
                a, b = uh[0, rows, :], uh[1, rows, :]
                r, w = wp[k, j, 0], wp[k, j, 1]
                re.append(mask[...] * (jnp.sum(a * r - b * w, 0, keepdims=True) * scale(j)))
                im.append(mask[...] * (jnp.sum(a * w + b * r, 0, keepdims=True) * scale(j)))
            put_rows(k, jp, re, im)
        return carry

    def adjoint_block(k, carry):
        for jp in range(3):
            re, im = [], []
            for j in (2 * jp, 2 * jp + 1):
                at = pl.multiple_of(k * 144 + j * 24, 8)
                r, w = wp[k, j, 0], wp[k, j, 1]
                gr = jnp.sum(lin[pl.ds(at, 24), :1024] * mask[...], 0, keepdims=True) * scale(j)
                gi = jnp.sum(lin[pl.ds(at + 432, 24), :1024] * mask[...], 0, keepdims=True) * scale(j)
                gh[k, j, 0:1, :] = gr
                gh[k, j, 1:2, :] = gi
                re.append(gr * r + gi * w)
                im.append(gi * r - gr * w)
            put_rows(k, jp, re, im)
        return carry

    def weight_terms(k, j):
        rows = pl.ds(pl.multiple_of(k * 144 + j * 24, 8), 24)
        a, b = uh[0, rows, :], uh[1, rows, :]
        gr, gi = gh[k, j, 0:1, :], gh[k, j, 1:2, :]
        return a * gr + b * gi, a * gi - b * gr

    def gs_copy():
        return remote(gss, gsr, gs_sem.at[0], gs_sem.at[1], twin)

    def weight_gradient_send():
        def block(k, carry):
            for jj in range(3):
                re, im = weight_terms(k, (1 - me_t) * 3 + jj)
                at = pl.multiple_of(k * 144 + jj * 48, 48)
                gss[pl.ds(at, 48), :] = jnp.concatenate([re, im], 0).astype(BF16)
            return carry

        lax.fori_loop(0, 3, block, 0)
        gs_copy().start()

    def weight_gradient_finish():
        gs_copy().wait_recv()

        def block(k, carry):
            for jj in range(3):
                re, im = weight_terms(k, me_t * 3 + jj)
                at = pl.multiple_of(k * 144 + jj * 48, 48)
                other = gsr[pl.ds(at, 48), :].astype(F32)
                gs_ref[k, jj, :, 0, :] = (re + other[:24])[:C, :C * KEPT]
                gs_ref[k, jj, :, 1, :] = (im + other[24:])[:C, :C * KEPT]
            return carry

        lax.fori_loop(0, 3, block, 0)

    def mixing_terms():
        lane = lax.broadcasted_iota(jnp.int32, (256, 256), 1) & (NZ - 1)
        row = lax.broadcasted_iota(jnp.int32, (256, 256), 0) & (NZ - 1)
        eye = jnp.where(lane == row, 1.0, 0.0).astype(F32)

        def block(cb, carry):
            cols = pl.ds(pl.multiple_of(cb * 256, 256), 256)
            for nb in range(5):
                o = lax.dot_general(
                    u[:, cols], g[:, nb * 256:(nb + 1) * 256], TN, preferred_element_type=F32
                )
                gmx[cb, 0:4, nb * 256:(nb + 1) * 256] = jnp.sum((o * eye).reshape(4, NZ, 256), 1)
            return carry

        gmx[...] = jnp.zeros_like(gmx)
        lax.fori_loop(0, 5, block, 0)
        v = gmx[...].reshape(40, CZ)
        hi = v.astype(BF16)
        low = (v - hi.astype(F32)).astype(BF16)
        sel = lax.broadcasted_iota(jnp.int32, (CZ, 128), 0) >> 6
        sel = jnp.where(sel == lax.broadcasted_iota(jnp.int32, (CZ, 128), 1), 1.0, 0.0).astype(BF16)
        gmy[0] = jnp.dot(hi, sel, preferred_element_type=F32) + jnp.dot(low, sel, preferred_element_type=F32)

    def gy_copy(rel):
        return remote(gmy.at[0], gmy.at[rel], gy_ss.at[rel], gy_rs.at[rel], at_y(rel))

    def gx_copy(d):
        return remote(gma.at[0], gma.at[d], gx_ss.at[d], gx_rs.at[d], at_x(d))

    def ta_copy():
        return remote(gma.at[16], gma.at[17], ta_sem.at[0], ta_sem.at[1], twin)

    for i in range(3):
        loads[i].wait()
    forward_block(u, 0, 2)
    pl.semaphore_wait(barrier, 19)
    rs_copy(0, 0).start()
    loads[4].wait()
    forward_block(u, 1, 2)
    rs_copy(0, 3).start()
    loads[3].wait()
    forward_block(u, 0, 3)
    rs_copy(0, 1).start()
    loads[5].wait()
    forward_block(u, 1, 1)
    rs_copy(0, 4).start()
    forward_block(u, 0, 1)
    loads[6].wait()
    forward_block(u, 0, 0)
    send_third(0, 0)
    rs_copy(0, 0).wait_recv()
    add_part(1, 0, dg[0, 0])
    rs_copy(0, 2).start()
    forward_block(u, 1, 3)
    rs_copy(0, 3).wait_recv()
    add_part(3, 1, dg[0, 1])
    rs_copy(0, 5).start()
    forward_block(u, 1, 0)
    send_third(0, 1)
    loads[7].wait()
    fill_weights()
    build_kron((((1,), (0,)), ((), ())))
    for i in range(8, 16):
        loads[i].wait()

    def sums(t):
        rs_copy(t, 1).wait_recv()
        rs_copy(t, 2).wait_recv()
        sum_and_send(t, 0)
        rs_copy(t, 4).wait_recv()
        rs_copy(t, 5).wait_recv()
        sum_and_send(t, 1)
        over_gx(lambda d: hb_copy(t, 0, d).wait_recv())
        over_gx(lambda d: hb_copy(t, 1, d).wait_recv())
        x_third(t)
        over_gx(lambda d: h_copy(t, 0, d).wait_recv())
        over_gx(lambda d: h_copy(t, 1, d).wait_recv())

    sums(0)

    x_transform(0, put_uh)
    lax.fori_loop(0, 3, mix_block, 0, unroll=True)
    x_inverse_and_send(0)

    def gather(t, src):
        third_inverse_and_send(t)
        gather_block(t, 0)
        ag_copy(t, 0).start()
        ag_copy(t, 1).start()
        gather_block(t, 1)
        ag_copy(t, 3).start()
        linear(src, 0)
        ag_copy(t, 0).wait_recv()
        ag_copy(t, 2).start()
        ag_copy(t, 4).start()
        ag_copy(t, 3).wait_recv()
        ag_copy(t, 5).start()
        linear(src, 1)

    gather(0, u)
    for i in range(6):
        rs_copy(0, i).wait_send()
    for xc in range(2):
        over_gx(lambda d: h_copy(0, xc, d).wait_send())
        over_gx(lambda d: b_copy(0, xc, d).wait_send())
        over_gx(lambda d: hb_copy(0, xc, d).wait_send())
        over_gx(lambda d: bb_copy(0, xc, d).wait_send())
    for rel in (1, 2, 3):
        pb_copy(0, rel).wait_send()

    ag_copy(0, 1).wait_recv()
    ag_copy(0, 2).wait_recv()
    gather_third(0, 0)
    y_inverse(0, 0)
    depth_inverse(0, finish_forward)
    act_out = [
        pltpu.make_async_copy(out.at[pl.ds(xc * HALF, HALF)], act_hbm.at[pl.ds(xc * HALF, HALF)], out_sem.at[0, xc])
        for xc in range(2)
    ]
    act_out[0].start()
    forward_block(g, 0, 2)
    rs_copy(1, 0).start()
    forward_block(g, 0, 3)
    rs_copy(1, 1).start()
    forward_block(g, 0, 1)
    forward_block(g, 0, 0)
    send_third(1, 0)
    ag_copy(0, 4).wait_recv()
    ag_copy(0, 5).wait_recv()
    gather_third(0, 1)
    y_inverse(0, 1)
    depth_inverse(1, finish_forward, 0, 3)
    rs_copy(1, 0).wait_recv()
    add_part(1, 0, dg[1, 0])
    rs_copy(1, 2).start()
    depth_inverse(1, finish_forward, 3, 5)
    act_out[1].start()
    forward_block(g, 1, 2)
    rs_copy(1, 3).start()
    forward_block(g, 1, 1)
    rs_copy(1, 4).start()
    forward_block(g, 1, 3)
    forward_block(g, 1, 0)
    send_third(1, 1)
    rs_copy(1, 3).wait_recv()
    add_part(3, 1, dg[1, 1])
    rs_copy(1, 5).start()
    mixing_terms()
    for rel in (1, 2, 3):
        gy_copy(rel).start()
    for rel in (1, 2, 3):
        gy_copy(rel).wait_recv()
    gma[0] = gmy[0] + gmy[1] + gmy[2] + gmy[3]
    over_gx(lambda d: gx_copy(d).start())
    sums(1)

    x_transform(1, put_lin)
    lax.fori_loop(0, 3, adjoint_block, 0, unroll=True)
    x_inverse_and_send(1)
    weight_gradient_send()
    build_kron(TN)
    gather(1, g)
    over_gx(lambda d: gx_copy(d).wait_recv())
    gma[16] = jnp.sum(gma[0:16], 0)
    ta_copy().start()
    weight_gradient_finish()
    act_out[0].wait()
    act_out[1].wait()
    ag_copy(1, 1).wait_recv()
    ag_copy(1, 2).wait_recv()
    gather_third(1, 0)
    y_inverse(1, 0)
    depth_inverse(0, finish_backward)
    gf_out = [
        pltpu.make_async_copy(out.at[pl.ds(xc * HALF, HALF)], gf_hbm.at[pl.ds(xc * HALF, HALF)], out_sem.at[1, xc])
        for xc in range(2)
    ]
    gf_out[0].start()
    ag_copy(1, 4).wait_recv()
    ag_copy(1, 5).wait_recv()
    gather_third(1, 1)
    y_inverse(1, 1)
    depth_inverse(1, finish_backward)
    gf_out[1].start()
    ta_copy().wait_recv()
    total = (gma[16] + gma[17]) * (1.0 / math.sqrt(2 * NX * NY * NZ))
    for cb in range(5):
        gm_ref[cb * 4:(cb + 1) * 4, :] = total[cb * 8:cb * 8 + 4, :C]

    for t in range(2):
        for i in range(6):
            ag_copy(t, i).wait_send()
    for i in range(6):
        rs_copy(1, i).wait_send()
    for xc in range(2):
        over_gx(lambda d: h_copy(1, xc, d).wait_send())
        over_gx(lambda d: b_copy(1, xc, d).wait_send())
        over_gx(lambda d: hb_copy(1, xc, d).wait_send())
        over_gx(lambda d: bb_copy(1, xc, d).wait_send())
    for rel in (1, 2, 3):
        pb_copy(1, rel).wait_send()
        yb_copy(0, rel).wait_send()
        yb_copy(1, rel).wait_send()
    gs_copy().wait_send()
    for rel in (1, 2, 3):
        gy_copy(rel).wait_send()
    over_gx(lambda d: gx_copy(d).wait_send())
    ta_copy().wait_send()
    gf_out[0].wait()
    gf_out[1].wait()


def hand_over(act_in, gf_in, gs_in, gm_in, act_out, gf_out, gs_out, gm_out, act, gf, gs, gm, in_sem, out_sem):
    pieces = [(gs_in.at[k], gs.at[k], gs_out.at[k]) for k in range(3)] + [(gm_in, gm, gm_out)]
    for i in range(4):
        rows = pl.ds(i * 256, 256)
        pieces.append((act_in.at[rows], act.at[rows], act_out.at[rows]))
        pieces.append((gf_in.at[rows], gf.at[rows], gf_out.at[rows]))
    loads = [pltpu.make_async_copy(p[0], p[1], in_sem.at[i]) for i, p in enumerate(pieces)]
    stores = [pltpu.make_async_copy(p[1], p[2], out_sem.at[i]) for i, p in enumerate(pieces)]
    for load in loads:
        load.start()
    for load, store in zip(loads, stores):
        load.wait()
        store.start()
    for store in stores:
        store.wait()


def shards(features, cotangent, spectral_weight, mixing_weight):
    consts = [jnp.asarray(t) for t in tables()]
    dma = pltpu.SemaphoreType.DMA
    vmem = pltpu.VMEM
    hbm = pl.BlockSpec(memory_space=pl.ANY)
    local = pl.BlockSpec(memory_space=pltpu.VMEM)
    results = (
        jax.ShapeDtypeStruct((ROWS, CZ), BF16),
        jax.ShapeDtypeStruct((ROWS, CZ), BF16),
        jax.ShapeDtypeStruct((3, 3, C, 2, C * KEPT), F32),
        jax.ShapeDtypeStruct((C, C), F32),
    )
    parts = pl.pallas_call(
        kernel,
        out_shape=results,
        in_specs=[hbm, hbm, hbm, local] + [hbm] * 9,
        out_specs=(hbm, hbm, local, local),
        scratch_shapes=[
            vmem((ROWS, CZ), BF16),
            vmem((ROWS, CZ), BF16),
            vmem((ROWS, CZ), BF16),
            vmem((ROWS, CZ), BF16),
            vmem((GY, CZ, 256), BF16),
            vmem((GY * 256, CZ), BF16),
            vmem((CZ, CZ), BF16),
            vmem((ROWS, CZ), F32),
            vmem((512, 128), BF16),
            vmem((144, 128), BF16),
            vmem((128, 144), BF16),
            vmem((2, 128, 1024), BF16),
            vmem((2, 1024, 128), BF16),
            vmem((192, 256), BF16),
            vmem((256, 192), BF16),
            vmem((3, 6, C, 2, C * KEPT), BF16),
            vmem((C, CZ), F32),
            vmem((3, 6, 2, 24, 1024), F32),
            vmem((2, 432, 1024), F32),
            vmem((576, 512), BF16),
            vmem((2, 128, 128), BF16),
            vmem((864, 1024), BF16),
            vmem((432, 1024), BF16),
            vmem((432, 1024), BF16),
            vmem((4, 2, 512, 128), BF16),
            vmem((2, 2, 512, 128), BF16),
            vmem((2, 2, 512, 128), BF16),
            vmem((2, 2, 512, 128), BF16),
            vmem((2, GX, 2, 16, 128), BF16),
            vmem((2, 2, GX, 2, 16, 128), BF16),
            vmem((2, GX, 2, 16, 128), BF16),
            vmem((2, 2, GX, 2, 16, 128), BF16),
            vmem((2, 4, 2, 512, 128), BF16),
            vmem((2, GX, GY, 16, 128), BF16),
            vmem((2, 2, GX, GY, 16, 128), BF16),
            vmem((2, GX, GY, 16, 128), BF16),
            vmem((2, 2, GX, GY, 16, 128), BF16),
            vmem((6, 144, 128), BF16),
            vmem((2, GY, 144, 128), BF16),
            vmem((2, GY, 128, 128), BF16),
            vmem((GY, 256, 128), BF16),
            vmem((HALF, 1024), BF16),
            vmem((512, 128), F32),
            vmem((256, 128), F32),
            vmem((24, 1024), F32),
            vmem((3, 6, 8, 1024), F32),
            vmem((5, 8, CZ), F32),
            vmem((4, 40, 128), F32),
            vmem((18, 40, 128), F32),
            dma((16,)),
            dma((2, 2)),
            dma((2, 6)),
            dma((2, 6)),
            dma((2, 2, GX)),
            dma((2, 2, GX)),
            dma((2, 2, GX)),
            dma((2, 2, GX)),
            dma((2, 6)),
            dma((2, 6)),
            dma((2, 2, GX)),
            dma((2, 2, GX)),
            dma((2, 2, GX)),
            dma((2, 2, GX)),
            dma((2, GY)),
            dma((2, GY)),
            dma((2, GY)),
            dma((2, GY)),
            dma((2,)),
            dma((4,)),
            dma((4,)),
            dma((GX,)),
            dma((GX,)),
            dma((2,)),
        ],
        compiler_params=pltpu.CompilerParams(
            collective_id=0, has_side_effects=True, vmem_limit_bytes=60 * 1024 * 1024
        ),
    )(
        features.reshape(ROWS, CZ), cotangent.reshape(ROWS, CZ),
        spectral_weight.transpose(0, 1, 3, 2, 4), mixing_weight, *consts,
    )
    act, gf, gs, gm = pl.pallas_call(
        hand_over,
        out_shape=results,
        in_specs=[hbm] * 4,
        out_specs=(hbm,) * 4,
        scratch_shapes=[vmem(r.shape, r.dtype) for r in results] + [dma((12,)), dma((12,))],
        compiler_params=pltpu.CompilerParams(vmem_limit_bytes=60 * 1024 * 1024),
    )(*parts)
    return act.reshape(features.shape), gf.reshape(features.shape), gs.transpose(0, 1, 3, 2, 4), gm


def solution(mesh):
    in_specs = (
        P("ta", "gx", "gy", None),
        P("ta", "gx", "gy", None),
        P("gx", "gy", None, None, None),
        P(),
    )
    out_specs = (
        P("ta", "gx", "gy", None),
        P("ta", "gx", "gy", None),
        P("gx", ("gy", "ta"), None, None, None),
        P(),
    )
    return jax.shard_map(shards, mesh=mesh, in_specs=in_specs, out_specs=out_specs, check_vma=False)
```

```python
import math

import jax
import jax.numpy as jnp
import ml_dtypes
import numpy as np
from jax import lax
from jax.experimental import pallas as pl
from jax.experimental.pallas import tpu as pltpu
from jax.sharding import PartitionSpec as P

NX = 256
NY = 256
NZ = 64
C = 20
M = 24
KEPT = 48
CZ = C * NZ
GX = 16
GY = 4
ROWS = 1024
HALF = 512
F32 = jnp.float32
BF16 = jnp.bfloat16
MESH = pl.DeviceIdType.MESH
NT = (((1,), (1,)), ((), ()))
TN = (((0,), (0,)), ((), ()))


def cos_sin(length, count, folded):
    freq = np.arange(count)
    if folded:
        freq = np.where(freq < count // 2, freq, freq + length - count)
    phases = np.arange(length)[:, None] * freq[None, :] % length
    angles = phases.astype(np.float32) * np.float32(2.0 * math.pi / length)
    return np.cos(angles), np.sin(angles)


def complex_table(length, count):
    cosine, sine = cos_sin(length, count, True)
    return np.stack([np.stack([cosine, -sine], 1), np.stack([sine, cosine], 1)], 0)


def tables():
    cosine, sine = cos_sin(NZ, M, False)
    depth = np.stack([cosine, -sine], 1)
    ee = np.zeros((GY, C, NZ, 2, 128), np.float32)
    for h in range(GY):
        for jl in range(6):
            for c in range(C):
                ee[h, c, :, :, jl * C + c] = depth[:, :, h * 6 + jl]
    ee = ee.reshape(GY, CZ, 256)
    eet = np.ascontiguousarray(ee.transpose(0, 2, 1)).reshape(GY * 256, CZ)
    height = complex_table(NY, KEPT).reshape(2, GY, 64, 2, KEPT)
    height = height.transpose(1, 3, 4, 0, 2).reshape(GY, 2, GX, 3, 2, 64)
    a2 = np.zeros((GY, 192, 2, 2, 64), np.float32)
    for x2 in range(2):
        a2[:, x2 * 64:x2 * 64 + 64, x2] = height[:, :, :, :2].reshape(GY, 64, 2, 64)
        a2[:, 128 + x2 * 32:160 + x2 * 32, x2] = height[:, :, :, 2].reshape(GY, 32, 2, 64)
    a2 = a2.reshape(GY, 192, 256)
    at2 = np.ascontiguousarray(a2.transpose(0, 2, 1))
    width = complex_table(NX, KEPT).reshape(2, GX, 2, 8, 2, KEPT)
    fx = np.zeros((2, GX, 2, 8, 2, 64), np.float32)
    fx[..., :KEPT] = width.transpose(2, 1, 0, 3, 4, 5)
    fx = fx.reshape(512, 128)
    spread = np.zeros((2, 128, 1024), np.float32)
    for q in range(2):
        for c in range(C):
            spread[q, q * 64 + np.arange(KEPT), c * KEPT + np.arange(KEPT)] = 1.0
    fold = np.ascontiguousarray(spread.transpose(0, 2, 1))
    pad = np.zeros((6, 24, 128), np.float32)
    for jl in range(6):
        for c in range(C):
            pad[jl, c, jl * C + c] = 1.0
    pad = pad.reshape(144, 128)
    padt = np.ascontiguousarray(pad.T)
    return [t.astype(ml_dtypes.bfloat16) for t in (ee, eet, a2, at2, fx, pad, padt, spread, fold)]


def kernel(
    u_hbm, cot_hbm, w_hbm, mix_ref, ee_hbm, eet_hbm, a2_hbm, at2_hbm, fx_hbm, pad_hbm, padt_hbm, spread_hbm, fold_hbm,
    act_hbm, gf_hbm, gs_ref, gm_ref,
    u, cot, g, out, ee, eet, kron, lin, fx, pad, padt, spread, fold, a2, at2, w, mixrows, wp, uh, ht, yk, lw, gss, gsr,
    part, dg, fl, fr, hs, hr, bs, br, ag, hsb, hrb, bsb, brb, pu, pb, yb, agb, by, s, sb, mask, gh, gmx, gmy, gma,
    in_sem, out_sem, rs_ss, rs_rs, h_ss, h_rs, b_ss, b_rs, ag_ss, ag_rs,
    hb_ss, hb_rs, bb_ss, bb_rs, pb_ss, pb_rs, yb_ss, yb_rs, gs_sem, gy_ss, gy_rs, gx_ss, gx_rs, ta_sem,
):
    me_x = lax.axis_index("gx")
    me_y = lax.axis_index("gy")
    me_t = lax.axis_index("ta")

    def at_y(rel):
        return (me_x, lax.rem(me_y + rel, GY), me_t)

    def at_x(d):
        return (lax.rem(me_x + d, GX), me_y, me_t)

    twin = (me_x, me_y, 1 - me_t)

    opposite, left = lax.rem(me_y + 2, GY), lax.rem(me_y + 3, GY)
    right = lax.rem(me_y + 1, GY)
    first, second = pl.ds(0, HALF), pl.ds(HALF, HALF)
    loads = [
        pltpu.make_async_copy(src, dst, in_sem.at[i])
        for i, (src, dst) in enumerate([
            (u_hbm.at[first], u.at[first]), (ee_hbm.at[opposite], ee.at[opposite]),
            (ee_hbm.at[right], ee.at[right]), (a2_hbm.at[me_y], a2),
            (ee_hbm.at[left], ee.at[left]), (ee_hbm.at[me_y], ee.at[me_y]), (u_hbm.at[second], u.at[second]),
            (w_hbm, w), (fx_hbm, fx), (pad_hbm, pad), (padt_hbm, padt),
            (spread_hbm, spread), (fold_hbm, fold), (at2_hbm.at[me_y], at2), (eet_hbm, eet), (cot_hbm, cot),
        ])
    ]

    def start_loads(*ids):
        for i in ids:
            loads[i].start()

    def wait_loads(*ids):
        for i in ids:
            loads[i].wait()

    start_loads(0, 1, 2, 3)

    barrier = pltpu.get_barrier_semaphore()
    for rel in (1, 2, 3):
        pl.semaphore_signal(barrier, inc=1, device_id=at_y(rel), device_id_type=MESH)

    def greet(d, carry):
        pl.semaphore_signal(barrier, inc=1, device_id=at_x(d), device_id_type=MESH)
        return carry

    lax.fori_loop(1, GX, greet, 0)
    pl.semaphore_signal(barrier, inc=1, device_id=twin, device_id_type=MESH)

    def remote(src, dst, ss, rs, dev):
        return pltpu.make_async_remote_copy(
            src_ref=src, dst_ref=dst, send_sem=ss, recv_sem=rs, device_id=dev, device_id_type=MESH
        )

    upper, lower = pl.ds(0, 256), pl.ds(256, 256)

    def rs_copy(t, c, i):
        src, dst, rel = [
            (part.at[2, c, upper], dg.at[t, c, upper], 1),
            (part.at[2, c, lower], dg.at[t, c, lower], 3),
            (part.at[1, c, lower], fl.at[t, c, lower], 1),
            (part.at[3, c, upper], fr.at[t, c, upper], 3),
            (part.at[1, c, upper], fl.at[t, c, upper], 1),
            (part.at[3, c, lower], fr.at[t, c, lower], 3),
        ][i]
        return remote(src, dst, rs_ss.at[t, c, i], rs_rs.at[t, c, i], at_y(rel))

    def ag_copy(t, c, i):
        src, dst, rel = [
            (ag.at[t, 0, c, upper], ag.at[t, 3, c, upper], 1),
            (ag.at[t, 0, c, lower], ag.at[t, 1, c, lower], 3),
            (ag.at[t, 0, c, lower], ag.at[t, 3, c, lower], 1),
            (ag.at[t, 0, c, upper], ag.at[t, 1, c, upper], 3),
            (ag.at[t, 3, c, upper], ag.at[t, 2, c, upper], 1),
            (ag.at[t, 1, c, lower], ag.at[t, 2, c, lower], 3),
        ][i]
        return remote(src, dst, ag_ss.at[t, c, i], ag_rs.at[t, c, i], at_y(rel))

    def h_copy(t, xc, d):
        to = lax.rem(me_x + d, GX)
        return remote(hs.at[xc, to], hr.at[t, xc, me_x], h_ss.at[t, xc, d], h_rs.at[t, xc, d], at_x(d))

    def b_copy(t, xc, d):
        to = lax.rem(me_x + d, GX)
        return remote(bs.at[xc, to], br.at[t, xc, me_x], b_ss.at[t, xc, d], b_rs.at[t, xc, d], at_x(d))

    def hb_copy(t, xc, d):
        to = lax.rem(me_x + d, GX)
        return remote(hsb.at[xc, to], hrb.at[t, xc, me_x], hb_ss.at[t, xc, d], hb_rs.at[t, xc, d], at_x(d))

    def bb_copy(t, xc, d):
        to = lax.rem(me_x + d, GX)
        return remote(bsb.at[xc, to], brb.at[t, xc, me_x], bb_ss.at[t, xc, d], bb_rs.at[t, xc, d], at_x(d))

    def pb_copy(t, rel):
        return remote(pu.at[2 + rel], pb.at[t, rel], pb_ss.at[t, rel], pb_rs.at[t, rel], at_y(rel))

    def yb_copy(t, rel):
        return remote(yb.at[t, 0], yb.at[t, GY - rel], yb_ss.at[t, rel], yb_rs.at[t, rel], at_y(rel))

    def over_gx(fn):
        def step(d, carry):
            fn(d)
            return carry

        lax.fori_loop(1, GX, step, 0)

    def scale(jl):
        first = (me_y == 0) & (jl == 0)
        return jnp.where(first, 1.0, 2.0).astype(F32) * (1.0 / float(NX * NY * NZ))

    def forward_block(src, xc, *rels):
        tab = [ee[lax.rem(me_y + rel, GY)] for rel in rels]
        tab = tab[0] if len(tab) == 1 else jnp.concatenate(tab, 1)
        both = jnp.dot(src[xc * HALF:(xc + 1) * HALF, :], tab, preferred_element_type=F32).astype(BF16)
        for i, rel in enumerate(rels):
            d = both[:, i * 256:(i + 1) * 256]
            for xp in range(4):
                r = xp * 128
                rhs = jnp.concatenate(
                    [d[r:r + 64, :128], d[r:r + 64, 128:], d[r + 64:r + 128, :128], d[r + 64:r + 128, 128:]], 0
                )
                o = jnp.dot(a2[...], rhs, preferred_element_type=F32)
                part[rel, xc, xp * 128:(xp + 1) * 128, :] = o[:128].astype(BF16)
                sb[i, xp * 64:(xp + 1) * 64, :] = o[128:]
        for i, rel in enumerate(rels):
            for gx in range(GX):
                top = sb[i, pl.ds(gx, 8, stride=32), :]
                low = sb[i, pl.ds(gx + GX, 8, stride=32), :]
                hsb[xc, gx, rel] = jnp.concatenate([top, low], 0).astype(BF16)

    def send_third(t, xc):
        over_gx(lambda d: hb_copy(t, xc, d).start())
        hrb[t, xc, me_x] = hsb[xc, me_x]

    def rs_start(t, c, *ids):
        for i in ids:
            rs_copy(t, c, i).start()

    def rs_forward(t, c):
        rs_copy(t, c, 0).wait_recv()
        part[1, c, :256] = (part[1, c, :256].astype(F32) + dg[t, c, :256].astype(F32)).astype(BF16)
        rs_start(t, c, 4)
        rs_copy(t, c, 1).wait_recv()
        part[3, c, 256:] = (part[3, c, 256:].astype(F32) + dg[t, c, 256:].astype(F32)).astype(BF16)
        rs_start(t, c, 5)

    def ag_start(t, c):
        for i in range(4):
            ag_copy(t, c, i).start()

    def ag_forward(t, c):
        for i in (0, 1):
            ag_copy(t, c, i).wait_recv()
            ag_copy(t, c, 4 + i).start()

    def ag_finish(t, c):
        for i in (2, 3, 4, 5):
            ag_copy(t, c, i).wait_recv()

    def sum_and_send(t, xc):
        s[...] = part[0, xc].astype(F32) + fl[t, xc].astype(F32) + fr[t, xc].astype(F32)

        def block(gx, carry):
            for k in range(2):
                r = gx * 2 + k
                top = s[pl.ds(r, 8, stride=64), :]
                low = s[pl.ds(r + 32, 8, stride=64), :]
                hs[xc, gx, k] = jnp.concatenate([top, low], 0).astype(BF16)
            return carry

        lax.fori_loop(0, GX, block, 0)
        over_gx(lambda d: h_copy(t, xc, d).start())
        hr[t, xc, me_x] = hs[xc, me_x]

    def x_third(t):
        for rel in range(GY):
            hk = hrb[t, :, :, rel].reshape(512, 128)
            ht[rel * 144:(rel + 1) * 144, :] = lax.dot_general(
                pad[...], hk, NT, preferred_element_type=F32
            ).astype(BF16)
        v = jnp.dot(ht[...], fx[...], preferred_element_type=F32).astype(BF16)
        pu[2] = v[:144]
        for rel in (1, 2, 3):
            pu[2 + rel] = v[rel * 144:(rel + 1) * 144]
            pb_copy(t, rel).start()

    def x_transform(t, put):
        for k in range(2):
            hk = hr[t, :, :, k].reshape(512, 128)
            v = lax.dot_general(pad[...], hk, NT, preferred_element_type=F32).astype(BF16)
            pu[k] = jnp.dot(v, fx[...], preferred_element_type=F32).astype(BF16)
        for rel in (1, 2, 3):
            pb_copy(t, rel).wait_recv()
        third = pu[2].astype(F32) + pb[t, 1].astype(F32) + pb[t, 2].astype(F32) + pb[t, 3].astype(F32)
        v = jnp.concatenate([pu[0], pu[1], third.astype(BF16)], 0)
        for q in range(2):
            for n in range(2):
                put(q, n * 512, jnp.dot(v, spread[q, :, n * 512:(n + 1) * 512], preferred_element_type=F32))

    def x_inverse_and_send(t):
        y = jnp.dot(lw[:432, :], fold[0], preferred_element_type=F32)
        y = (y + jnp.dot(lw[432:, :], fold[1], preferred_element_type=F32)).astype(BF16)
        for k in (2, 0, 1):
            v = jnp.dot(padt[...], y[k * 144:(k + 1) * 144], preferred_element_type=F32).astype(BF16)
            if k == 2:
                yb[t, 0] = v
                for rel in (1, 2, 3):
                    yb_copy(t, rel).start()
            else:
                yk[k] = v
        for xc in range(2):
            for k in range(2):
                bx = lax.dot_general(fx[xc * 256:(xc + 1) * 256, :], yk[k], NT, preferred_element_type=F32)
                bs[xc, :, k] = bx.astype(BF16).reshape(GX, 16, 128)
            over_gx(lambda d: b_copy(t, xc, d).start())
            br[t, xc, me_x] = bs[xc, me_x]

    def third_inverse_and_send(t):
        for rel in (1, 2, 3):
            yb_copy(t, rel).wait_recv()
        for xc in range(2):
            for rel in range(GY):
                bx = lax.dot_general(fx[xc * 256:(xc + 1) * 256, :], yb[t, rel], NT, preferred_element_type=F32)
                bsb[xc, :, rel] = bx.astype(BF16).reshape(GX, 16, 128)
            over_gx(lambda d: bb_copy(t, xc, d).start())
            brb[t, xc, me_x] = bsb[xc, me_x]

    def gather_block(t, xc):
        over_gx(lambda d: b_copy(t, xc, d).wait_recv())

        def block(gx, carry):
            for k in range(2):
                r = gx * 2 + k
                v = br[t, xc, gx, k].astype(F32)
                s[pl.ds(r, 8, stride=64), :] = v[:8]
                s[pl.ds(r + 32, 8, stride=64), :] = v[8:]
            return carry

        lax.fori_loop(0, GX, block, 0)
        ag[t, 0, xc] = s[...].astype(BF16)

    def gather_third(t, xc):
        over_gx(lambda d: bb_copy(t, xc, d).wait_recv())
        for rel in range(GY):
            for gx in range(GX):
                v = brb[t, xc, gx, rel].astype(F32)
                sb[rel, pl.ds(gx, 8, stride=32), :] = v[:8]
                sb[rel, pl.ds(gx + GX, 8, stride=32), :] = v[8:]
            agb[rel] = sb[rel].astype(BF16)

    def y_inverse(t, xc):
        for rel in range(GY):
            h = lax.rem(me_y + rel, GY)
            off = pl.multiple_of(h * 256, 256)
            for xp in range(4):
                rhs = jnp.concatenate(
                    [ag[t, rel, xc, xp * 128:(xp + 1) * 128, :], agb[rel, xp * 64:(xp + 1) * 64, :]], 0
                )
                v = jnp.dot(at2[...], rhs, preferred_element_type=F32).astype(BF16)
                for x2 in range(2):
                    rows = slice(xp * 128 + x2 * 64, xp * 128 + x2 * 64 + 64)
                    by[rows, pl.ds(off, 128)] = v[x2 * 128:x2 * 128 + 64]
                    by[rows, pl.ds(off + 128, 128)] = v[x2 * 128 + 64:x2 * 128 + 128]

    def depth_inverse(xc, finish, start=0, stop=5):
        def block(n, carry):
            cols = pl.ds(pl.multiple_of(n * 256, 256), 256)
            for rb in range(2):
                rows = slice(xc * HALF + rb * 256, xc * HALF + rb * 256 + 256)
                v = jnp.dot(by[rb * 256:rb * 256 + 256, :], eet[:, cols], preferred_element_type=F32)
                finish(rows, cols, v + lin[rows, cols])
            return carry

        lax.fori_loop(start, stop, block, 0, unroll=True)

    def finish_forward(rows, cols, x):
        k0 = math.sqrt(2.0 / math.pi)
        x2 = x * x
        th = jnp.tanh(k0 * x * (1.0 + 0.044715 * x2))
        half = 0.5 * (1.0 + th)
        out[rows, cols] = (x * half).astype(BF16)
        slope = half + 0.5 * x * (1.0 - th * th) * (k0 * (1.0 + 3.0 * 0.044715 * x2))
        g[rows, cols] = (cot[rows, cols].astype(F32) * slope).astype(BF16)

    def finish_backward(rows, cols, x):
        out[rows, cols] = x.astype(BF16)

    def build_kron(dims):
        at = lax.broadcasted_iota(jnp.int32, (C, CZ), 1) >> 6
        one = jnp.where(at == lax.broadcasted_iota(jnp.int32, (C, CZ), 0), 1.0, 0.0).astype(BF16)
        mixrows[...] = lax.dot_general(mix_ref[...], one, dims, preferred_element_type=F32)

        lane = lax.broadcasted_iota(jnp.int32, (NZ, CZ), 1) & (NZ - 1)
        row = lax.broadcasted_iota(jnp.int32, (NZ, CZ), 0)
        eye = jnp.where(lane == row, 1.0, 0.0).astype(F32)

        def block(c, carry):
            kron[pl.ds(pl.multiple_of(c * NZ, NZ), NZ), :] = (eye * mixrows[pl.ds(c, 1), :]).astype(BF16)
            return carry

        lax.fori_loop(0, C, block, 0)

    def linear(src, rb):
        def block(n, carry):
            cols = pl.ds(pl.multiple_of(n * 256, 256), 256)
            rows = slice(rb * 512, rb * 512 + 512)
            lin[rows, cols] = jnp.dot(src[rows, :], kron[:, cols], preferred_element_type=F32)
            return carry

        lax.fori_loop(0, 5, block, 0, unroll=True)

    def fill_weights():
        wp[...] = jnp.zeros_like(wp)
        for k in range(3):
            def block(j, carry):
                v = w[k, j].astype(F32)
                for p in range(2):
                    wp[k, j, p, :C, :C * KEPT] = v[:, p, :]
                return carry

            lax.fori_loop(0, 6, block, 0)
        lane = lax.broadcasted_iota(jnp.int32, (24, 1024), 1)
        first = lax.broadcasted_iota(jnp.int32, (24, 1024), 0) * KEPT
        mask[...] = jnp.where((lane >= first) & (lane < first + KEPT) & (lane < C * KEPT), 1.0, 0.0).astype(F32)

    def put_uh(q, at, v):
        uh[q, :, at:at + 512] = v

    def put_lin(q, at, v):
        lin[q * 432:(q + 1) * 432, at:at + 512] = v

    def put_rows(k, jp, re, im):
        at = pl.multiple_of(k * 144 + jp * 48, 48)
        lw[pl.ds(at, 48), :] = jnp.concatenate(re, 0).astype(BF16)
        lw[pl.ds(at + 432, 48), :] = jnp.concatenate(im, 0).astype(BF16)

    def mix_block(k, carry):
        for jp in range(3):
            re, im = [], []
            for j in (2 * jp, 2 * jp + 1):
                rows = pl.ds(pl.multiple_of(k * 144 + j * 24, 8), 24)
                a, b = uh[0, rows, :], uh[1, rows, :]
                r, w = wp[k, j, 0], wp[k, j, 1]
                re.append(mask[...] * (jnp.sum(a * r - b * w, 0, keepdims=True) * scale(j)))
                im.append(mask[...] * (jnp.sum(a * w + b * r, 0, keepdims=True) * scale(j)))
            put_rows(k, jp, re, im)
        return carry

    def adjoint_block(k, carry):
        for jp in range(3):
            re, im = [], []
            for j in (2 * jp, 2 * jp + 1):
                at = pl.multiple_of(k * 144 + j * 24, 8)
                r, w = wp[k, j, 0], wp[k, j, 1]
                gr = jnp.sum(lin[pl.ds(at, 24), :1024] * mask[...], 0, keepdims=True) * scale(j)
                gi = jnp.sum(lin[pl.ds(at + 432, 24), :1024] * mask[...], 0, keepdims=True) * scale(j)
                gh[k, j, 0:1, :] = gr
                gh[k, j, 1:2, :] = gi
                re.append(gr * r + gi * w)
                im.append(gi * r - gr * w)
            put_rows(k, jp, re, im)
        return carry

    def weight_terms(k, j):
        rows = pl.ds(pl.multiple_of(k * 144 + j * 24, 8), 24)
        a, b = uh[0, rows, :], uh[1, rows, :]
        gr, gi = gh[k, j, 0:1, :], gh[k, j, 1:2, :]
        return a * gr + b * gi, a * gi - b * gr

    def gs_copy():
        return remote(gss, gsr, gs_sem.at[0], gs_sem.at[1], twin)

    def weight_gradient_send():
        def block(k, carry):
            for jj in range(3):
                re, im = weight_terms(k, (1 - me_t) * 3 + jj)
                at = pl.multiple_of(k * 144 + jj * 48, 48)
                gss[pl.ds(at, 48), :] = jnp.concatenate([re, im], 0).astype(BF16)
            return carry

        lax.fori_loop(0, 3, block, 0)
        gs_copy().start()

    def weight_gradient_finish():
        gs_copy().wait_recv()

        def block(k, carry):
            for jj in range(3):
                re, im = weight_terms(k, me_t * 3 + jj)
                at = pl.multiple_of(k * 144 + jj * 48, 48)
                other = gsr[pl.ds(at, 48), :].astype(F32)
                gs_ref[k, jj, :, 0, :] = (re + other[:24])[:C, :C * KEPT]
                gs_ref[k, jj, :, 1, :] = (im + other[24:])[:C, :C * KEPT]
            return carry

        lax.fori_loop(0, 3, block, 0)

    def mixing_terms():
        lane = lax.broadcasted_iota(jnp.int32, (256, 256), 1) & (NZ - 1)
        row = lax.broadcasted_iota(jnp.int32, (256, 256), 0) & (NZ - 1)
        eye = jnp.where(lane == row, 1.0, 0.0).astype(F32)

        def block(cb, carry):
            cols = pl.ds(pl.multiple_of(cb * 256, 256), 256)
            for nb in range(5):
                o = lax.dot_general(
                    u[:, cols], g[:, nb * 256:(nb + 1) * 256], TN, preferred_element_type=F32
                )
                gmx[cb, 0:4, nb * 256:(nb + 1) * 256] = jnp.sum((o * eye).reshape(4, NZ, 256), 1)
            return carry

        gmx[...] = jnp.zeros_like(gmx)
        lax.fori_loop(0, 5, block, 0)
        v = gmx[...].reshape(40, CZ)
        hi = v.astype(BF16)
        low = (v - hi.astype(F32)).astype(BF16)
        sel = lax.broadcasted_iota(jnp.int32, (CZ, 128), 0) >> 6
        sel = jnp.where(sel == lax.broadcasted_iota(jnp.int32, (CZ, 128), 1), 1.0, 0.0).astype(BF16)
        gmy[0] = jnp.dot(hi, sel, preferred_element_type=F32) + jnp.dot(low, sel, preferred_element_type=F32)

    def gy_copy(rel):
        return remote(gmy.at[0], gmy.at[rel], gy_ss.at[rel], gy_rs.at[rel], at_y(rel))

    def gx_copy(d):
        return remote(gma.at[0], gma.at[d], gx_ss.at[d], gx_rs.at[d], at_x(d))

    def ta_copy():
        return remote(gma.at[16], gma.at[17], ta_sem.at[0], ta_sem.at[1], twin)

    wait_loads(0, 1, 2, 3)
    start_loads(4, 5, 6)
    forward_block(u, 0, 2, 1)
    pl.semaphore_wait(barrier, 19)
    rs_start(0, 0, 0, 1, 2)
    wait_loads(4, 5)
    forward_block(u, 0, 3, 0)
    rs_start(0, 0, 3)
    send_third(0, 0)
    wait_loads(6)
    start_loads(*range(7, 16))
    forward_block(u, 1, 2, 1)
    rs_start(0, 1, 0, 1)
    forward_block(u, 1, 3, 0)
    send_third(0, 1)
    rs_forward(0, 0)
    rs_start(0, 1, 2, 3)
    wait_loads(7)
    fill_weights()
    rs_forward(0, 1)
    build_kron((((1,), (0,)), ((), ())))
    wait_loads(*range(8, 16))

    def sums(t, meanwhile):
        for c in range(2):
            for i in (2, 3, 4, 5):
                rs_copy(t, c, i).wait_recv()
            sum_and_send(t, c)
        meanwhile()
        over_gx(lambda d: hb_copy(t, 0, d).wait_recv())
        over_gx(lambda d: hb_copy(t, 1, d).wait_recv())
        x_third(t)
        over_gx(lambda d: h_copy(t, 0, d).wait_recv())
        over_gx(lambda d: h_copy(t, 1, d).wait_recv())

    sums(0, lambda: None)

    x_transform(0, put_uh)
    lax.fori_loop(0, 3, mix_block, 0, unroll=True)
    x_inverse_and_send(0)

    def gather(t, src):
        third_inverse_and_send(t)
        gather_block(t, 0)
        ag_start(t, 0)
        gather_block(t, 1)
        linear(src, 0)
        ag_forward(t, 0)
        ag_start(t, 1)
        linear(src, 1)
        ag_forward(t, 1)

    gather(0, u)
    for i in range(6):
        rs_copy(0, 0, i).wait_send()
        rs_copy(0, 1, i).wait_send()
    for xc in range(2):
        over_gx(lambda d: h_copy(0, xc, d).wait_send())
        over_gx(lambda d: b_copy(0, xc, d).wait_send())
        over_gx(lambda d: hb_copy(0, xc, d).wait_send())
        over_gx(lambda d: bb_copy(0, xc, d).wait_send())
    for rel in (1, 2, 3):
        pb_copy(0, rel).wait_send()

    ag_finish(0, 0)
    gather_third(0, 0)
    y_inverse(0, 0)
    depth_inverse(0, finish_forward)
    act_out = [
        pltpu.make_async_copy(out.at[pl.ds(xc * HALF, HALF)], act_hbm.at[pl.ds(xc * HALF, HALF)], out_sem.at[0, xc])
        for xc in range(2)
    ]
    act_out[0].start()
    forward_block(g, 0, 2, 1)
    rs_start(1, 0, 0, 1, 2)
    forward_block(g, 0, 3, 0)
    rs_start(1, 0, 3)
    send_third(1, 0)
    ag_finish(0, 1)
    gather_third(0, 1)
    y_inverse(0, 1)
    depth_inverse(1, finish_forward, 0, 3)
    rs_forward(1, 0)
    depth_inverse(1, finish_forward, 3, 5)
    act_out[1].start()
    forward_block(g, 1, 2, 1)
    rs_start(1, 1, 0, 1, 2)
    forward_block(g, 1, 3, 0)
    rs_start(1, 1, 3)
    send_third(1, 1)
    rs_forward(1, 1)

    def mixing_send():
        mixing_terms()
        for rel in (1, 2, 3):
            gy_copy(rel).start()

    sums(1, mixing_send)

    x_transform(1, put_lin)
    lax.fori_loop(0, 3, adjoint_block, 0, unroll=True)
    x_inverse_and_send(1)
    weight_gradient_send()
    for rel in (1, 2, 3):
        gy_copy(rel).wait_recv()
    gma[0] = gmy[0] + gmy[1] + gmy[2] + gmy[3]
    over_gx(lambda d: gx_copy(d).start())
    build_kron(TN)
    gather(1, g)
    over_gx(lambda d: gx_copy(d).wait_recv())
    gma[16] = jnp.sum(gma[0:16], 0)
    ta_copy().start()
    weight_gradient_finish()
    act_out[0].wait()
    act_out[1].wait()
    ag_finish(1, 0)
    gather_third(1, 0)
    y_inverse(1, 0)
    depth_inverse(0, finish_backward)
    gf_out = [
        pltpu.make_async_copy(out.at[pl.ds(xc * HALF, HALF)], gf_hbm.at[pl.ds(xc * HALF, HALF)], out_sem.at[1, xc])
        for xc in range(2)
    ]
    gf_out[0].start()
    ag_finish(1, 1)
    gather_third(1, 1)
    y_inverse(1, 1)
    depth_inverse(1, finish_backward)
    gf_out[1].start()
    ta_copy().wait_recv()
    total = (gma[16] + gma[17]) * (1.0 / math.sqrt(2 * NX * NY * NZ))
    for cb in range(5):
        gm_ref[cb * 4:(cb + 1) * 4, :] = total[cb * 8:cb * 8 + 4, :C]

    for i in range(6):
        for c in range(2):
            ag_copy(0, c, i).wait_send()
            ag_copy(1, c, i).wait_send()
            rs_copy(1, c, i).wait_send()
    for xc in range(2):
        over_gx(lambda d: h_copy(1, xc, d).wait_send())
        over_gx(lambda d: b_copy(1, xc, d).wait_send())
        over_gx(lambda d: hb_copy(1, xc, d).wait_send())
        over_gx(lambda d: bb_copy(1, xc, d).wait_send())
    for rel in (1, 2, 3):
        pb_copy(1, rel).wait_send()
        yb_copy(0, rel).wait_send()
        yb_copy(1, rel).wait_send()
    gs_copy().wait_send()
    for rel in (1, 2, 3):
        gy_copy(rel).wait_send()
    over_gx(lambda d: gx_copy(d).wait_send())
    ta_copy().wait_send()
    gf_out[0].wait()
    gf_out[1].wait()


def hand_over(act_in, gf_in, gs_in, gm_in, act_out, gf_out, gs_out, gm_out, act, gf, gs, gm, in_sem, out_sem):
    pieces = [(gs_in.at[k], gs.at[k], gs_out.at[k]) for k in range(3)] + [(gm_in, gm, gm_out)]
    for i in range(4):
        rows = pl.ds(i * 256, 256)
        pieces.append((act_in.at[rows], act.at[rows], act_out.at[rows]))
        pieces.append((gf_in.at[rows], gf.at[rows], gf_out.at[rows]))
    loads = [pltpu.make_async_copy(p[0], p[1], in_sem.at[i]) for i, p in enumerate(pieces)]
    stores = [pltpu.make_async_copy(p[1], p[2], out_sem.at[i]) for i, p in enumerate(pieces)]
    for load in loads:
        load.start()
    for load, store in zip(loads, stores):
        load.wait()
        store.start()
    for store in stores:
        store.wait()


def shards(features, cotangent, spectral_weight, mixing_weight):
    consts = [jnp.asarray(t) for t in tables()]
    dma = pltpu.SemaphoreType.DMA
    vmem = pltpu.VMEM
    hbm = pl.BlockSpec(memory_space=pl.ANY)
    local = pl.BlockSpec(memory_space=pltpu.VMEM)
    results = (
        jax.ShapeDtypeStruct((ROWS, CZ), BF16),
        jax.ShapeDtypeStruct((ROWS, CZ), BF16),
        jax.ShapeDtypeStruct((3, 3, C, 2, C * KEPT), F32),
        jax.ShapeDtypeStruct((C, C), F32),
    )
    parts = pl.pallas_call(
        kernel,
        out_shape=results,
        in_specs=[hbm, hbm, hbm, local] + [hbm] * 9,
        out_specs=(hbm, hbm, local, local),
        scratch_shapes=[
            vmem((ROWS, CZ), BF16),
            vmem((ROWS, CZ), BF16),
            vmem((ROWS, CZ), BF16),
            vmem((ROWS, CZ), BF16),
            vmem((GY, CZ, 256), BF16),
            vmem((GY * 256, CZ), BF16),
            vmem((CZ, CZ), BF16),
            vmem((ROWS, CZ), F32),
            vmem((512, 128), BF16),
            vmem((144, 128), BF16),
            vmem((128, 144), BF16),
            vmem((2, 128, 1024), BF16),
            vmem((2, 1024, 128), BF16),
            vmem((192, 256), BF16),
            vmem((256, 192), BF16),
            vmem((3, 6, C, 2, C * KEPT), BF16),
            vmem((C, CZ), F32),
            vmem((3, 6, 2, 24, 1024), F32),
            vmem((2, 432, 1024), F32),
            vmem((576, 512), BF16),
            vmem((2, 128, 128), BF16),
            vmem((864, 1024), BF16),
            vmem((432, 1024), BF16),
            vmem((432, 1024), BF16),
            vmem((4, 2, 512, 128), BF16),
            vmem((2, 2, 512, 128), BF16),
            vmem((2, 2, 512, 128), BF16),
            vmem((2, 2, 512, 128), BF16),
            vmem((2, GX, 2, 16, 128), BF16),
            vmem((2, 2, GX, 2, 16, 128), BF16),
            vmem((2, GX, 2, 16, 128), BF16),
            vmem((2, 2, GX, 2, 16, 128), BF16),
            vmem((2, 4, 2, 512, 128), BF16),
            vmem((2, GX, GY, 16, 128), BF16),
            vmem((2, 2, GX, GY, 16, 128), BF16),
            vmem((2, GX, GY, 16, 128), BF16),
            vmem((2, 2, GX, GY, 16, 128), BF16),
            vmem((6, 144, 128), BF16),
            vmem((2, GY, 144, 128), BF16),
            vmem((2, GY, 128, 128), BF16),
            vmem((GY, 256, 128), BF16),
            vmem((HALF, 1024), BF16),
            vmem((512, 128), F32),
            vmem((GY, 256, 128), F32),
            vmem((24, 1024), F32),
            vmem((3, 6, 8, 1024), F32),
            vmem((5, 8, CZ), F32),
            vmem((4, 40, 128), F32),
            vmem((18, 40, 128), F32),
            dma((16,)),
            dma((2, 2)),
            dma((2, 2, 6)),
            dma((2, 2, 6)),
            dma((2, 2, GX)),
            dma((2, 2, GX)),
            dma((2, 2, GX)),
            dma((2, 2, GX)),
            dma((2, 2, 6)),
            dma((2, 2, 6)),
            dma((2, 2, GX)),
            dma((2, 2, GX)),
            dma((2, 2, GX)),
            dma((2, 2, GX)),
            dma((2, GY)),
            dma((2, GY)),
            dma((2, GY)),
            dma((2, GY)),
            dma((2,)),
            dma((4,)),
            dma((4,)),
            dma((GX,)),
            dma((GX,)),
            dma((2,)),
        ],
        compiler_params=pltpu.CompilerParams(
            collective_id=0, has_side_effects=True, vmem_limit_bytes=60 * 1024 * 1024
        ),
    )(
        features.reshape(ROWS, CZ), cotangent.reshape(ROWS, CZ),
        spectral_weight.transpose(0, 1, 3, 2, 4), mixing_weight, *consts,
    )
    act, gf, gs, gm = pl.pallas_call(
        hand_over,
        out_shape=results,
        in_specs=[hbm] * 4,
        out_specs=(hbm,) * 4,
        scratch_shapes=[vmem(r.shape, r.dtype) for r in results] + [dma((12,)), dma((12,))],
        compiler_params=pltpu.CompilerParams(vmem_limit_bytes=60 * 1024 * 1024),
    )(*parts)
    return act.reshape(features.shape), gf.reshape(features.shape), gs.transpose(0, 1, 3, 2, 4), gm


def solution(mesh):
    in_specs = (
        P("ta", "gx", "gy", None),
        P("ta", "gx", "gy", None),
        P("gx", "gy", None, None, None),
        P(),
    )
    out_specs = (
        P("ta", "gx", "gy", None),
        P("ta", "gx", "gy", None),
        P("gx", ("gy", "ta"), None, None, None),
        P(),
    )
    return jax.shard_map(shards, mesh=mesh, in_specs=in_specs, out_specs=out_specs, check_vma=False)
```

```python
import math

import jax
import jax.numpy as jnp
import ml_dtypes
import numpy as np
from jax import lax
from jax.experimental import pallas as pl
from jax.experimental.pallas import tpu as pltpu
from jax.sharding import PartitionSpec as P

NX = 256
NY = 256
NZ = 64
C = 20
M = 24
KEPT = 48
CZ = C * NZ
GX = 16
GY = 4
ROWS = 1024
HALF = 512
F32 = jnp.float32
BF16 = jnp.bfloat16
MESH = pl.DeviceIdType.MESH
NT = (((1,), (1,)), ((), ()))
TN = (((0,), (0,)), ((), ()))


def cos_sin(length, count, folded):
    freq = np.arange(count)
    if folded:
        freq = np.where(freq < count // 2, freq, freq + length - count)
    phases = np.arange(length)[:, None] * freq[None, :] % length
    angles = phases.astype(np.float32) * np.float32(2.0 * math.pi / length)
    return np.cos(angles), np.sin(angles)


def complex_table(length, count):
    cosine, sine = cos_sin(length, count, True)
    return np.stack([np.stack([cosine, -sine], 1), np.stack([sine, cosine], 1)], 0)


def tables():
    cosine, sine = cos_sin(NZ, M, False)
    depth = np.stack([cosine, -sine], 1)
    ee = np.zeros((GY, C, NZ, 2, 128), np.float32)
    for h in range(GY):
        for jl in range(6):
            for c in range(C):
                ee[h, c, :, :, jl * C + c] = depth[:, :, h * 6 + jl]
    ee = ee.reshape(GY, CZ, 256)
    eet = np.ascontiguousarray(ee.transpose(0, 2, 1)).reshape(GY * 256, CZ)
    height = complex_table(NY, KEPT).reshape(2, GY, 64, 2, KEPT)
    height = height.transpose(1, 3, 4, 0, 2).reshape(GY, 2, GX, 3, 2, 64)
    a2 = np.zeros((GY, 192, 2, 2, 64), np.float32)
    for x2 in range(2):
        a2[:, x2 * 64:x2 * 64 + 64, x2] = height[:, :, :, :2].reshape(GY, 64, 2, 64)
        a2[:, 128 + x2 * 32:160 + x2 * 32, x2] = height[:, :, :, 2].reshape(GY, 32, 2, 64)
    a2 = a2.reshape(GY, 192, 256)
    at2 = np.ascontiguousarray(a2.transpose(0, 2, 1))
    width = complex_table(NX, KEPT).reshape(2, GX, 2, 8, 2, KEPT)
    fx = np.zeros((2, GX, 2, 8, 2, 64), np.float32)
    fx[..., :KEPT] = width.transpose(2, 1, 0, 3, 4, 5)
    fx = fx.reshape(512, 128)
    spread = np.zeros((2, 128, 1024), np.float32)
    for q in range(2):
        for c in range(C):
            spread[q, q * 64 + np.arange(KEPT), c * KEPT + np.arange(KEPT)] = 1.0
    fold = np.ascontiguousarray(spread.transpose(0, 2, 1))
    pad = np.zeros((6, 24, 128), np.float32)
    for jl in range(6):
        for c in range(C):
            pad[jl, c, jl * C + c] = 1.0
    pad = pad.reshape(144, 128)
    padt = np.ascontiguousarray(pad.T)
    return [t.astype(ml_dtypes.bfloat16) for t in (ee, eet, a2, at2, fx, pad, padt, spread, fold)]


def kernel(
    u_hbm, cot_hbm, w_hbm, mix_ref, ee_hbm, eet_hbm, a2_hbm, at2_hbm, fx_hbm, pad_hbm, padt_hbm, spread_hbm, fold_hbm,
    act_hbm, gf_hbm, gs_ref, gm_ref,
    u, cot, g, out, ee, eet, kron, lin, fx, pad, padt, spread, fold, a2, at2, w, mixrows, wp, uh, ht, yk, lw, gss, gsr,
    part, dg, fl, fr, hs, hr, bs, br, ag, hsb, hrb, bsb, brb, pu, pb, yb, agb, by, s, sb, mask, gh, gmx, gmy, gma,
    in_sem, out_sem, rs_ss, rs_rs, ag_ss, ag_rs, ex_ss, ex_rs, third_ss, third_rs, gs_sem, gm_ss, gm_rs, ta_sem,
):
    me_x = lax.axis_index("gx")
    me_y = lax.axis_index("gy")
    me_t = lax.axis_index("ta")

    def at_y(rel):
        return (me_x, lax.rem(me_y + rel, GY), me_t)

    def at_x(d):
        return (lax.rem(me_x + d, GX), me_y, me_t)

    twin = (me_x, me_y, 1 - me_t)

    opposite, left = lax.rem(me_y + 2, GY), lax.rem(me_y + 3, GY)
    right = lax.rem(me_y + 1, GY)
    first, second = pl.ds(0, HALF), pl.ds(HALF, HALF)
    loads = [
        pltpu.make_async_copy(src, dst, in_sem.at[i])
        for i, (src, dst) in enumerate([
            (u_hbm.at[first], u.at[first]), (ee_hbm.at[opposite], ee.at[opposite]),
            (ee_hbm.at[right], ee.at[right]), (a2_hbm.at[me_y], a2),
            (ee_hbm.at[left], ee.at[left]), (ee_hbm.at[me_y], ee.at[me_y]), (u_hbm.at[second], u.at[second]),
            (w_hbm, w), (fx_hbm, fx), (pad_hbm, pad), (padt_hbm, padt),
            (spread_hbm, spread), (fold_hbm, fold), (at2_hbm.at[me_y], at2), (eet_hbm, eet), (cot_hbm, cot),
        ])
    ]

    def start_loads(*ids):
        for i in ids:
            loads[i].start()

    def wait_loads(*ids):
        for i in ids:
            loads[i].wait()

    start_loads(0, 1, 2, 3)

    barrier = pltpu.get_barrier_semaphore()
    for rel in (1, 2, 3):
        pl.semaphore_signal(barrier, inc=1, device_id=at_y(rel), device_id_type=MESH)

    def greet(d, carry):
        pl.semaphore_signal(barrier, inc=1, device_id=at_x(d), device_id_type=MESH)
        return carry

    lax.fori_loop(1, GX, greet, 0)
    pl.semaphore_signal(barrier, inc=1, device_id=twin, device_id_type=MESH)

    def remote(src, dst, ss, rs, dev):
        return pltpu.make_async_remote_copy(
            src_ref=src, dst_ref=dst, send_sem=ss, recv_sem=rs, device_id=dev, device_id_type=MESH
        )

    upper, lower = pl.ds(0, 256), pl.ds(256, 256)

    def rs_copy(t, c, i):
        src, dst, rel = [
            (part.at[2, c, upper], dg.at[t, c, upper], 1),
            (part.at[2, c, lower], dg.at[t, c, lower], 3),
            (part.at[1, c, lower], fl.at[t, c, lower], 1),
            (part.at[3, c, upper], fr.at[t, c, upper], 3),
            (part.at[1, c, upper], fl.at[t, c, upper], 1),
            (part.at[3, c, lower], fr.at[t, c, lower], 3),
        ][i]
        return remote(src, dst, rs_ss.at[t], rs_rs.at[t, c, min(i, 2)], at_y(rel))

    def ag_copy(t, c, i):
        src, dst, rel = [
            (ag.at[t, 0, c, upper], ag.at[t, 3, c, upper], 1),
            (ag.at[t, 0, c, lower], ag.at[t, 1, c, lower], 3),
            (ag.at[t, 0, c, lower], ag.at[t, 3, c, lower], 1),
            (ag.at[t, 0, c, upper], ag.at[t, 1, c, upper], 3),
            (ag.at[t, 3, c, upper], ag.at[t, 2, c, upper], 1),
            (ag.at[t, 1, c, lower], ag.at[t, 2, c, lower], 3),
        ][i]
        return remote(src, dst, ag_ss.at[t], ag_rs.at[t, c, min(i, 2)], at_y(rel))

    def rs_rest(t, c):
        remote(part.at[0], fl.at[t], rs_ss.at[t], rs_rs.at[t, c, 2], at_y(1)).wait_recv()

    def rs_sent(t):
        remote(part.at[pl.ds(0, 3)], part.at[pl.ds(0, 3)], rs_ss.at[t], rs_rs.at[t, 0, 2], at_y(1)).wait_send()

    def ag_sent(t):
        blocks = ag.at[t, pl.ds(0, 3)]
        remote(blocks, blocks, ag_ss.at[t], ag_rs.at[t, 0, 2], at_y(1)).wait_send()

    H, B, HB, BB = range(4)
    pairs = ((hs, hr), (bs, br), (hsb, hrb), (bsb, brb))
    others = pl.ds(0, GX - 1)

    def exchange(kind, t, xc):
        src, dst = pairs[kind]

        def step(d, carry):
            to = lax.rem(me_x + d, GX)
            remote(
                src.at[xc, to], dst.at[t, xc, me_x], ex_ss.at[kind, t], ex_rs.at[kind, t, xc], at_x(d)
            ).start()
            return carry

        lax.fori_loop(1, GX, step, 0)
        dst[t, xc, me_x] = src[xc, me_x]

    def arrived(kind, t, xc):
        src, dst = pairs[kind]
        remote(
            src.at[xc, others], dst.at[t, xc, others], ex_ss.at[kind, t], ex_rs.at[kind, t, xc], at_x(1)
        ).wait_recv()

    def departed(kind, t):
        src, dst = pairs[kind]
        remote(
            src.at[:, others], dst.at[t, :, others], ex_ss.at[kind, t], ex_rs.at[kind, t, 0], at_x(1)
        ).wait_send()

    def pb_copy(t, rel):
        return remote(pu.at[2 + rel], pb.at[t, rel], third_ss.at[t, 0], third_rs.at[t, 0], at_y(rel))

    def yb_copy(t, rel):
        return remote(yb.at[t, 0], yb.at[t, GY - rel], third_ss.at[t, 1], third_rs.at[t, 1], at_y(rel))

    def pb_all(t):
        return remote(pu.at[pl.ds(0, 3)], pb.at[t, pl.ds(0, 3)], third_ss.at[t, 0], third_rs.at[t, 0], at_y(1))

    def yb_all(t):
        blocks = yb.at[t, pl.ds(0, 3)]
        return remote(blocks, blocks, third_ss.at[t, 1], third_rs.at[t, 1], at_y(1))

    def over_gx(fn):
        def step(d, carry):
            fn(d)
            return carry

        lax.fori_loop(1, GX, step, 0)

    def scale(jl):
        first = (me_y == 0) & (jl == 0)
        return jnp.where(first, 1.0, 2.0).astype(F32) * (1.0 / float(NX * NY * NZ))

    def forward_block(src, xc, *rels):
        tab = [ee[lax.rem(me_y + rel, GY)] for rel in rels]
        tab = tab[0] if len(tab) == 1 else jnp.concatenate(tab, 1)
        both = jnp.dot(src[xc * HALF:(xc + 1) * HALF, :], tab, preferred_element_type=F32).astype(BF16)
        for i, rel in enumerate(rels):
            d = both[:, i * 256:(i + 1) * 256]
            for xp in range(4):
                r = xp * 128
                rhs = jnp.concatenate(
                    [d[r:r + 64, :128], d[r:r + 64, 128:], d[r + 64:r + 128, :128], d[r + 64:r + 128, 128:]], 0
                )
                o = jnp.dot(a2[...], rhs, preferred_element_type=F32)
                part[rel, xc, xp * 128:(xp + 1) * 128, :] = o[:128].astype(BF16)
                sb[i, xp * 64:(xp + 1) * 64, :] = o[128:]
        for i, rel in enumerate(rels):
            for gx in range(GX):
                top = sb[i, pl.ds(gx, 8, stride=32), :]
                low = sb[i, pl.ds(gx + GX, 8, stride=32), :]
                hsb[xc, gx, rel] = jnp.concatenate([top, low], 0).astype(BF16)

    def send_third(t, xc):
        exchange(HB, t, xc)

    def rs_start(t, c, *ids):
        for i in ids:
            rs_copy(t, c, i).start()

    def rs_forward(t, c):
        rs_copy(t, c, 0).wait_recv()
        part[1, c, :256] = (part[1, c, :256].astype(F32) + dg[t, c, :256].astype(F32)).astype(BF16)
        rs_start(t, c, 4)
        rs_copy(t, c, 1).wait_recv()
        part[3, c, 256:] = (part[3, c, 256:].astype(F32) + dg[t, c, 256:].astype(F32)).astype(BF16)
        rs_start(t, c, 5)

    def ag_start(t, c):
        for i in range(4):
            ag_copy(t, c, i).start()

    def ag_forward(t, c):
        for i in (0, 1):
            ag_copy(t, c, i).wait_recv()
            ag_copy(t, c, 4 + i).start()

    def ag_finish(t, c):
        remote(ag.at[t, 0], ag.at[t, 0], ag_ss.at[t], ag_rs.at[t, c, 2], at_y(1)).wait_recv()

    def sum_and_send(t, xc):
        s[...] = part[0, xc].astype(F32) + fl[t, xc].astype(F32) + fr[t, xc].astype(F32)

        def block(gx, carry):
            for k in range(2):
                r = gx * 2 + k
                top = s[pl.ds(r, 8, stride=64), :]
                low = s[pl.ds(r + 32, 8, stride=64), :]
                hs[xc, gx, k] = jnp.concatenate([top, low], 0).astype(BF16)
            return carry

        lax.fori_loop(0, GX, block, 0)
        exchange(H, t, xc)

    def x_third(t):
        for rel in range(GY):
            hk = hrb[t, :, :, rel].reshape(512, 128)
            ht[rel * 144:(rel + 1) * 144, :] = lax.dot_general(
                pad[...], hk, NT, preferred_element_type=F32
            ).astype(BF16)
        v = jnp.dot(ht[...], fx[...], preferred_element_type=F32).astype(BF16)
        pu[2] = v[:144]
        for rel in (1, 2, 3):
            pu[2 + rel] = v[rel * 144:(rel + 1) * 144]
            pb_copy(t, rel).start()

    def x_transform(t, put):
        for k in range(2):
            hk = hr[t, :, :, k].reshape(512, 128)
            v = lax.dot_general(pad[...], hk, NT, preferred_element_type=F32).astype(BF16)
            pu[k] = jnp.dot(v, fx[...], preferred_element_type=F32).astype(BF16)
        pb_all(t).wait_recv()
        third = pu[2].astype(F32) + pb[t, 1].astype(F32) + pb[t, 2].astype(F32) + pb[t, 3].astype(F32)
        v = jnp.concatenate([pu[0], pu[1], third.astype(BF16)], 0)
        for q in range(2):
            for n in range(2):
                put(q, n * 512, jnp.dot(v, spread[q, :, n * 512:(n + 1) * 512], preferred_element_type=F32))

    def x_inverse_and_send(t):
        y = jnp.dot(lw[:432, :], fold[0], preferred_element_type=F32)
        y = (y + jnp.dot(lw[432:, :], fold[1], preferred_element_type=F32)).astype(BF16)
        for k in (2, 0, 1):
            v = jnp.dot(padt[...], y[k * 144:(k + 1) * 144], preferred_element_type=F32).astype(BF16)
            if k == 2:
                yb[t, 0] = v
                for rel in (1, 2, 3):
                    yb_copy(t, rel).start()
            else:
                yk[k] = v
        for xc in range(2):
            for k in range(2):
                bx = lax.dot_general(fx[xc * 256:(xc + 1) * 256, :], yk[k], NT, preferred_element_type=F32)
                bs[xc, :, k] = bx.astype(BF16).reshape(GX, 16, 128)
            exchange(B, t, xc)

    def third_inverse_and_send(t):
        yb_all(t).wait_recv()
        for xc in range(2):
            for rel in range(GY):
                bx = lax.dot_general(fx[xc * 256:(xc + 1) * 256, :], yb[t, rel], NT, preferred_element_type=F32)
                bsb[xc, :, rel] = bx.astype(BF16).reshape(GX, 16, 128)
            exchange(BB, t, xc)

    def gather_block(t, xc):
        arrived(B, t, xc)

        def block(gx, carry):
            for k in range(2):
                r = gx * 2 + k
                v = br[t, xc, gx, k].astype(F32)
                s[pl.ds(r, 8, stride=64), :] = v[:8]
                s[pl.ds(r + 32, 8, stride=64), :] = v[8:]
            return carry

        lax.fori_loop(0, GX, block, 0)
        ag[t, 0, xc] = s[...].astype(BF16)

    def gather_third(t, xc):
        arrived(BB, t, xc)
        for rel in range(GY):
            for gx in range(GX):
                v = brb[t, xc, gx, rel].astype(F32)
                sb[rel, pl.ds(gx, 8, stride=32), :] = v[:8]
                sb[rel, pl.ds(gx + GX, 8, stride=32), :] = v[8:]
            agb[rel] = sb[rel].astype(BF16)

    def y_inverse(t, xc):
        for rel in range(GY):
            h = lax.rem(me_y + rel, GY)
            off = pl.multiple_of(h * 256, 256)
            for xp in range(4):
                rhs = jnp.concatenate(
                    [ag[t, rel, xc, xp * 128:(xp + 1) * 128, :], agb[rel, xp * 64:(xp + 1) * 64, :]], 0
                )
                v = jnp.dot(at2[...], rhs, preferred_element_type=F32).astype(BF16)
                for x2 in range(2):
                    rows = slice(xp * 128 + x2 * 64, xp * 128 + x2 * 64 + 64)
                    by[rows, pl.ds(off, 128)] = v[x2 * 128:x2 * 128 + 64]
                    by[rows, pl.ds(off + 128, 128)] = v[x2 * 128 + 64:x2 * 128 + 128]

    def depth_inverse(xc, finish, start=0, stop=5):
        def block(n, carry):
            cols = pl.ds(pl.multiple_of(n * 256, 256), 256)
            for rb in range(2):
                rows = slice(xc * HALF + rb * 256, xc * HALF + rb * 256 + 256)
                v = jnp.dot(by[rb * 256:rb * 256 + 256, :], eet[:, cols], preferred_element_type=F32)
                finish(rows, cols, v + lin[rows, cols])
            return carry

        lax.fori_loop(start, stop, block, 0, unroll=True)

    def finish_forward(rows, cols, x):
        k0 = math.sqrt(2.0 / math.pi)
        x2 = x * x
        th = jnp.tanh(k0 * x * (1.0 + 0.044715 * x2))
        half = 0.5 * (1.0 + th)
        out[rows, cols] = (x * half).astype(BF16)
        slope = half + 0.5 * x * (1.0 - th * th) * (k0 * (1.0 + 3.0 * 0.044715 * x2))
        g[rows, cols] = (cot[rows, cols].astype(F32) * slope).astype(BF16)

    def finish_backward(rows, cols, x):
        out[rows, cols] = x.astype(BF16)

    def build_kron(dims):
        at = lax.broadcasted_iota(jnp.int32, (C, CZ), 1) >> 6
        one = jnp.where(at == lax.broadcasted_iota(jnp.int32, (C, CZ), 0), 1.0, 0.0).astype(BF16)
        mixrows[...] = lax.dot_general(mix_ref[...], one, dims, preferred_element_type=F32)

        lane = lax.broadcasted_iota(jnp.int32, (NZ, CZ), 1) & (NZ - 1)
        row = lax.broadcasted_iota(jnp.int32, (NZ, CZ), 0)
        eye = jnp.where(lane == row, 1.0, 0.0).astype(F32)

        def block(c, carry):
            kron[pl.ds(pl.multiple_of(c * NZ, NZ), NZ), :] = (eye * mixrows[pl.ds(c, 1), :]).astype(BF16)
            return carry

        lax.fori_loop(0, C, block, 0)

    def linear(src, rb):
        def block(n, carry):
            cols = pl.ds(pl.multiple_of(n * 256, 256), 256)
            rows = slice(rb * 512, rb * 512 + 512)
            lin[rows, cols] = jnp.dot(src[rows, :], kron[:, cols], preferred_element_type=F32)
            return carry

        lax.fori_loop(0, 5, block, 0, unroll=True)

    def fill_weights():
        wp[...] = jnp.zeros_like(wp)
        for k in range(3):
            def block(j, carry):
                v = w[k, j].astype(F32)
                for p in range(2):
                    wp[k, j, p, :C, :C * KEPT] = v[:, p, :]
                return carry

            lax.fori_loop(0, 6, block, 0)
        lane = lax.broadcasted_iota(jnp.int32, (24, 1024), 1)
        first = lax.broadcasted_iota(jnp.int32, (24, 1024), 0) * KEPT
        mask[...] = jnp.where((lane >= first) & (lane < first + KEPT) & (lane < C * KEPT), 1.0, 0.0).astype(F32)

    def put_uh(q, at, v):
        uh[q, :, at:at + 512] = v

    def put_lin(q, at, v):
        lin[q * 432:(q + 1) * 432, at:at + 512] = v

    def put_rows(k, jp, re, im):
        at = pl.multiple_of(k * 144 + jp * 48, 48)
        lw[pl.ds(at, 48), :] = jnp.concatenate(re, 0).astype(BF16)
        lw[pl.ds(at + 432, 48), :] = jnp.concatenate(im, 0).astype(BF16)

    def mix_block(k, carry):
        for jp in range(3):
            re, im = [], []
            for j in (2 * jp, 2 * jp + 1):
                rows = pl.ds(pl.multiple_of(k * 144 + j * 24, 8), 24)
                a, b = uh[0, rows, :], uh[1, rows, :]
                r, w = wp[k, j, 0], wp[k, j, 1]
                re.append(mask[...] * (jnp.sum(a * r - b * w, 0, keepdims=True) * scale(j)))
                im.append(mask[...] * (jnp.sum(a * w + b * r, 0, keepdims=True) * scale(j)))
            put_rows(k, jp, re, im)
        return carry

    def adjoint_block(k, carry):
        for jp in range(3):
            re, im = [], []
            for j in (2 * jp, 2 * jp + 1):
                at = pl.multiple_of(k * 144 + j * 24, 8)
                r, w = wp[k, j, 0], wp[k, j, 1]
                gr = jnp.sum(lin[pl.ds(at, 24), :1024] * mask[...], 0, keepdims=True) * scale(j)
                gi = jnp.sum(lin[pl.ds(at + 432, 24), :1024] * mask[...], 0, keepdims=True) * scale(j)
                gh[k, j, 0:1, :] = gr
                gh[k, j, 1:2, :] = gi
                re.append(gr * r + gi * w)
                im.append(gi * r - gr * w)
            put_rows(k, jp, re, im)
        return carry

    def weight_terms(k, j):
        rows = pl.ds(pl.multiple_of(k * 144 + j * 24, 8), 24)
        a, b = uh[0, rows, :], uh[1, rows, :]
        gr, gi = gh[k, j, 0:1, :], gh[k, j, 1:2, :]
        return a * gr + b * gi, a * gi - b * gr

    def gs_copy():
        return remote(gss, gsr, gs_sem.at[0], gs_sem.at[1], twin)

    def weight_gradient_send():
        def block(k, carry):
            for jj in range(3):
                re, im = weight_terms(k, (1 - me_t) * 3 + jj)
                at = pl.multiple_of(k * 144 + jj * 48, 48)
                gss[pl.ds(at, 48), :] = jnp.concatenate([re, im], 0).astype(BF16)
            return carry

        lax.fori_loop(0, 3, block, 0)
        gs_copy().start()

    def weight_gradient_finish():
        gs_copy().wait_recv()

        def block(k, carry):
            for jj in range(3):
                re, im = weight_terms(k, me_t * 3 + jj)
                at = pl.multiple_of(k * 144 + jj * 48, 48)
                other = gsr[pl.ds(at, 48), :].astype(F32)
                gs_ref[k, jj, :, 0, :] = (re + other[:24])[:C, :C * KEPT]
                gs_ref[k, jj, :, 1, :] = (im + other[24:])[:C, :C * KEPT]
            return carry

        lax.fori_loop(0, 3, block, 0)

    def mixing_terms():
        lane = lax.broadcasted_iota(jnp.int32, (256, 256), 1) & (NZ - 1)
        row = lax.broadcasted_iota(jnp.int32, (256, 256), 0) & (NZ - 1)
        eye = jnp.where(lane == row, 1.0, 0.0).astype(F32)

        def block(cb, carry):
            cols = pl.ds(pl.multiple_of(cb * 256, 256), 256)
            for nb in range(5):
                o = lax.dot_general(
                    u[:, cols], g[:, nb * 256:(nb + 1) * 256], TN, preferred_element_type=F32
                )
                gmx[cb, 0:4, nb * 256:(nb + 1) * 256] = jnp.sum((o * eye).reshape(4, NZ, 256), 1)
            return carry

        gmx[...] = jnp.zeros_like(gmx)
        lax.fori_loop(0, 5, block, 0)
        v = gmx[...].reshape(40, CZ)
        hi = v.astype(BF16)
        low = (v - hi.astype(F32)).astype(BF16)
        sel = lax.broadcasted_iota(jnp.int32, (CZ, 128), 0) >> 6
        sel = jnp.where(sel == lax.broadcasted_iota(jnp.int32, (CZ, 128), 1), 1.0, 0.0).astype(BF16)
        gmy[0] = jnp.dot(hi, sel, preferred_element_type=F32) + jnp.dot(low, sel, preferred_element_type=F32)

    def gy_copy(rel):
        return remote(gmy.at[0], gmy.at[rel], gm_ss.at[0], gm_rs.at[0], at_y(rel))

    def gy_all():
        return remote(gmy.at[pl.ds(0, 3)], gmy.at[pl.ds(0, 3)], gm_ss.at[0], gm_rs.at[0], at_y(1))

    def gx_copy(d):
        return remote(gma.at[0], gma.at[d], gm_ss.at[1], gm_rs.at[1], at_x(d))

    def gx_all():
        return remote(gma.at[others], gma.at[others], gm_ss.at[1], gm_rs.at[1], at_x(1))

    def ta_copy():
        return remote(gma.at[16], gma.at[17], ta_sem.at[0], ta_sem.at[1], twin)

    wait_loads(0, 1, 2, 3)
    start_loads(4, 5, 6)
    forward_block(u, 0, 2, 1)
    pl.semaphore_wait(barrier, 19)
    rs_start(0, 0, 0, 1, 2)
    wait_loads(4, 5)
    forward_block(u, 0, 3, 0)
    rs_start(0, 0, 3)
    send_third(0, 0)
    wait_loads(6)
    start_loads(*range(7, 16))
    forward_block(u, 1, 2, 1)
    rs_start(0, 1, 0, 1)
    forward_block(u, 1, 3, 0)
    send_third(0, 1)
    rs_forward(0, 0)
    rs_start(0, 1, 2, 3)
    wait_loads(7)
    fill_weights()
    rs_forward(0, 1)
    build_kron((((1,), (0,)), ((), ())))
    wait_loads(*range(8, 16))

    def sums(t, meanwhile):
        for c in range(2):
            rs_rest(t, c)
            sum_and_send(t, c)
        meanwhile()
        arrived(HB, t, 0)
        arrived(HB, t, 1)
        x_third(t)
        arrived(H, t, 0)
        arrived(H, t, 1)

    sums(0, lambda: None)

    x_transform(0, put_uh)
    lax.fori_loop(0, 3, mix_block, 0, unroll=True)
    x_inverse_and_send(0)

    def gather(t, src):
        third_inverse_and_send(t)
        gather_block(t, 0)
        ag_start(t, 0)
        gather_block(t, 1)
        linear(src, 0)
        ag_forward(t, 0)
        ag_start(t, 1)
        linear(src, 1)
        ag_forward(t, 1)

    gather(0, u)
    rs_sent(0)
    for kind in (H, B, HB, BB):
        departed(kind, 0)
    pb_all(0).wait_send()

    ag_finish(0, 0)
    gather_third(0, 0)
    y_inverse(0, 0)
    depth_inverse(0, finish_forward)
    act_out = [
        pltpu.make_async_copy(out.at[pl.ds(xc * HALF, HALF)], act_hbm.at[pl.ds(xc * HALF, HALF)], out_sem.at[0, xc])
        for xc in range(2)
    ]
    act_out[0].start()
    forward_block(g, 0, 2, 1)
    rs_start(1, 0, 0, 1, 2)
    forward_block(g, 0, 3, 0)
    rs_start(1, 0, 3)
    send_third(1, 0)
    ag_finish(0, 1)
    gather_third(0, 1)
    y_inverse(0, 1)
    depth_inverse(1, finish_forward, 0, 3)
    rs_forward(1, 0)
    depth_inverse(1, finish_forward, 3, 5)
    act_out[1].start()
    forward_block(g, 1, 2, 1)
    rs_start(1, 1, 0, 1, 2)
    forward_block(g, 1, 3, 0)
    rs_start(1, 1, 3)
    send_third(1, 1)
    rs_forward(1, 1)

    def mixing_send():
        mixing_terms()
        for rel in (1, 2, 3):
            gy_copy(rel).start()

    sums(1, mixing_send)

    x_transform(1, put_lin)
    lax.fori_loop(0, 3, adjoint_block, 0, unroll=True)
    x_inverse_and_send(1)
    weight_gradient_send()
    gy_all().wait_recv()
    gma[0] = gmy[0] + gmy[1] + gmy[2] + gmy[3]
    over_gx(lambda d: gx_copy(d).start())
    build_kron(TN)
    gather(1, g)
    gx_all().wait_recv()
    gma[16] = jnp.sum(gma[0:16], 0)
    ta_copy().start()
    weight_gradient_finish()
    act_out[0].wait()
    act_out[1].wait()
    ag_finish(1, 0)
    gather_third(1, 0)
    y_inverse(1, 0)
    depth_inverse(0, finish_backward)
    gf_out = [
        pltpu.make_async_copy(out.at[pl.ds(xc * HALF, HALF)], gf_hbm.at[pl.ds(xc * HALF, HALF)], out_sem.at[1, xc])
        for xc in range(2)
    ]
    gf_out[0].start()
    ag_finish(1, 1)
    gather_third(1, 1)
    y_inverse(1, 1)
    depth_inverse(1, finish_backward)
    gf_out[1].start()
    ta_copy().wait_recv()
    total = (gma[16] + gma[17]) * (1.0 / math.sqrt(2 * NX * NY * NZ))
    for cb in range(5):
        gm_ref[cb * 4:(cb + 1) * 4, :] = total[cb * 8:cb * 8 + 4, :C]

    ag_sent(0)
    ag_sent(1)
    rs_sent(1)
    for kind in (H, B, HB, BB):
        departed(kind, 1)
    pb_all(1).wait_send()
    yb_all(0).wait_send()
    yb_all(1).wait_send()
    gs_copy().wait_send()
    gy_all().wait_send()
    gx_all().wait_send()
    ta_copy().wait_send()
    gf_out[0].wait()
    gf_out[1].wait()


def hand_over(act_in, gf_in, gs_in, gm_in, act_out, gf_out, gs_out, gm_out, act, gf, gs, gm, in_sem, out_sem):
    pieces = [(gs_in.at[k], gs.at[k], gs_out.at[k]) for k in range(3)] + [(gm_in, gm, gm_out)]
    for i in range(4):
        rows = pl.ds(i * 256, 256)
        pieces.append((act_in.at[rows], act.at[rows], act_out.at[rows]))
        pieces.append((gf_in.at[rows], gf.at[rows], gf_out.at[rows]))
    loads = [pltpu.make_async_copy(p[0], p[1], in_sem.at[i]) for i, p in enumerate(pieces)]
    stores = [pltpu.make_async_copy(p[1], p[2], out_sem.at[i]) for i, p in enumerate(pieces)]
    for load in loads:
        load.start()
    for load, store in zip(loads, stores):
        load.wait()
        store.start()
    for store in stores:
        store.wait()


def shards(features, cotangent, spectral_weight, mixing_weight):
    consts = [jnp.asarray(t) for t in tables()]
    dma = pltpu.SemaphoreType.DMA
    vmem = pltpu.VMEM
    hbm = pl.BlockSpec(memory_space=pl.ANY)
    local = pl.BlockSpec(memory_space=pltpu.VMEM)
    results = (
        jax.ShapeDtypeStruct((ROWS, CZ), BF16),
        jax.ShapeDtypeStruct((ROWS, CZ), BF16),
        jax.ShapeDtypeStruct((3, 3, C, 2, C * KEPT), F32),
        jax.ShapeDtypeStruct((C, C), F32),
    )
    parts = pl.pallas_call(
        kernel,
        out_shape=results,
        in_specs=[hbm, hbm, hbm, local] + [hbm] * 9,
        out_specs=(hbm, hbm, local, local),
        scratch_shapes=[
            vmem((ROWS, CZ), BF16),
            vmem((ROWS, CZ), BF16),
            vmem((ROWS, CZ), BF16),
            vmem((ROWS, CZ), BF16),
            vmem((GY, CZ, 256), BF16),
            vmem((GY * 256, CZ), BF16),
            vmem((CZ, CZ), BF16),
            vmem((ROWS, CZ), F32),
            vmem((512, 128), BF16),
            vmem((144, 128), BF16),
            vmem((128, 144), BF16),
            vmem((2, 128, 1024), BF16),
            vmem((2, 1024, 128), BF16),
            vmem((192, 256), BF16),
            vmem((256, 192), BF16),
            vmem((3, 6, C, 2, C * KEPT), BF16),
            vmem((C, CZ), F32),
            vmem((3, 6, 2, 24, 1024), F32),
            vmem((2, 432, 1024), F32),
            vmem((576, 512), BF16),
            vmem((2, 128, 128), BF16),
            vmem((864, 1024), BF16),
            vmem((432, 1024), BF16),
            vmem((432, 1024), BF16),
            vmem((4, 2, 512, 128), BF16),
            vmem((2, 2, 512, 128), BF16),
            vmem((2, 2, 512, 128), BF16),
            vmem((2, 2, 512, 128), BF16),
            vmem((2, GX, 2, 16, 128), BF16),
            vmem((2, 2, GX, 2, 16, 128), BF16),
            vmem((2, GX, 2, 16, 128), BF16),
            vmem((2, 2, GX, 2, 16, 128), BF16),
            vmem((2, 4, 2, 512, 128), BF16),
            vmem((2, GX, GY, 16, 128), BF16),
            vmem((2, 2, GX, GY, 16, 128), BF16),
            vmem((2, GX, GY, 16, 128), BF16),
            vmem((2, 2, GX, GY, 16, 128), BF16),
            vmem((6, 144, 128), BF16),
            vmem((2, GY, 144, 128), BF16),
            vmem((2, GY, 128, 128), BF16),
            vmem((GY, 256, 128), BF16),
            vmem((HALF, 1024), BF16),
            vmem((512, 128), F32),
            vmem((GY, 256, 128), F32),
            vmem((24, 1024), F32),
            vmem((3, 6, 8, 1024), F32),
            vmem((5, 8, CZ), F32),
            vmem((4, 40, 128), F32),
            vmem((18, 40, 128), F32),
            dma((16,)),
            dma((2, 2)),
            dma((2,)),
            dma((2, 2, 3)),
            dma((2,)),
            dma((2, 2, 3)),
            dma((4, 2)),
            dma((4, 2, 2)),
            dma((2, 2)),
            dma((2, 2)),
            dma((2,)),
            dma((2,)),
            dma((2,)),
            dma((2,)),
        ],
        compiler_params=pltpu.CompilerParams(
            collective_id=0, has_side_effects=True, vmem_limit_bytes=60 * 1024 * 1024
        ),
    )(
        features.reshape(ROWS, CZ), cotangent.reshape(ROWS, CZ),
        spectral_weight.transpose(0, 1, 3, 2, 4), mixing_weight, *consts,
    )
    act, gf, gs, gm = pl.pallas_call(
        hand_over,
        out_shape=results,
        in_specs=[hbm] * 4,
        out_specs=(hbm,) * 4,
        scratch_shapes=[vmem(r.shape, r.dtype) for r in results] + [dma((12,)), dma((12,))],
        compiler_params=pltpu.CompilerParams(vmem_limit_bytes=60 * 1024 * 1024),
    )(*parts)
    return act.reshape(features.shape), gf.reshape(features.shape), gs.transpose(0, 1, 3, 2, 4), gm


def solution(mesh):
    in_specs = (
        P("ta", "gx", "gy", None),
        P("ta", "gx", "gy", None),
        P("gx", "gy", None, None, None),
        P(),
    )
    out_specs = (
        P("ta", "gx", "gy", None),
        P("ta", "gx", "gy", None),
        P("gx", ("gy", "ta"), None, None, None),
        P(),
    )
    return jax.shard_map(shards, mesh=mesh, in_specs=in_specs, out_specs=out_specs, check_vma=False)
```

```python
import math

import jax
import jax.numpy as jnp
import ml_dtypes
import numpy as np
from jax import lax
from jax.experimental import pallas as pl
from jax.experimental.pallas import tpu as pltpu
from jax.sharding import PartitionSpec as P

NX = 256
NY = 256
NZ = 64
C = 20
M = 24
KEPT = 48
CZ = C * NZ
GX = 16
GY = 4
ROWS = 1024
HALF = 512
F32 = jnp.float32
BF16 = jnp.bfloat16
MESH = pl.DeviceIdType.MESH
NT = (((1,), (1,)), ((), ()))
TN = (((0,), (0,)), ((), ()))


def cos_sin(length, count, folded):
    freq = np.arange(count)
    if folded:
        freq = np.where(freq < count // 2, freq, freq + length - count)
    phases = np.arange(length)[:, None] * freq[None, :] % length
    angles = phases.astype(np.float32) * np.float32(2.0 * math.pi / length)
    return np.cos(angles), np.sin(angles)


def complex_table(length, count):
    cosine, sine = cos_sin(length, count, True)
    return np.stack([np.stack([cosine, -sine], 1), np.stack([sine, cosine], 1)], 0)


def tables():
    cosine, sine = cos_sin(NZ, M, False)
    depth = np.stack([cosine, -sine], 1)
    ee = np.zeros((GY, C, NZ, 2, 128), np.float32)
    for h in range(GY):
        for jl in range(6):
            for c in range(C):
                ee[h, c, :, :, jl * C + c] = depth[:, :, h * 6 + jl]
    ee = ee.reshape(GY, CZ, 256)
    eet = np.ascontiguousarray(ee.transpose(0, 2, 1)).reshape(GY * 256, CZ)
    height = complex_table(NY, KEPT).reshape(2, GY, 64, 2, KEPT)
    height = height.transpose(1, 3, 4, 0, 2).reshape(GY, 2, GX, 3, 2, 64)
    a2 = np.zeros((GY, 192, 2, 2, 64), np.float32)
    for x2 in range(2):
        a2[:, x2 * 64:x2 * 64 + 64, x2] = height[:, :, :, :2].reshape(GY, 64, 2, 64)
        a2[:, 128 + x2 * 32:160 + x2 * 32, x2] = height[:, :, :, 2].reshape(GY, 32, 2, 64)
    a2 = a2.reshape(GY, 192, 256)
    at2 = np.ascontiguousarray(a2.transpose(0, 2, 1))
    width = complex_table(NX, KEPT).reshape(2, GX, 2, 8, 2, KEPT)
    fx = np.zeros((2, GX, 2, 8, 2, 64), np.float32)
    fx[..., :KEPT] = width.transpose(2, 1, 0, 3, 4, 5)
    fx = fx.reshape(512, 128)
    spread = np.zeros((2, 128, 1024), np.float32)
    for q in range(2):
        for c in range(C):
            spread[q, q * 64 + np.arange(KEPT), c * KEPT + np.arange(KEPT)] = 1.0
    fold = np.ascontiguousarray(spread.transpose(0, 2, 1))
    pad = np.zeros((6, 24, 128), np.float32)
    for jl in range(6):
        for c in range(C):
            pad[jl, c, jl * C + c] = 1.0
    pad = pad.reshape(144, 128)
    padt = np.ascontiguousarray(pad.T)
    return [t.astype(ml_dtypes.bfloat16) for t in (ee, eet, a2, at2, fx, pad, padt, spread, fold)]


def kernel(
    u_hbm, cot_hbm, w_hbm, mix_ref, ee_hbm, eet_hbm, a2_hbm, at2_hbm, fx_hbm, pad_hbm, padt_hbm, spread_hbm, fold_hbm,
    act_hbm, gf_hbm, gs_ref, gm_ref,
    u, cot, g, out, ee, eet, kron, lin, fx, pad, padt, spread, fold, a2, at2, w, mixrows, wp, uh, ht, yk, lw, gss, gsr,
    part, dg, fl, fr, hs, hr, bs, br, ag, hsb, hrb, bsb, brb, pu, pb, yb, agb, by, s, sb, mask, gh, gmx, gmy, gma,
    in_sem, out_sem, rs_ss, rs_rs, ag_ss, ag_rs, ex_ss, ex_rs, third_ss, third_rs, gs_sem, gm_ss, gm_rs, ta_sem,
):
    me_x = lax.axis_index("gx")
    me_y = lax.axis_index("gy")
    me_t = lax.axis_index("ta")

    def at_y(rel):
        return (me_x, lax.rem(me_y + rel, GY), me_t)

    def at_x(d):
        return (lax.rem(me_x + d, GX), me_y, me_t)

    twin = (me_x, me_y, 1 - me_t)

    opposite, left = lax.rem(me_y + 2, GY), lax.rem(me_y + 3, GY)
    right = lax.rem(me_y + 1, GY)
    first, second = pl.ds(0, HALF), pl.ds(HALF, HALF)
    loads = [
        pltpu.make_async_copy(src, dst, in_sem.at[i])
        for i, (src, dst) in enumerate([
            (u_hbm.at[first], u.at[first]), (ee_hbm.at[opposite], ee.at[opposite]),
            (ee_hbm.at[right], ee.at[right]), (a2_hbm.at[me_y], a2),
            (ee_hbm.at[left], ee.at[left]), (ee_hbm.at[me_y], ee.at[me_y]), (u_hbm.at[second], u.at[second]),
            (w_hbm, w), (fx_hbm, fx), (pad_hbm, pad), (padt_hbm, padt),
            (spread_hbm, spread), (fold_hbm, fold), (at2_hbm.at[me_y], at2), (eet_hbm, eet), (cot_hbm, cot),
        ])
    ]

    def start_loads(*ids):
        for i in ids:
            loads[i].start()

    def wait_loads(*ids):
        for i in ids:
            loads[i].wait()

    start_loads(0, 1, 2, 3)

    barrier = pltpu.get_barrier_semaphore()
    for rel in (1, 2, 3):
        pl.semaphore_signal(barrier, inc=1, device_id=at_y(rel), device_id_type=MESH)

    def greet(d, carry):
        pl.semaphore_signal(barrier, inc=1, device_id=at_x(d), device_id_type=MESH)
        return carry

    lax.fori_loop(1, GX, greet, 0)
    pl.semaphore_signal(barrier, inc=1, device_id=twin, device_id_type=MESH)

    def remote(src, dst, ss, rs, dev):
        return pltpu.make_async_remote_copy(
            src_ref=src, dst_ref=dst, send_sem=ss, recv_sem=rs, device_id=dev, device_id_type=MESH
        )

    upper, lower = pl.ds(0, 256), pl.ds(256, 256)

    def rs_copy(t, c, i):
        src, dst, rel = [
            (part.at[2, c, upper], dg.at[t, c, upper], 1),
            (part.at[2, c, lower], dg.at[t, c, lower], 3),
            (part.at[1, c, lower], fl.at[t, c, lower], 1),
            (part.at[3, c, upper], fr.at[t, c, upper], 3),
            (part.at[1, c, upper], fl.at[t, c, upper], 1),
            (part.at[3, c, lower], fr.at[t, c, lower], 3),
        ][i]
        return remote(src, dst, rs_ss.at[t], rs_rs.at[t, c, min(i, 2)], at_y(rel))

    def ag_copy(t, c, i):
        src, dst, rel = [
            (ag.at[t, 0, c, upper], ag.at[t, 3, c, upper], 1),
            (ag.at[t, 0, c, lower], ag.at[t, 1, c, lower], 3),
            (ag.at[t, 0, c, lower], ag.at[t, 3, c, lower], 1),
            (ag.at[t, 0, c, upper], ag.at[t, 1, c, upper], 3),
            (ag.at[t, 3, c, upper], ag.at[t, 2, c, upper], 1),
            (ag.at[t, 1, c, lower], ag.at[t, 2, c, lower], 3),
        ][i]
        return remote(src, dst, ag_ss.at[t], ag_rs.at[t, c, min(i, 2)], at_y(rel))

    def rs_rest(t, c):
        remote(part.at[0], fl.at[t], rs_ss.at[t], rs_rs.at[t, c, 2], at_y(1)).wait_recv()

    def rs_sent(t):
        remote(part.at[pl.ds(0, 3)], part.at[pl.ds(0, 3)], rs_ss.at[t], rs_rs.at[t, 0, 2], at_y(1)).wait_send()

    def ag_sent(t):
        blocks = ag.at[t, pl.ds(0, 3)]
        remote(blocks, blocks, ag_ss.at[t], ag_rs.at[t, 0, 2], at_y(1)).wait_send()

    H, B, HB, BB = range(4)
    pairs = ((hs, hr), (bs, br), (hsb, hrb), (bsb, brb))
    others = pl.ds(0, GX - 1)

    def exchange(kind, t, xc):
        src, dst = pairs[kind]

        def step(d, carry):
            to = lax.rem(me_x + d, GX)
            remote(
                src.at[xc, to], dst.at[t, xc, me_x], ex_ss.at[kind, t], ex_rs.at[kind, t, xc], at_x(d)
            ).start()
            return carry

        lax.fori_loop(1, GX, step, 0)
        dst[t, xc, me_x] = src[xc, me_x]

    def arrived(kind, t, xc):
        src, dst = pairs[kind]
        remote(
            src.at[xc, others], dst.at[t, xc, others], ex_ss.at[kind, t], ex_rs.at[kind, t, xc], at_x(1)
        ).wait_recv()

    def departed(kind, t):
        src, dst = pairs[kind]
        remote(
            src.at[:, others], dst.at[t, :, others], ex_ss.at[kind, t], ex_rs.at[kind, t, 0], at_x(1)
        ).wait_send()

    def pb_copy(t, rel):
        return remote(pu.at[2 + rel], pb.at[t, rel], third_ss.at[t, 0], third_rs.at[t, 0], at_y(rel))

    def yb_copy(t, rel):
        return remote(yb.at[t, 0], yb.at[t, GY - rel], third_ss.at[t, 1], third_rs.at[t, 1], at_y(rel))

    def pb_all(t):
        return remote(pu.at[pl.ds(0, 3)], pb.at[t, pl.ds(0, 3)], third_ss.at[t, 0], third_rs.at[t, 0], at_y(1))

    def yb_all(t):
        blocks = yb.at[t, pl.ds(0, 3)]
        return remote(blocks, blocks, third_ss.at[t, 1], third_rs.at[t, 1], at_y(1))

    def over_gx(fn):
        def step(d, carry):
            fn(d)
            return carry

        lax.fori_loop(1, GX, step, 0)

    def scale(jl):
        first = (me_y == 0) & (jl == 0)
        return jnp.where(first, 1.0, 2.0).astype(F32) * (1.0 / float(NX * NY * NZ))

    def forward_block(src, xc, *rels):
        tab = [ee[lax.rem(me_y + rel, GY)] for rel in rels]
        tab = tab[0] if len(tab) == 1 else jnp.concatenate(tab, 1)
        both = jnp.dot(src[xc * HALF:(xc + 1) * HALF, :], tab, preferred_element_type=F32).astype(BF16)
        for xp in range(4):
            r = xp * 128
            rhs = jnp.concatenate([
                jnp.concatenate(
                    [both[row:row + 64, i * 256 + p * 128:i * 256 + p * 128 + 128] for i in range(len(rels))], 1
                )
                for row in (r, r + 64) for p in range(2)
            ], 0)
            o = jnp.dot(a2[...], rhs, preferred_element_type=F32)
            for i, rel in enumerate(rels):
                part[rel, xc, xp * 128:(xp + 1) * 128, :] = o[:128, i * 128:(i + 1) * 128].astype(BF16)
                sb[i, xp * 64:(xp + 1) * 64, :] = o[128:, i * 128:(i + 1) * 128]
        for i, rel in enumerate(rels):
            for gx in range(GX):
                top = sb[i, pl.ds(gx, 8, stride=32), :]
                low = sb[i, pl.ds(gx + GX, 8, stride=32), :]
                hsb[xc, gx, rel] = jnp.concatenate([top, low], 0).astype(BF16)

    def send_third(t, xc):
        exchange(HB, t, xc)

    def rs_start(t, c, *ids):
        for i in ids:
            rs_copy(t, c, i).start()

    def rs_forward(t, c):
        rs_copy(t, c, 0).wait_recv()
        part[1, c, :256] = (part[1, c, :256].astype(F32) + dg[t, c, :256].astype(F32)).astype(BF16)
        rs_start(t, c, 4)
        rs_copy(t, c, 1).wait_recv()
        part[3, c, 256:] = (part[3, c, 256:].astype(F32) + dg[t, c, 256:].astype(F32)).astype(BF16)
        rs_start(t, c, 5)

    def ag_start(t, c):
        for i in range(4):
            ag_copy(t, c, i).start()

    def ag_forward(t, c):
        for i in (0, 1):
            ag_copy(t, c, i).wait_recv()
            ag_copy(t, c, 4 + i).start()

    def ag_finish(t, c):
        remote(ag.at[t, 0], ag.at[t, 0], ag_ss.at[t], ag_rs.at[t, c, 2], at_y(1)).wait_recv()

    def sum_and_send(t, xc):
        s[...] = part[0, xc].astype(F32) + fl[t, xc].astype(F32) + fr[t, xc].astype(F32)

        def block(gx, carry):
            for k in range(2):
                r = gx * 2 + k
                top = s[pl.ds(r, 8, stride=64), :]
                low = s[pl.ds(r + 32, 8, stride=64), :]
                hs[xc, gx, k] = jnp.concatenate([top, low], 0).astype(BF16)
            return carry

        lax.fori_loop(0, GX, block, 0)
        exchange(H, t, xc)

    def x_third(t):
        for rel in range(GY):
            hk = hrb[t, :, :, rel].reshape(512, 128)
            ht[rel * 144:(rel + 1) * 144, :] = lax.dot_general(
                pad[...], hk, NT, preferred_element_type=F32
            ).astype(BF16)
        v = jnp.dot(ht[...], fx[...], preferred_element_type=F32).astype(BF16)
        pu[2] = v[:144]
        for rel in (1, 2, 3):
            pu[2 + rel] = v[rel * 144:(rel + 1) * 144]
            pb_copy(t, rel).start()

    def x_transform(t, put):
        for k in range(2):
            hk = hr[t, :, :, k].reshape(512, 128)
            v = lax.dot_general(pad[...], hk, NT, preferred_element_type=F32).astype(BF16)
            pu[k] = jnp.dot(v, fx[...], preferred_element_type=F32).astype(BF16)
        pb_all(t).wait_recv()
        third = pu[2].astype(F32) + pb[t, 1].astype(F32) + pb[t, 2].astype(F32) + pb[t, 3].astype(F32)
        v = jnp.concatenate([pu[0], pu[1], third.astype(BF16)], 0)
        for q in range(2):
            for n in range(2):
                put(q, n * 512, jnp.dot(v, spread[q, :, n * 512:(n + 1) * 512], preferred_element_type=F32))

    def x_inverse_and_send(t):
        y = jnp.dot(lw[:432, :], fold[0], preferred_element_type=F32)
        y = (y + jnp.dot(lw[432:, :], fold[1], preferred_element_type=F32)).astype(BF16)
        for k in (2, 0, 1):
            v = jnp.dot(padt[...], y[k * 144:(k + 1) * 144], preferred_element_type=F32).astype(BF16)
            if k == 2:
                yb[t, 0] = v
                for rel in (1, 2, 3):
                    yb_copy(t, rel).start()
            else:
                yk[k] = v
        for xc in range(2):
            for k in range(2):
                bx = lax.dot_general(fx[xc * 256:(xc + 1) * 256, :], yk[k], NT, preferred_element_type=F32)
                bs[xc, :, k] = bx.astype(BF16).reshape(GX, 16, 128)
            exchange(B, t, xc)

    def third_inverse_and_send(t):
        yb_all(t).wait_recv()
        for xc in range(2):
            for rel in range(GY):
                bx = lax.dot_general(fx[xc * 256:(xc + 1) * 256, :], yb[t, rel], NT, preferred_element_type=F32)
                bsb[xc, :, rel] = bx.astype(BF16).reshape(GX, 16, 128)
            exchange(BB, t, xc)

    def gather_block(t, xc):
        arrived(B, t, xc)

        def block(gx, carry):
            for k in range(2):
                r = gx * 2 + k
                v = br[t, xc, gx, k].astype(F32)
                s[pl.ds(r, 8, stride=64), :] = v[:8]
                s[pl.ds(r + 32, 8, stride=64), :] = v[8:]
            return carry

        lax.fori_loop(0, GX, block, 0)
        ag[t, 0, xc] = s[...].astype(BF16)

    def gather_third(t, xc):
        arrived(BB, t, xc)
        for rel in range(GY):
            for gx in range(GX):
                v = brb[t, xc, gx, rel].astype(F32)
                sb[rel, pl.ds(gx, 8, stride=32), :] = v[:8]
                sb[rel, pl.ds(gx + GX, 8, stride=32), :] = v[8:]
            agb[rel] = sb[rel].astype(BF16)

    def y_inverse(t, xc):
        for xp in range(4):
            two, third = slice(xp * 128, (xp + 1) * 128), slice(xp * 64, (xp + 1) * 64)
            rhs = jnp.concatenate([
                jnp.concatenate([ag[t, rel, xc, two, :] for rel in range(GY)], 1),
                jnp.concatenate([agb[rel, third, :] for rel in range(GY)], 1),
            ], 0)
            v = jnp.dot(at2[...], rhs, preferred_element_type=F32).astype(BF16)
            for rel in range(GY):
                off = pl.multiple_of(lax.rem(me_y + rel, GY) * 256, 256)
                w_rel = v[:, rel * 128:(rel + 1) * 128]
                for x2 in range(2):
                    rows = slice(xp * 128 + x2 * 64, xp * 128 + x2 * 64 + 64)
                    by[rows, pl.ds(off, 128)] = w_rel[x2 * 128:x2 * 128 + 64]
                    by[rows, pl.ds(off + 128, 128)] = w_rel[x2 * 128 + 64:x2 * 128 + 128]

    def depth_inverse(xc, finish, start=0, stop=3):
        for n in range(start, stop):
            cols = slice(n * 512, min(n * 512 + 512, CZ))
            for rb in range(2):
                rows = slice(xc * HALF + rb * 256, xc * HALF + rb * 256 + 256)
                v = jnp.dot(by[rb * 256:rb * 256 + 256, :], eet[:, cols], preferred_element_type=F32)
                finish(rows, cols, v + lin[rows, cols])

    def finish_forward(rows, cols, x):
        k0 = math.sqrt(2.0 / math.pi)
        x2 = x * x
        th = jnp.tanh(k0 * x * (1.0 + 0.044715 * x2))
        half = 0.5 * (1.0 + th)
        out[rows, cols] = (x * half).astype(BF16)
        slope = half + 0.5 * x * (1.0 - th * th) * (k0 * (1.0 + 3.0 * 0.044715 * x2))
        g[rows, cols] = (cot[rows, cols].astype(F32) * slope).astype(BF16)

    def finish_backward(rows, cols, x):
        out[rows, cols] = x.astype(BF16)

    def build_kron(dims):
        at = lax.broadcasted_iota(jnp.int32, (C, CZ), 1) >> 6
        one = jnp.where(at == lax.broadcasted_iota(jnp.int32, (C, CZ), 0), 1.0, 0.0).astype(BF16)
        mixrows[...] = lax.dot_general(mix_ref[...], one, dims, preferred_element_type=F32)

        lane = lax.broadcasted_iota(jnp.int32, (NZ, CZ), 1) & (NZ - 1)
        row = lax.broadcasted_iota(jnp.int32, (NZ, CZ), 0)
        eye = jnp.where(lane == row, 1.0, 0.0).astype(F32)

        def block(c, carry):
            kron[pl.ds(pl.multiple_of(c * NZ, NZ), NZ), :] = (eye * mixrows[pl.ds(c, 1), :]).astype(BF16)
            return carry

        lax.fori_loop(0, C, block, 0)

    def linear(src, rb):
        def block(n, carry):
            cols = pl.ds(pl.multiple_of(n * 256, 256), 256)
            rows = slice(rb * 512, rb * 512 + 512)
            lin[rows, cols] = jnp.dot(src[rows, :], kron[:, cols], preferred_element_type=F32)
            return carry

        lax.fori_loop(0, 5, block, 0, unroll=True)

    def fill_weights():
        wp[...] = jnp.zeros_like(wp)
        for k in range(3):
            def block(j, carry):
                v = w[k, j].astype(F32)
                for p in range(2):
                    wp[k, j, p, :C, :C * KEPT] = v[:, p, :]
                return carry

            lax.fori_loop(0, 6, block, 0)
        lane = lax.broadcasted_iota(jnp.int32, (24, 1024), 1)
        first = lax.broadcasted_iota(jnp.int32, (24, 1024), 0) * KEPT
        mask[...] = jnp.where((lane >= first) & (lane < first + KEPT) & (lane < C * KEPT), 1.0, 0.0).astype(F32)

    def put_uh(q, at, v):
        uh[q, :, at:at + 512] = v

    def put_lin(q, at, v):
        lin[q * 432:(q + 1) * 432, at:at + 512] = v

    def put_rows(k, jp, re, im):
        at = pl.multiple_of(k * 144 + jp * 48, 48)
        lw[pl.ds(at, 48), :] = jnp.concatenate(re, 0).astype(BF16)
        lw[pl.ds(at + 432, 48), :] = jnp.concatenate(im, 0).astype(BF16)

    def mix_block(k, carry):
        for jp in range(3):
            re, im = [], []
            for j in (2 * jp, 2 * jp + 1):
                rows = pl.ds(pl.multiple_of(k * 144 + j * 24, 8), 24)
                a, b = uh[0, rows, :], uh[1, rows, :]
                r, w = wp[k, j, 0], wp[k, j, 1]
                re.append(mask[...] * (jnp.sum(a * r - b * w, 0, keepdims=True) * scale(j)))
                im.append(mask[...] * (jnp.sum(a * w + b * r, 0, keepdims=True) * scale(j)))
            put_rows(k, jp, re, im)
        return carry

    def adjoint_block(k, carry):
        for jp in range(3):
            re, im = [], []
            for j in (2 * jp, 2 * jp + 1):
                at = pl.multiple_of(k * 144 + j * 24, 8)
                r, w = wp[k, j, 0], wp[k, j, 1]
                gr = jnp.sum(lin[pl.ds(at, 24), :1024] * mask[...], 0, keepdims=True) * scale(j)
                gi = jnp.sum(lin[pl.ds(at + 432, 24), :1024] * mask[...], 0, keepdims=True) * scale(j)
                gh[k, j, 0:1, :] = gr
                gh[k, j, 1:2, :] = gi
                re.append(gr * r + gi * w)
                im.append(gi * r - gr * w)
            put_rows(k, jp, re, im)
        return carry

    def weight_terms(k, j):
        rows = pl.ds(pl.multiple_of(k * 144 + j * 24, 8), 24)
        a, b = uh[0, rows, :], uh[1, rows, :]
        gr, gi = gh[k, j, 0:1, :], gh[k, j, 1:2, :]
        return a * gr + b * gi, a * gi - b * gr

    def gs_copy():
        return remote(gss, gsr, gs_sem.at[0], gs_sem.at[1], twin)

    def weight_gradient_send():
        def block(k, carry):
            for jj in range(3):
                re, im = weight_terms(k, (1 - me_t) * 3 + jj)
                at = pl.multiple_of(k * 144 + jj * 48, 48)
                gss[pl.ds(at, 48), :] = jnp.concatenate([re, im], 0).astype(BF16)
            return carry

        lax.fori_loop(0, 3, block, 0)
        gs_copy().start()

    def weight_gradient_finish():
        gs_copy().wait_recv()

        def block(k, carry):
            for jj in range(3):
                re, im = weight_terms(k, me_t * 3 + jj)
                at = pl.multiple_of(k * 144 + jj * 48, 48)
                other = gsr[pl.ds(at, 48), :].astype(F32)
                gs_ref[k, jj, :, 0, :] = (re + other[:24])[:C, :C * KEPT]
                gs_ref[k, jj, :, 1, :] = (im + other[24:])[:C, :C * KEPT]
            return carry

        lax.fori_loop(0, 3, block, 0)

    def mixing_terms():
        lane = lax.broadcasted_iota(jnp.int32, (256, 256), 1) & (NZ - 1)
        row = lax.broadcasted_iota(jnp.int32, (256, 256), 0) & (NZ - 1)
        eye = jnp.where(lane == row, 1.0, 0.0).astype(F32)

        def block(cb, carry):
            cols = pl.ds(pl.multiple_of(cb * 256, 256), 256)
            for nb in range(5):
                o = lax.dot_general(
                    u[:, cols], g[:, nb * 256:(nb + 1) * 256], TN, preferred_element_type=F32
                )
                gmx[cb, 0:4, nb * 256:(nb + 1) * 256] = jnp.sum((o * eye).reshape(4, NZ, 256), 1)
            return carry

        gmx[...] = jnp.zeros_like(gmx)
        lax.fori_loop(0, 5, block, 0)
        v = gmx[...].reshape(40, CZ)
        hi = v.astype(BF16)
        low = (v - hi.astype(F32)).astype(BF16)
        sel = lax.broadcasted_iota(jnp.int32, (CZ, 128), 0) >> 6
        sel = jnp.where(sel == lax.broadcasted_iota(jnp.int32, (CZ, 128), 1), 1.0, 0.0).astype(BF16)
        gmy[0] = jnp.dot(hi, sel, preferred_element_type=F32) + jnp.dot(low, sel, preferred_element_type=F32)

    def gy_copy(rel):
        return remote(gmy.at[0], gmy.at[rel], gm_ss.at[0], gm_rs.at[0], at_y(rel))

    def gy_all():
        return remote(gmy.at[pl.ds(0, 3)], gmy.at[pl.ds(0, 3)], gm_ss.at[0], gm_rs.at[0], at_y(1))

    def gx_copy(d):
        return remote(gma.at[0], gma.at[d], gm_ss.at[1], gm_rs.at[1], at_x(d))

    def gx_all():
        return remote(gma.at[others], gma.at[others], gm_ss.at[1], gm_rs.at[1], at_x(1))

    def ta_copy():
        return remote(gma.at[16], gma.at[17], ta_sem.at[0], ta_sem.at[1], twin)

    wait_loads(0, 1, 2, 3)
    start_loads(4, 5, 6)
    forward_block(u, 0, 2, 1)
    pl.semaphore_wait(barrier, 19)
    rs_start(0, 0, 0, 1, 2)
    wait_loads(4, 5)
    forward_block(u, 0, 3, 0)
    rs_start(0, 0, 3)
    send_third(0, 0)
    wait_loads(6)
    start_loads(*range(7, 16))
    forward_block(u, 1, 2, 1)
    rs_start(0, 1, 0, 1)
    forward_block(u, 1, 3, 0)
    send_third(0, 1)
    rs_forward(0, 0)
    rs_start(0, 1, 2, 3)
    wait_loads(7)
    fill_weights()
    rs_forward(0, 1)
    build_kron((((1,), (0,)), ((), ())))
    wait_loads(*range(8, 16))

    def sums(t, meanwhile):
        for c in range(2):
            rs_rest(t, c)
            sum_and_send(t, c)
        arrived(HB, t, 0)
        arrived(HB, t, 1)
        x_third(t)
        meanwhile()
        arrived(H, t, 0)
        arrived(H, t, 1)

    sums(0, lambda: None)

    x_transform(0, put_uh)
    lax.fori_loop(0, 3, mix_block, 0, unroll=True)
    x_inverse_and_send(0)

    def gather(t, src):
        third_inverse_and_send(t)
        gather_block(t, 0)
        ag_start(t, 0)
        gather_block(t, 1)
        linear(src, 0)
        ag_forward(t, 0)
        ag_start(t, 1)
        linear(src, 1)
        ag_forward(t, 1)

    gather(0, u)
    rs_sent(0)
    for kind in (H, B, HB, BB):
        departed(kind, 0)
    pb_all(0).wait_send()

    ag_finish(0, 0)
    gather_third(0, 0)
    y_inverse(0, 0)
    depth_inverse(0, finish_forward)
    act_out = [
        pltpu.make_async_copy(out.at[pl.ds(xc * HALF, HALF)], act_hbm.at[pl.ds(xc * HALF, HALF)], out_sem.at[0, xc])
        for xc in range(2)
    ]
    act_out[0].start()
    forward_block(g, 0, 2, 1)
    rs_start(1, 0, 0, 1, 2)
    forward_block(g, 0, 3, 0)
    rs_start(1, 0, 3)
    send_third(1, 0)
    ag_finish(0, 1)
    gather_third(0, 1)
    y_inverse(0, 1)
    depth_inverse(1, finish_forward, 0, 2)
    rs_forward(1, 0)
    depth_inverse(1, finish_forward, 2, 3)
    act_out[1].start()
    forward_block(g, 1, 2, 1)
    rs_start(1, 1, 0, 1, 2)
    forward_block(g, 1, 3, 0)
    rs_start(1, 1, 3)
    send_third(1, 1)
    rs_forward(1, 1)

    def mixing_send():
        mixing_terms()
        for rel in (1, 2, 3):
            gy_copy(rel).start()

    sums(1, mixing_send)

    x_transform(1, put_lin)
    lax.fori_loop(0, 3, adjoint_block, 0, unroll=True)
    x_inverse_and_send(1)
    weight_gradient_send()
    gy_all().wait_recv()
    gma[0] = gmy[0] + gmy[1] + gmy[2] + gmy[3]
    over_gx(lambda d: gx_copy(d).start())
    build_kron(TN)
    gather(1, g)
    gx_all().wait_recv()
    gma[16] = jnp.sum(gma[0:16], 0)
    ta_copy().start()
    weight_gradient_finish()
    act_out[0].wait()
    act_out[1].wait()
    ag_finish(1, 0)
    gather_third(1, 0)
    y_inverse(1, 0)
    depth_inverse(0, finish_backward)
    gf_out = [
        pltpu.make_async_copy(out.at[pl.ds(xc * HALF, HALF)], gf_hbm.at[pl.ds(xc * HALF, HALF)], out_sem.at[1, xc])
        for xc in range(2)
    ]
    gf_out[0].start()
    ag_finish(1, 1)
    gather_third(1, 1)
    y_inverse(1, 1)
    depth_inverse(1, finish_backward)
    gf_out[1].start()
    ta_copy().wait_recv()
    total = (gma[16] + gma[17]) * (1.0 / math.sqrt(2 * NX * NY * NZ))
    for cb in range(5):
        gm_ref[cb * 4:(cb + 1) * 4, :] = total[cb * 8:cb * 8 + 4, :C]

    ag_sent(0)
    ag_sent(1)
    rs_sent(1)
    for kind in (H, B, HB, BB):
        departed(kind, 1)
    pb_all(1).wait_send()
    yb_all(0).wait_send()
    yb_all(1).wait_send()
    gs_copy().wait_send()
    gy_all().wait_send()
    gx_all().wait_send()
    ta_copy().wait_send()
    gf_out[0].wait()
    gf_out[1].wait()


def hand_over(act_in, gf_in, gs_in, gm_in, act_out, gf_out, gs_out, gm_out, act, gf, gs, gm, in_sem, out_sem):
    pieces = [(gs_in.at[k], gs.at[k], gs_out.at[k]) for k in range(3)] + [(gm_in, gm, gm_out)]
    for i in range(4):
        rows = pl.ds(i * 256, 256)
        pieces.append((act_in.at[rows], act.at[rows], act_out.at[rows]))
        pieces.append((gf_in.at[rows], gf.at[rows], gf_out.at[rows]))
    loads = [pltpu.make_async_copy(p[0], p[1], in_sem.at[i]) for i, p in enumerate(pieces)]
    stores = [pltpu.make_async_copy(p[1], p[2], out_sem.at[i]) for i, p in enumerate(pieces)]
    for load in loads:
        load.start()
    for load, store in zip(loads, stores):
        load.wait()
        store.start()
    for store in stores:
        store.wait()


def shards(features, cotangent, spectral_weight, mixing_weight):
    consts = [jnp.asarray(t) for t in tables()]
    dma = pltpu.SemaphoreType.DMA
    vmem = pltpu.VMEM
    hbm = pl.BlockSpec(memory_space=pl.ANY)
    local = pl.BlockSpec(memory_space=pltpu.VMEM)
    results = (
        jax.ShapeDtypeStruct((ROWS, CZ), BF16),
        jax.ShapeDtypeStruct((ROWS, CZ), BF16),
        jax.ShapeDtypeStruct((3, 3, C, 2, C * KEPT), F32),
        jax.ShapeDtypeStruct((C, C), F32),
    )
    parts = pl.pallas_call(
        kernel,
        out_shape=results,
        in_specs=[hbm, hbm, hbm, local] + [hbm] * 9,
        out_specs=(hbm, hbm, local, local),
        scratch_shapes=[
            vmem((ROWS, CZ), BF16),
            vmem((ROWS, CZ), BF16),
            vmem((ROWS, CZ), BF16),
            vmem((ROWS, CZ), BF16),
            vmem((GY, CZ, 256), BF16),
            vmem((GY * 256, CZ), BF16),
            vmem((CZ, CZ), BF16),
            vmem((ROWS, CZ), F32),
            vmem((512, 128), BF16),
            vmem((144, 128), BF16),
            vmem((128, 144), BF16),
            vmem((2, 128, 1024), BF16),
            vmem((2, 1024, 128), BF16),
            vmem((192, 256), BF16),
            vmem((256, 192), BF16),
            vmem((3, 6, C, 2, C * KEPT), BF16),
            vmem((C, CZ), F32),
            vmem((3, 6, 2, 24, 1024), F32),
            vmem((2, 432, 1024), F32),
            vmem((576, 512), BF16),
            vmem((2, 128, 128), BF16),
            vmem((864, 1024), BF16),
            vmem((432, 1024), BF16),
            vmem((432, 1024), BF16),
            vmem((4, 2, 512, 128), BF16),
            vmem((2, 2, 512, 128), BF16),
            vmem((2, 2, 512, 128), BF16),
            vmem((2, 2, 512, 128), BF16),
            vmem((2, GX, 2, 16, 128), BF16),
            vmem((2, 2, GX, 2, 16, 128), BF16),
            vmem((2, GX, 2, 16, 128), BF16),
            vmem((2, 2, GX, 2, 16, 128), BF16),
            vmem((2, 4, 2, 512, 128), BF16),
            vmem((2, GX, GY, 16, 128), BF16),
            vmem((2, 2, GX, GY, 16, 128), BF16),
            vmem((2, GX, GY, 16, 128), BF16),
            vmem((2, 2, GX, GY, 16, 128), BF16),
            vmem((6, 144, 128), BF16),
            vmem((2, GY, 144, 128), BF16),
            vmem((2, GY, 128, 128), BF16),
            vmem((GY, 256, 128), BF16),
            vmem((HALF, 1024), BF16),
            vmem((512, 128), F32),
            vmem((GY, 256, 128), F32),
            vmem((24, 1024), F32),
            vmem((3, 6, 8, 1024), F32),
            vmem((5, 8, CZ), F32),
            vmem((4, 40, 128), F32),
            vmem((18, 40, 128), F32),
            dma((16,)),
            dma((2, 2)),
            dma((2,)),
            dma((2, 2, 3)),
            dma((2,)),
            dma((2, 2, 3)),
            dma((4, 2)),
            dma((4, 2, 2)),
            dma((2, 2)),
            dma((2, 2)),
            dma((2,)),
            dma((2,)),
            dma((2,)),
            dma((2,)),
        ],
        compiler_params=pltpu.CompilerParams(
            collective_id=0, has_side_effects=True, vmem_limit_bytes=60 * 1024 * 1024
        ),
    )(
        features.reshape(ROWS, CZ), cotangent.reshape(ROWS, CZ),
        spectral_weight.transpose(0, 1, 3, 2, 4), mixing_weight, *consts,
    )
    act, gf, gs, gm = pl.pallas_call(
        hand_over,
        out_shape=results,
        in_specs=[hbm] * 4,
        out_specs=(hbm,) * 4,
        scratch_shapes=[vmem(r.shape, r.dtype) for r in results] + [dma((12,)), dma((12,))],
        compiler_params=pltpu.CompilerParams(vmem_limit_bytes=60 * 1024 * 1024),
    )(*parts)
    return act.reshape(features.shape), gf.reshape(features.shape), gs.transpose(0, 1, 3, 2, 4), gm


def solution(mesh):
    in_specs = (
        P("ta", "gx", "gy", None),
        P("ta", "gx", "gy", None),
        P("gx", "gy", None, None, None),
        P(),
    )
    out_specs = (
        P("ta", "gx", "gy", None),
        P("ta", "gx", "gy", None),
        P("gx", ("gy", "ta"), None, None, None),
        P(),
    )
    return jax.shard_map(shards, mesh=mesh, in_specs=in_specs, out_specs=out_specs, check_vma=False)
```

```python
import math

import jax
import jax.numpy as jnp
import ml_dtypes
import numpy as np
from jax import lax
from jax.experimental import pallas as pl
from jax.experimental.pallas import tpu as pltpu
from jax.sharding import PartitionSpec as P

NX = 256
NY = 256
NZ = 64
C = 20
M = 24
KEPT = 48
CZ = C * NZ
GX = 16
GY = 4
ROWS = 1024
HALF = 512
F32 = jnp.float32
BF16 = jnp.bfloat16
MESH = pl.DeviceIdType.MESH
NT = (((1,), (1,)), ((), ()))
TN = (((0,), (0,)), ((), ()))


def cos_sin(length, count, folded):
    freq = np.arange(count)
    if folded:
        freq = np.where(freq < count // 2, freq, freq + length - count)
    phases = np.arange(length)[:, None] * freq[None, :] % length
    angles = phases.astype(np.float32) * np.float32(2.0 * math.pi / length)
    return np.cos(angles), np.sin(angles)


def complex_table(length, count):
    cosine, sine = cos_sin(length, count, True)
    return np.stack([np.stack([cosine, -sine], 1), np.stack([sine, cosine], 1)], 0)


def tables():
    cosine, sine = cos_sin(NZ, M, False)
    depth = np.stack([cosine, -sine], 1)
    ee = np.zeros((GY, C, NZ, 2, 128), np.float32)
    for h in range(GY):
        for jl in range(6):
            for c in range(C):
                ee[h, c, :, :, jl * C + c] = depth[:, :, h * 6 + jl]
    ee = ee.reshape(GY, CZ, 256)
    eet = np.ascontiguousarray(ee.transpose(0, 2, 1)).reshape(GY * 256, CZ)
    height = complex_table(NY, KEPT).reshape(2, GY, 64, 2, KEPT)
    height = height.transpose(1, 3, 4, 0, 2).reshape(GY, 2, GX, 3, 2, 64)
    a2 = np.zeros((GY, 192, 2, 2, 64), np.float32)
    for x2 in range(2):
        a2[:, x2 * 64:x2 * 64 + 64, x2] = height[:, :, :, :2].reshape(GY, 64, 2, 64)
        a2[:, 128 + x2 * 32:160 + x2 * 32, x2] = height[:, :, :, 2].reshape(GY, 32, 2, 64)
    a2 = a2.reshape(GY, 192, 256)
    at2 = np.ascontiguousarray(a2.transpose(0, 2, 1))
    width = complex_table(NX, KEPT).reshape(2, GX, 2, 8, 2, KEPT)
    fx = np.zeros((2, GX, 2, 8, 2, 64), np.float32)
    fx[..., :KEPT] = width.transpose(2, 1, 0, 3, 4, 5)
    fx = fx.reshape(512, 128)
    spread = np.zeros((2, 128, 1024), np.float32)
    for q in range(2):
        for c in range(C):
            spread[q, q * 64 + np.arange(KEPT), c * KEPT + np.arange(KEPT)] = 1.0
    fold = np.ascontiguousarray(spread.transpose(0, 2, 1))
    pad = np.zeros((6, 24, 128), np.float32)
    for jl in range(6):
        for c in range(C):
            pad[jl, c, jl * C + c] = 1.0
    pad = pad.reshape(144, 128)
    padt = np.ascontiguousarray(pad.T)
    return [t.astype(ml_dtypes.bfloat16) for t in (ee, eet, a2, at2, fx, pad, padt, spread, fold)]


def kernel(
    u_hbm, cot_hbm, w_hbm, mix_ref, ee_hbm, eet_hbm, a2_hbm, at2_hbm, fx_hbm, pad_hbm, padt_hbm, spread_hbm, fold_hbm,
    act_hbm, gf_hbm, gs_ref, gm_ref,
    u, cot, g, out, ee, eet, kron, lin, fx, pad, padt, spread, fold, a2, at2, w, mixrows, wp, uh, ht, yk, lw, gss, gsr,
    part, dg, fl, fr, hs, hr, bs, br, ag, hsb, hrb, bsb, brb, pu, pb, yb, agb, by, s, sb, mask, gh, gmx, gmy, gma,
    in_sem, out_sem, rs_ss, rs_rs, ag_ss, ag_rs, ex_ss, ex_rs, third_ss, third_rs, gs_sem, gm_ss, gm_rs, ta_sem,
):
    me_x = lax.axis_index("gx")
    me_y = lax.axis_index("gy")
    me_t = lax.axis_index("ta")

    def at_y(rel):
        return (me_x, lax.rem(me_y + rel, GY), me_t)

    def at_x(d):
        return (lax.rem(me_x + d, GX), me_y, me_t)

    twin = (me_x, me_y, 1 - me_t)

    opposite, left = lax.rem(me_y + 2, GY), lax.rem(me_y + 3, GY)
    right = lax.rem(me_y + 1, GY)
    first, second = pl.ds(0, HALF), pl.ds(HALF, HALF)
    loads = [
        pltpu.make_async_copy(src, dst, in_sem.at[i])
        for i, (src, dst) in enumerate([
            (u_hbm.at[first], u.at[first]), (ee_hbm.at[opposite], ee.at[opposite]),
            (ee_hbm.at[right], ee.at[right]), (a2_hbm.at[me_y], a2),
            (ee_hbm.at[left], ee.at[left]), (ee_hbm.at[me_y], ee.at[me_y]), (u_hbm.at[second], u.at[second]),
            (w_hbm, w), (fx_hbm, fx), (pad_hbm, pad), (padt_hbm, padt),
            (spread_hbm, spread), (fold_hbm, fold), (at2_hbm.at[me_y], at2), (eet_hbm, eet), (cot_hbm, cot),
        ])
    ]

    def start_loads(*ids):
        for i in ids:
            loads[i].start()

    def wait_loads(*ids):
        for i in ids:
            loads[i].wait()

    start_loads(0, 1, 2, 3)

    barrier = pltpu.get_barrier_semaphore()
    for rel in (1, 2, 3):
        pl.semaphore_signal(barrier, inc=1, device_id=at_y(rel), device_id_type=MESH)

    def greet(d, carry):
        pl.semaphore_signal(barrier, inc=1, device_id=at_x(d), device_id_type=MESH)
        return carry

    lax.fori_loop(1, GX, greet, 0)
    pl.semaphore_signal(barrier, inc=1, device_id=twin, device_id_type=MESH)

    def remote(src, dst, ss, rs, dev):
        return pltpu.make_async_remote_copy(
            src_ref=src, dst_ref=dst, send_sem=ss, recv_sem=rs, device_id=dev, device_id_type=MESH
        )

    upper, lower = pl.ds(0, 256), pl.ds(256, 256)

    def rs_copy(t, c, i):
        src, dst, rel = [
            (part.at[2, c, upper], dg.at[t, c, upper], 1),
            (part.at[2, c, lower], dg.at[t, c, lower], 3),
            (part.at[1, c, lower], fl.at[t, c, lower], 1),
            (part.at[3, c, upper], fr.at[t, c, upper], 3),
            (part.at[1, c, upper], fl.at[t, c, upper], 1),
            (part.at[3, c, lower], fr.at[t, c, lower], 3),
        ][i]
        return remote(src, dst, rs_ss.at[t], rs_rs.at[t, c, min(i, 2)], at_y(rel))

    def ag_copy(t, c, i):
        src, dst, rel = [
            (ag.at[t, 0, c, upper], ag.at[t, 3, c, upper], 1),
            (ag.at[t, 0, c, lower], ag.at[t, 1, c, lower], 3),
            (ag.at[t, 0, c, lower], ag.at[t, 3, c, lower], 1),
            (ag.at[t, 0, c, upper], ag.at[t, 1, c, upper], 3),
            (ag.at[t, 3, c, upper], ag.at[t, 2, c, upper], 1),
            (ag.at[t, 1, c, lower], ag.at[t, 2, c, lower], 3),
        ][i]
        return remote(src, dst, ag_ss.at[t], ag_rs.at[t, c, min(i, 2)], at_y(rel))

    def rs_rest(t, c):
        remote(part.at[0], fl.at[t], rs_ss.at[t], rs_rs.at[t, c, 2], at_y(1)).wait_recv()

    def rs_sent(t):
        remote(part.at[pl.ds(0, 3)], part.at[pl.ds(0, 3)], rs_ss.at[t], rs_rs.at[t, 0, 2], at_y(1)).wait_send()

    def ag_sent(t):
        blocks = ag.at[t, pl.ds(0, 3)]
        remote(blocks, blocks, ag_ss.at[t], ag_rs.at[t, 0, 2], at_y(1)).wait_send()

    H, B, HB, BB = range(4)
    pairs = ((hs, hr), (bs, br), (hsb, hrb), (bsb, brb))
    others = pl.ds(0, GX - 1)

    def exchange(kind, t, xc):
        src, dst = pairs[kind]

        def step(d, carry):
            to = lax.rem(me_x + d, GX)
            remote(
                src.at[xc, to], dst.at[t, xc, me_x], ex_ss.at[kind, t], ex_rs.at[kind, t, xc], at_x(d)
            ).start()
            return carry

        lax.fori_loop(1, GX, step, 0)
        dst[t, xc, me_x] = src[xc, me_x]

    def arrived(kind, t, xc):
        src, dst = pairs[kind]
        remote(
            src.at[xc, others], dst.at[t, xc, others], ex_ss.at[kind, t], ex_rs.at[kind, t, xc], at_x(1)
        ).wait_recv()

    def departed(kind, t):
        src, dst = pairs[kind]
        remote(
            src.at[:, others], dst.at[t, :, others], ex_ss.at[kind, t], ex_rs.at[kind, t, 0], at_x(1)
        ).wait_send()

    def pb_copy(t, rel):
        return remote(pu.at[2 + rel], pb.at[t, rel], third_ss.at[t, 0], third_rs.at[t, 0], at_y(rel))

    def yb_copy(t, rel):
        return remote(yb.at[t, 0], yb.at[t, GY - rel], third_ss.at[t, 1], third_rs.at[t, 1], at_y(rel))

    def pb_all(t):
        return remote(pu.at[pl.ds(0, 3)], pb.at[t, pl.ds(0, 3)], third_ss.at[t, 0], third_rs.at[t, 0], at_y(1))

    def yb_all(t):
        blocks = yb.at[t, pl.ds(0, 3)]
        return remote(blocks, blocks, third_ss.at[t, 1], third_rs.at[t, 1], at_y(1))

    def over_gx(fn):
        def step(d, carry):
            fn(d)
            return carry

        lax.fori_loop(1, GX, step, 0)

    def scale(jl):
        first = (me_y == 0) & (jl == 0)
        return jnp.where(first, 1.0, 2.0).astype(F32) * (1.0 / float(NX * NY * NZ))

    def forward_block(src, xc, *rels):
        tab = [ee[lax.rem(me_y + rel, GY)] for rel in rels]
        tab = tab[0] if len(tab) == 1 else jnp.concatenate(tab, 1)
        both = jnp.dot(src[xc * HALF:(xc + 1) * HALF, :], tab, preferred_element_type=F32).astype(BF16)
        for xp in range(4):
            r = xp * 128
            rhs = jnp.concatenate([
                jnp.concatenate(
                    [both[row:row + 64, i * 256 + p * 128:i * 256 + p * 128 + 128] for i in range(len(rels))], 1
                )
                for row in (r, r + 64) for p in range(2)
            ], 0)
            o = jnp.dot(a2[...], rhs, preferred_element_type=F32)
            for i, rel in enumerate(rels):
                part[rel, xc, xp * 128:(xp + 1) * 128, :] = o[:128, i * 128:(i + 1) * 128].astype(BF16)
                sb[i, xp * 64:(xp + 1) * 64, :] = o[128:, i * 128:(i + 1) * 128]
        for i, rel in enumerate(rels):
            for gx in range(GX):
                top = sb[i, pl.ds(gx, 8, stride=32), :]
                low = sb[i, pl.ds(gx + GX, 8, stride=32), :]
                hsb[xc, gx, rel] = jnp.concatenate([top, low], 0).astype(BF16)

    def send_third(t, xc):
        exchange(HB, t, xc)

    def rs_start(t, c, *ids):
        for i in ids:
            rs_copy(t, c, i).start()

    def rs_forward(t, c):
        rs_copy(t, c, 0).wait_recv()
        part[1, c, :256] = (part[1, c, :256].astype(F32) + dg[t, c, :256].astype(F32)).astype(BF16)
        rs_start(t, c, 4)
        rs_copy(t, c, 1).wait_recv()
        part[3, c, 256:] = (part[3, c, 256:].astype(F32) + dg[t, c, 256:].astype(F32)).astype(BF16)
        rs_start(t, c, 5)

    def ag_start(t, c):
        for i in range(4):
            ag_copy(t, c, i).start()

    def ag_forward(t, c):
        for i in (0, 1):
            ag_copy(t, c, i).wait_recv()
            ag_copy(t, c, 4 + i).start()

    def ag_finish(t, c):
        remote(ag.at[t, 0], ag.at[t, 0], ag_ss.at[t], ag_rs.at[t, c, 2], at_y(1)).wait_recv()

    def sum_and_send(t, xc):
        s[...] = part[0, xc].astype(F32) + fl[t, xc].astype(F32) + fr[t, xc].astype(F32)

        def block(gx, carry):
            for k in range(2):
                r = gx * 2 + k
                top = s[pl.ds(r, 8, stride=64), :]
                low = s[pl.ds(r + 32, 8, stride=64), :]
                hs[xc, gx, k] = jnp.concatenate([top, low], 0).astype(BF16)
            return carry

        lax.fori_loop(0, GX, block, 0)
        exchange(H, t, xc)

    def x_third(t):
        for rel in range(GY):
            hk = hrb[t, :, :, rel].reshape(512, 128)
            ht[rel * 144:(rel + 1) * 144, :] = lax.dot_general(
                pad[...], hk, NT, preferred_element_type=F32
            ).astype(BF16)
        v = jnp.dot(ht[...], fx[...], preferred_element_type=F32).astype(BF16)
        pu[2] = v[:144]
        for rel in (1, 2, 3):
            pu[2 + rel] = v[rel * 144:(rel + 1) * 144]
            pb_copy(t, rel).start()

    def x_transform(t, put):
        for k in range(2):
            hk = hr[t, :, :, k].reshape(512, 128)
            v = lax.dot_general(pad[...], hk, NT, preferred_element_type=F32).astype(BF16)
            pu[k] = jnp.dot(v, fx[...], preferred_element_type=F32).astype(BF16)
        pb_all(t).wait_recv()
        third = pu[2].astype(F32) + pb[t, 1].astype(F32) + pb[t, 2].astype(F32) + pb[t, 3].astype(F32)
        v = jnp.concatenate([pu[0], pu[1], third.astype(BF16)], 0)
        for q in range(2):
            for n in range(2):
                put(q, n * 512, jnp.dot(v, spread[q, :, n * 512:(n + 1) * 512], preferred_element_type=F32))

    def x_inverse_and_send(t):
        y = jnp.dot(lw[:432, :], fold[0], preferred_element_type=F32)
        y = (y + jnp.dot(lw[432:, :], fold[1], preferred_element_type=F32)).astype(BF16)
        for k in (2, 0, 1):
            v = jnp.dot(padt[...], y[k * 144:(k + 1) * 144], preferred_element_type=F32).astype(BF16)
            if k == 2:
                yb[t, 0] = v
                for rel in (1, 2, 3):
                    yb_copy(t, rel).start()
            else:
                yk[k] = v
        for xc in range(2):
            for k in range(2):
                bx = lax.dot_general(fx[xc * 256:(xc + 1) * 256, :], yk[k], NT, preferred_element_type=F32)
                bs[xc, :, k] = bx.astype(BF16).reshape(GX, 16, 128)
            exchange(B, t, xc)

    def third_inverse_and_send(t):
        yb_all(t).wait_recv()
        for xc in range(2):
            for rel in range(GY):
                bx = lax.dot_general(fx[xc * 256:(xc + 1) * 256, :], yb[t, rel], NT, preferred_element_type=F32)
                bsb[xc, :, rel] = bx.astype(BF16).reshape(GX, 16, 128)
            exchange(BB, t, xc)

    def gather_block(t, xc):
        arrived(B, t, xc)

        def block(gx, carry):
            for k in range(2):
                r = gx * 2 + k
                v = br[t, xc, gx, k].astype(F32)
                s[pl.ds(r, 8, stride=64), :] = v[:8]
                s[pl.ds(r + 32, 8, stride=64), :] = v[8:]
            return carry

        lax.fori_loop(0, GX, block, 0)
        ag[t, 0, xc] = s[...].astype(BF16)

    def gather_third(t, xc):
        arrived(BB, t, xc)
        for rel in range(GY):
            for gx in range(GX):
                v = brb[t, xc, gx, rel].astype(F32)
                sb[rel, pl.ds(gx, 8, stride=32), :] = v[:8]
                sb[rel, pl.ds(gx + GX, 8, stride=32), :] = v[8:]
            agb[rel] = sb[rel].astype(BF16)

    def y_inverse(t, xc):
        for xp in range(4):
            two, third = slice(xp * 128, (xp + 1) * 128), slice(xp * 64, (xp + 1) * 64)
            rhs = jnp.concatenate([
                jnp.concatenate([ag[t, rel, xc, two, :] for rel in range(GY)], 1),
                jnp.concatenate([agb[rel, third, :] for rel in range(GY)], 1),
            ], 0)
            v = jnp.dot(at2[...], rhs, preferred_element_type=F32).astype(BF16)
            for rel in range(GY):
                off = pl.multiple_of(lax.rem(me_y + rel, GY) * 256, 256)
                w_rel = v[:, rel * 128:(rel + 1) * 128]
                for x2 in range(2):
                    rows = slice(xp * 128 + x2 * 64, xp * 128 + x2 * 64 + 64)
                    by[rows, pl.ds(off, 128)] = w_rel[x2 * 128:x2 * 128 + 64]
                    by[rows, pl.ds(off + 128, 128)] = w_rel[x2 * 128 + 64:x2 * 128 + 128]

    def depth_inverse(xc, finish, start=0, stop=3):
        for n in range(start, stop):
            cols = slice(n * 512, min(n * 512 + 512, CZ))
            for rb in range(2):
                rows = slice(xc * HALF + rb * 256, xc * HALF + rb * 256 + 256)
                v = jnp.dot(by[rb * 256:rb * 256 + 256, :], eet[:, cols], preferred_element_type=F32)
                finish(rows, cols, v + lin[rows, cols])

    def finish_forward(rows, cols, x):
        k0 = math.sqrt(2.0 / math.pi)
        x2 = x * x
        th = jnp.tanh(k0 * x * (1.0 + 0.044715 * x2))
        half = 0.5 * (1.0 + th)
        out[rows, cols] = (x * half).astype(BF16)
        slope = half + 0.5 * x * (1.0 - th * th) * (k0 * (1.0 + 3.0 * 0.044715 * x2))
        g[rows, cols] = (cot[rows, cols].astype(F32) * slope).astype(BF16)

    def finish_backward(rows, cols, x):
        out[rows, cols] = x.astype(BF16)

    def build_kron(dims):
        at = lax.broadcasted_iota(jnp.int32, (C, CZ), 1) >> 6
        one = jnp.where(at == lax.broadcasted_iota(jnp.int32, (C, CZ), 0), 1.0, 0.0).astype(BF16)
        mixrows[...] = lax.dot_general(mix_ref[...], one, dims, preferred_element_type=F32)

        lane = lax.broadcasted_iota(jnp.int32, (NZ, CZ), 1) & (NZ - 1)
        row = lax.broadcasted_iota(jnp.int32, (NZ, CZ), 0)
        eye = jnp.where(lane == row, 1.0, 0.0).astype(F32)

        def block(c, carry):
            kron[pl.ds(pl.multiple_of(c * NZ, NZ), NZ), :] = (eye * mixrows[pl.ds(c, 1), :]).astype(BF16)
            return carry

        lax.fori_loop(0, C, block, 0)

    def linear(src, rb):
        def block(n, carry):
            cols = pl.ds(pl.multiple_of(n * 256, 256), 256)
            rows = slice(rb * 512, rb * 512 + 512)
            lin[rows, cols] = jnp.dot(src[rows, :], kron[:, cols], preferred_element_type=F32)
            return carry

        lax.fori_loop(0, 5, block, 0, unroll=True)

    def fill_weights():
        wp[...] = jnp.zeros_like(wp)
        for k in range(3):
            def block(j, carry):
                v = w[k, j].astype(F32)
                for p in range(2):
                    wp[k, j, p, :C, :C * KEPT] = v[:, p, :]
                return carry

            lax.fori_loop(0, 6, block, 0)
        lane = lax.broadcasted_iota(jnp.int32, (24, 1024), 1)
        first = lax.broadcasted_iota(jnp.int32, (24, 1024), 0) * KEPT
        mask[...] = jnp.where((lane >= first) & (lane < first + KEPT) & (lane < C * KEPT), 1.0, 0.0).astype(F32)

    def put_uh(q, at, v):
        uh[q, :, at:at + 512] = v

    def put_lin(q, at, v):
        lin[q * 432:(q + 1) * 432, at:at + 512] = v

    def put_rows(k, jp, re, im):
        at = pl.multiple_of(k * 144 + jp * 48, 48)
        lw[pl.ds(at, 48), :] = jnp.concatenate(re, 0).astype(BF16)
        lw[pl.ds(at + 432, 48), :] = jnp.concatenate(im, 0).astype(BF16)

    def mix_block(k, carry):
        for jp in range(3):
            re, im = [], []
            for j in (2 * jp, 2 * jp + 1):
                rows = pl.ds(pl.multiple_of(k * 144 + j * 24, 8), 24)
                a, b = uh[0, rows, :], uh[1, rows, :]
                r, w = wp[k, j, 0], wp[k, j, 1]
                re.append(mask[...] * (jnp.sum(a * r - b * w, 0, keepdims=True) * scale(j)))
                im.append(mask[...] * (jnp.sum(a * w + b * r, 0, keepdims=True) * scale(j)))
            put_rows(k, jp, re, im)
        return carry

    def adjoint_block(k, carry):
        for jp in range(3):
            re, im = [], []
            for j in (2 * jp, 2 * jp + 1):
                at = pl.multiple_of(k * 144 + j * 24, 8)
                r, w = wp[k, j, 0], wp[k, j, 1]
                gr = jnp.sum(lin[pl.ds(at, 24), :1024] * mask[...], 0, keepdims=True) * scale(j)
                gi = jnp.sum(lin[pl.ds(at + 432, 24), :1024] * mask[...], 0, keepdims=True) * scale(j)
                gh[k, j, 0:1, :] = gr
                gh[k, j, 1:2, :] = gi
                re.append(gr * r + gi * w)
                im.append(gi * r - gr * w)
            put_rows(k, jp, re, im)
        return carry

    def weight_terms(k, j):
        rows = pl.ds(pl.multiple_of(k * 144 + j * 24, 8), 24)
        a, b = uh[0, rows, :], uh[1, rows, :]
        gr, gi = gh[k, j, 0:1, :], gh[k, j, 1:2, :]
        return a * gr + b * gi, a * gi - b * gr

    def gs_copy():
        return remote(gss, gsr, gs_sem.at[0], gs_sem.at[1], twin)

    def weight_gradient_send():
        def block(k, carry):
            for jj in range(3):
                re, im = weight_terms(k, (1 - me_t) * 3 + jj)
                at = pl.multiple_of(k * 144 + jj * 48, 48)
                gss[pl.ds(at, 48), :] = jnp.concatenate([re, im], 0).astype(BF16)
            return carry

        lax.fori_loop(0, 3, block, 0)
        gs_copy().start()

    def weight_gradient_finish():
        gs_copy().wait_recv()

        def block(k, carry):
            for jj in range(3):
                re, im = weight_terms(k, me_t * 3 + jj)
                at = pl.multiple_of(k * 144 + jj * 48, 48)
                other = gsr[pl.ds(at, 48), :].astype(F32)
                gs_ref[k, jj, :, 0, :] = (re + other[:24])[:C, :C * KEPT]
                gs_ref[k, jj, :, 1, :] = (im + other[24:])[:C, :C * KEPT]
            return carry

        lax.fori_loop(0, 3, block, 0)

    def mixing_terms():
        lane = lax.broadcasted_iota(jnp.int32, (256, 256), 1) & (NZ - 1)
        row = lax.broadcasted_iota(jnp.int32, (256, 256), 0) & (NZ - 1)
        eye = jnp.where(lane == row, 1.0, 0.0).astype(F32)

        def block(cb, carry):
            cols = pl.ds(pl.multiple_of(cb * 256, 256), 256)
            for nb in range(5):
                o = lax.dot_general(
                    u[:, cols], g[:, nb * 256:(nb + 1) * 256], TN, preferred_element_type=F32
                )
                gmx[cb, 0:4, nb * 256:(nb + 1) * 256] = jnp.sum((o * eye).reshape(4, NZ, 256), 1)
            return carry

        gmx[...] = jnp.zeros_like(gmx)
        lax.fori_loop(0, 5, block, 0)
        v = gmx[...].reshape(40, CZ)
        hi = v.astype(BF16)
        low = (v - hi.astype(F32)).astype(BF16)
        sel = lax.broadcasted_iota(jnp.int32, (CZ, 128), 0) >> 6
        sel = jnp.where(sel == lax.broadcasted_iota(jnp.int32, (CZ, 128), 1), 1.0, 0.0).astype(BF16)
        gmy[0] = jnp.dot(hi, sel, preferred_element_type=F32) + jnp.dot(low, sel, preferred_element_type=F32)

    def gy_copy(rel):
        return remote(gmy.at[0], gmy.at[rel], gm_ss.at[0], gm_rs.at[0], at_y(rel))

    def gy_all():
        return remote(gmy.at[pl.ds(0, 3)], gmy.at[pl.ds(0, 3)], gm_ss.at[0], gm_rs.at[0], at_y(1))

    def gx_copy(d):
        return remote(gma.at[0], gma.at[d], gm_ss.at[1], gm_rs.at[1], at_x(d))

    def gx_all():
        return remote(gma.at[others], gma.at[others], gm_ss.at[1], gm_rs.at[1], at_x(1))

    def ta_copy():
        return remote(gma.at[16], gma.at[17], ta_sem.at[0], ta_sem.at[1], twin)

    wait_loads(0, 1, 2, 3)
    start_loads(4, 5, 6)
    forward_block(u, 0, 2, 1)
    pl.semaphore_wait(barrier, 19)
    rs_start(0, 0, 0, 1, 2)
    wait_loads(4, 5)
    forward_block(u, 0, 3, 0)
    rs_start(0, 0, 3)
    send_third(0, 0)
    wait_loads(6)
    start_loads(*range(7, 16))
    forward_block(u, 1, 2, 1)
    rs_start(0, 1, 0, 1)
    forward_block(u, 1, 3, 0)
    send_third(0, 1)
    rs_forward(0, 0)
    rs_start(0, 1, 2, 3)
    wait_loads(7)
    fill_weights()
    rs_forward(0, 1)
    build_kron((((1,), (0,)), ((), ())))
    wait_loads(*range(8, 16))

    def sums(t, meanwhile):
        for c in range(2):
            rs_rest(t, c)
            sum_and_send(t, c)
        arrived(HB, t, 0)
        arrived(HB, t, 1)
        x_third(t)
        meanwhile()
        arrived(H, t, 0)
        arrived(H, t, 1)

    sums(0, lambda: None)

    x_transform(0, put_uh)
    lax.fori_loop(0, 3, mix_block, 0, unroll=True)
    x_inverse_and_send(0)

    def gather(t, src):
        third_inverse_and_send(t)
        gather_block(t, 0)
        ag_start(t, 0)
        gather_block(t, 1)
        linear(src, 0)
        ag_forward(t, 0)
        ag_start(t, 1)
        linear(src, 1)
        ag_forward(t, 1)

    gather(0, u)
    rs_sent(0)
    for kind in (H, B, HB, BB):
        departed(kind, 0)
    pb_all(0).wait_send()

    gather_third(0, 0)
    ag_finish(0, 0)
    y_inverse(0, 0)
    depth_inverse(0, finish_forward)
    act_out = [
        pltpu.make_async_copy(out.at[pl.ds(xc * HALF, HALF)], act_hbm.at[pl.ds(xc * HALF, HALF)], out_sem.at[0, xc])
        for xc in range(2)
    ]
    act_out[0].start()
    forward_block(g, 0, 2, 1)
    rs_start(1, 0, 0, 1, 2)
    forward_block(g, 0, 3, 0)
    rs_start(1, 0, 3)
    send_third(1, 0)
    gather_third(0, 1)
    ag_finish(0, 1)
    y_inverse(0, 1)
    depth_inverse(1, finish_forward, 0, 2)
    rs_forward(1, 0)
    depth_inverse(1, finish_forward, 2, 3)
    act_out[1].start()
    forward_block(g, 1, 2, 1)
    rs_start(1, 1, 0, 1, 2)
    forward_block(g, 1, 3, 0)
    rs_start(1, 1, 3)
    send_third(1, 1)
    rs_forward(1, 1)

    def mixing_send():
        mixing_terms()
        for rel in (1, 2, 3):
            gy_copy(rel).start()

    sums(1, mixing_send)

    x_transform(1, put_lin)
    lax.fori_loop(0, 3, adjoint_block, 0, unroll=True)
    x_inverse_and_send(1)
    weight_gradient_send()
    gy_all().wait_recv()
    gma[0] = gmy[0] + gmy[1] + gmy[2] + gmy[3]
    over_gx(lambda d: gx_copy(d).start())
    build_kron(TN)
    gather(1, g)
    gx_all().wait_recv()
    gma[16] = jnp.sum(gma[0:16], 0)
    ta_copy().start()
    weight_gradient_finish()
    act_out[0].wait()
    act_out[1].wait()
    gather_third(1, 0)
    ag_finish(1, 0)
    y_inverse(1, 0)
    depth_inverse(0, finish_backward)
    gf_out = [
        pltpu.make_async_copy(out.at[pl.ds(xc * HALF, HALF)], gf_hbm.at[pl.ds(xc * HALF, HALF)], out_sem.at[1, xc])
        for xc in range(2)
    ]
    gf_out[0].start()
    gather_third(1, 1)
    ag_finish(1, 1)
    y_inverse(1, 1)
    depth_inverse(1, finish_backward)
    gf_out[1].start()
    ta_copy().wait_recv()
    total = (gma[16] + gma[17]) * (1.0 / math.sqrt(2 * NX * NY * NZ))
    for cb in range(5):
        gm_ref[cb * 4:(cb + 1) * 4, :] = total[cb * 8:cb * 8 + 4, :C]

    ag_sent(0)
    ag_sent(1)
    rs_sent(1)
    for kind in (H, B, HB, BB):
        departed(kind, 1)
    pb_all(1).wait_send()
    yb_all(0).wait_send()
    yb_all(1).wait_send()
    gs_copy().wait_send()
    gy_all().wait_send()
    gx_all().wait_send()
    ta_copy().wait_send()
    gf_out[0].wait()
    gf_out[1].wait()


def hand_over(act_in, gf_in, gs_in, gm_in, act_out, gf_out, gs_out, gm_out, act, gf, gs, gm, in_sem, out_sem):
    pieces = [(gs_in.at[k], gs.at[k], gs_out.at[k]) for k in range(3)] + [(gm_in, gm, gm_out)]
    for i in range(4):
        rows = pl.ds(i * 256, 256)
        pieces.append((act_in.at[rows], act.at[rows], act_out.at[rows]))
        pieces.append((gf_in.at[rows], gf.at[rows], gf_out.at[rows]))
    loads = [pltpu.make_async_copy(p[0], p[1], in_sem.at[i]) for i, p in enumerate(pieces)]
    stores = [pltpu.make_async_copy(p[1], p[2], out_sem.at[i]) for i, p in enumerate(pieces)]
    for load in loads:
        load.start()
    for load, store in zip(loads, stores):
        load.wait()
        store.start()
    for store in stores:
        store.wait()


def shards(features, cotangent, spectral_weight, mixing_weight):
    consts = [jnp.asarray(t) for t in tables()]
    dma = pltpu.SemaphoreType.DMA
    vmem = pltpu.VMEM
    hbm = pl.BlockSpec(memory_space=pl.ANY)
    local = pl.BlockSpec(memory_space=pltpu.VMEM)
    results = (
        jax.ShapeDtypeStruct((ROWS, CZ), BF16),
        jax.ShapeDtypeStruct((ROWS, CZ), BF16),
        jax.ShapeDtypeStruct((3, 3, C, 2, C * KEPT), F32),
        jax.ShapeDtypeStruct((C, C), F32),
    )
    parts = pl.pallas_call(
        kernel,
        out_shape=results,
        in_specs=[hbm, hbm, hbm, local] + [hbm] * 9,
        out_specs=(hbm, hbm, local, local),
        scratch_shapes=[
            vmem((ROWS, CZ), BF16),
            vmem((ROWS, CZ), BF16),
            vmem((ROWS, CZ), BF16),
            vmem((ROWS, CZ), BF16),
            vmem((GY, CZ, 256), BF16),
            vmem((GY * 256, CZ), BF16),
            vmem((CZ, CZ), BF16),
            vmem((ROWS, CZ), F32),
            vmem((512, 128), BF16),
            vmem((144, 128), BF16),
            vmem((128, 144), BF16),
            vmem((2, 128, 1024), BF16),
            vmem((2, 1024, 128), BF16),
            vmem((192, 256), BF16),
            vmem((256, 192), BF16),
            vmem((3, 6, C, 2, C * KEPT), BF16),
            vmem((C, CZ), F32),
            vmem((3, 6, 2, 24, 1024), F32),
            vmem((2, 432, 1024), F32),
            vmem((576, 512), BF16),
            vmem((2, 128, 128), BF16),
            vmem((864, 1024), BF16),
            vmem((432, 1024), BF16),
            vmem((432, 1024), BF16),
            vmem((4, 2, 512, 128), BF16),
            vmem((2, 2, 512, 128), BF16),
            vmem((2, 2, 512, 128), BF16),
            vmem((2, 2, 512, 128), BF16),
            vmem((2, GX, 2, 16, 128), BF16),
            vmem((2, 2, GX, 2, 16, 128), BF16),
            vmem((2, GX, 2, 16, 128), BF16),
            vmem((2, 2, GX, 2, 16, 128), BF16),
            vmem((2, 4, 2, 512, 128), BF16),
            vmem((2, GX, GY, 16, 128), BF16),
            vmem((2, 2, GX, GY, 16, 128), BF16),
            vmem((2, GX, GY, 16, 128), BF16),
            vmem((2, 2, GX, GY, 16, 128), BF16),
            vmem((6, 144, 128), BF16),
            vmem((2, GY, 144, 128), BF16),
            vmem((2, GY, 128, 128), BF16),
            vmem((GY, 256, 128), BF16),
            vmem((HALF, 1024), BF16),
            vmem((512, 128), F32),
            vmem((GY, 256, 128), F32),
            vmem((24, 1024), F32),
            vmem((3, 6, 8, 1024), F32),
            vmem((5, 8, CZ), F32),
            vmem((4, 40, 128), F32),
            vmem((18, 40, 128), F32),
            dma((16,)),
            dma((2, 2)),
            dma((2,)),
            dma((2, 2, 3)),
            dma((2,)),
            dma((2, 2, 3)),
            dma((4, 2)),
            dma((4, 2, 2)),
            dma((2, 2)),
            dma((2, 2)),
            dma((2,)),
            dma((2,)),
            dma((2,)),
            dma((2,)),
        ],
        compiler_params=pltpu.CompilerParams(
            collective_id=0, has_side_effects=True, vmem_limit_bytes=60 * 1024 * 1024
        ),
    )(
        features.reshape(ROWS, CZ), cotangent.reshape(ROWS, CZ),
        spectral_weight.transpose(0, 1, 3, 2, 4), mixing_weight, *consts,
    )
    act, gf, gs, gm = pl.pallas_call(
        hand_over,
        out_shape=results,
        in_specs=[hbm] * 4,
        out_specs=(hbm,) * 4,
        scratch_shapes=[vmem(r.shape, r.dtype) for r in results] + [dma((12,)), dma((12,))],
        compiler_params=pltpu.CompilerParams(vmem_limit_bytes=60 * 1024 * 1024),
    )(*parts)
    return act.reshape(features.shape), gf.reshape(features.shape), gs.transpose(0, 1, 3, 2, 4), gm


def solution(mesh):
    in_specs = (
        P("ta", "gx", "gy", None),
        P("ta", "gx", "gy", None),
        P("gx", "gy", None, None, None),
        P(),
    )
    out_specs = (
        P("ta", "gx", "gy", None),
        P("ta", "gx", "gy", None),
        P("gx", ("gy", "ta"), None, None, None),
        P(),
    )
    return jax.shard_map(shards, mesh=mesh, in_specs=in_specs, out_specs=out_specs, check_vma=False)
```
